512 devices in a mesh: gx: 64 (over x, z), gy: 8 (over y, core).
Axes of the slice: x: 4, y: 4, z: 16, core: 2. Of those that a mesh axis runs over, the one named last changes fastest.
Arguments:
- residual: float32 [1, 2048, 128, 128], P(None, 'gx', 'gy'), may hold values from -6 to 6
- elem_class: int32 [256, 16, 16], P('gx', 'gy'), may hold values from 0 to 7
- basis: float32 [8, 3, 10, 10], replicated, may hold values from -2 to 2
- eigenvalues: float32 [8, 3, 10], replicated, may hold values from 0.1 to 3
- vertex_number: int32 [320, 24, 17], P('gx', 'gy'), may hold values from 0 to 254, as said below
- panels: float32 [16320, 23544], P('gx', 'gy'), may hold values from -1 to 1
Outputs:
- correction: float32 [1, 2048, 128, 128], P(None, 'gx', 'gy')
The draws below stay inside these ranges and needn't reach their ends.
Inputs may be any that keep to these rules, and one draw needn't show every extreme that they name: `vertex_number`: within each block of (5) x (3) x (17) entries, the block (p, q) starting at (5) p and (3) q, every number 0 to 254 appears once.
All inputs are finite; a program needn't handle non-finite values.
Results may differ from the reference program's by a relative error of at most 0.0001.
Values sent between devices are 32-bit elements; how exact they have to be, the bound alone decides.
No kernel may reach another device: no remote copies, remote signals or barrier semaphores. Data moves between devices by JAX's collectives and lax.ppermute only.
A program may use at most 128 MiB of HBM per device.

```python
import math
import jax
import jax.numpy as jnp
from jax import lax

NPR = 8
NEXT = 10
NCLASS = 8
EX = 4
EY = 2
EZ = 16
NRHS = 1
EXG = 256
EYG = 16
NX = 2048
NY = 128
NZ = 128
V = 255
LX = 6
LY = 3
KY = 128
KX = 384
KTOT = 2943
N_GX = 64
N_GY = 8


def draw_vertex_number(key, part):
    key = jax.random.fold_in(key, 7)
    subkeys = jax.random.split(key, N_GX * N_GY)

    def one_block(subkey):
        return jax.random.permutation(subkey, V).astype(jnp.int32)
    orders = jax.vmap(one_block)(subkeys)
    blocks = orders.reshape(N_GX, N_GY, EX + 1, EY + 1, EZ + 1)
    return blocks.transpose(0, 2, 1, 3, 4).reshape(N_GX * (EX + 1), N_GY * (EY + 1), EZ + 1).astype(jnp.int32)


def draw_panels(key, part):
    key = jax.random.fold_in(key, 11)
    height = N_GX * V
    breadth = N_GY * KTOT
    noise = jax.random.truncated_normal(key, -4.0, 4.0, (height, breadth), jnp.float32)
    column = jnp.arange(breadth, dtype=jnp.int32) % KTOT
    upper_y = 1 + (column - V) // KY
    upper_x = 1 + LY + (column - V - LY * KY) // KX
    level = jnp.where(column < V, 0, jnp.where(column < V + LY * KY, upper_y, upper_x))
    scaling = 0.15 * jnp.exp2(-level.astype(jnp.float32) / 4.0) / math.sqrt(V)
    return (noise * scaling[None, :]).astype(jnp.float32)


def place_ends(array, stream_key, smallest, top_value):
    longest = array.shape.index(max(array.shape))
    spots = []
    for shift in (0, 1):
        where = [jax.random.randint(jax.random.fold_in(stream_key, axis), (), 0, length) for axis, length in enumerate(array.shape)]
        where[longest] = (where[longest] + shift) % array.shape[longest]
        spots.append(tuple(where))
    return array.at[spots[0]].set(smallest).at[spots[1]].set(top_value)


def shard_levels(rng, shape, cuts, least, top_value):
    factor_of, own = 1.0, jax.random.fold_in(rng, 6)
    for position, blocks in cuts:
        heights = jnp.exp(jax.random.uniform(jax.random.fold_in(own, position), (blocks,), jnp.float32, least / len(cuts), top_value / len(cuts)))
        factor_of = factor_of * jnp.repeat(heights, shape[position] // blocks).reshape([-1 if axis == position else 1 for axis in range(len(shape))])
    return factor_of


def bell_draw(stream_key, dims, deviation, reach, cuts=(), kind=jnp.bfloat16):
    loudness = shard_levels(stream_key, dims, cuts, -0.22, 0.18) if cuts else 1.0
    drawn = jax.random.normal(stream_key, dims, jnp.float32) * deviation * loudness
    return jnp.minimum(jnp.maximum(drawn, -reach), reach).astype(kind)


def setup_inputs(seed: int = 0) -> dict:
    arg_keys = jax.random.split(jax.random.key(seed), 7)
    return {
        "residual": bell_draw(arg_keys[0], (NRHS, NX, NY, NZ), 1.0, 6.0, ((1, 64), (2, 8)), jnp.float32),
        "elem_class": place_ends(jax.random.randint(arg_keys[1], (EXG, EYG, EZ), 0, NCLASS), jax.random.fold_in(arg_keys[1], 1), 0, NCLASS - 1).astype(jnp.int32),
        "basis": bell_draw(arg_keys[2], (NCLASS, 3, NEXT, NEXT), NEXT ** -0.5, 2.0, (), jnp.float32),
        "eigenvalues": jnp.clip(jnp.exp(jax.random.uniform(arg_keys[3], (NCLASS, 3, NEXT), jnp.float32, math.log(0.1), math.log(3.0))), 0.1, 3.0),
        "vertex_number": draw_vertex_number(jax.random.fold_in(arg_keys[6], 71), 0),
        "panels": draw_panels(jax.random.fold_in(arg_keys[6], 71), 0),
    }


precise = lax.Precision.HIGHEST


def hat_table():
    points = (2.0 * jnp.arange(NPR, dtype=jnp.float32) + 1.0) / NPR - 1.0
    return jnp.stack([(1.0 - points) / 2.0, (1.0 + points) / 2.0])


def windows(source, dimension):
    moved_field = jnp.moveaxis(source, dimension, 0)
    element_count = (moved_field.shape[0] - 2) // NPR
    trailing = moved_field.shape[1:]
    head_part = moved_field[:element_count * NPR].reshape((element_count, NPR) + trailing)
    extended = jnp.concatenate([moved_field, jnp.zeros((NPR - 2,) + trailing, moved_field.dtype)], axis=0)
    tail_part = extended[NPR:].reshape((element_count, NPR) + trailing)[:, :2]
    joined = jnp.concatenate([head_part, tail_part], axis=1)
    return jnp.moveaxis(joined, (0, 1), (dimension, dimension + 1))


def unwindows(blocks, dimension):
    moved_field = jnp.moveaxis(blocks, (dimension, dimension + 1), (0, 1))
    element_count = moved_field.shape[0]
    trailing = moved_field.shape[2:]
    head_part = moved_field[:, :NPR].reshape((element_count * NPR,) + trailing)
    tail_part = jnp.concatenate([moved_field[:, NPR:], jnp.zeros((element_count, NPR - 2) + trailing, moved_field.dtype)], axis=1)
    tail_part = tail_part.reshape((element_count * NPR,) + trailing)
    front = jnp.concatenate([head_part, jnp.zeros((2,) + trailing, moved_field.dtype)], axis=0)
    behind = jnp.concatenate([jnp.zeros((NPR,) + trailing, moved_field.dtype), tail_part], axis=0)[:element_count * NPR + 2]
    return jnp.moveaxis(front + behind, 0, dimension)


def solve_block(window, bases, values):
    first = jnp.einsum('yzia,ryzijk->ryzajk', bases[:, :, 0], window, precision=precise)
    second = jnp.einsum('yzjb,ryzajk->ryzabk', bases[:, :, 1], first, precision=precise)
    third = jnp.einsum('yzkc,ryzabk->ryzabc', bases[:, :, 2], second, precision=precise)
    denom = values[:, :, 0, :, None, None] + values[:, :, 1, None, :, None] + values[:, :, 2, None, None, :]
    scaled = third / denom[None]
    back_x = jnp.einsum('yzia,ryzabc->ryzibc', bases[:, :, 0], scaled, precision=precise)
    back_y = jnp.einsum('yzjb,ryzibc->ryzijc', bases[:, :, 1], back_x, precision=precise)
    return jnp.einsum('yzkc,ryzijc->ryzijk', bases[:, :, 2], back_y, precision=precise)


def fine_part(residual, elem_class, basis, eigenvalues):
    padded = jnp.pad(residual, ((0, 0), (1, 1), (1, 1), (1, 1)))

    def column_step(accumulated, column):
        begin_row = column * NPR
        layer_rows = lax.dynamic_slice_in_dim(padded, begin_row, NEXT, 1)
        pieces = windows(windows(layer_rows, 2), 4)
        window = pieces.transpose(0, 2, 4, 1, 3, 5)
        classes = lax.dynamic_index_in_dim(elem_class, column, 0, keepdims=False)
        local_fix = solve_block(window, basis[classes], eigenvalues[classes])
        placed = unwindows(unwindows(local_fix.transpose(0, 3, 1, 4, 2, 5), 4), 2)
        current = lax.dynamic_slice_in_dim(accumulated, begin_row, NEXT, 1)
        return lax.dynamic_update_slice_in_dim(accumulated, current + placed, begin_row, 1), None

    accumulated, unused = lax.scan(column_step, jnp.zeros_like(padded), jnp.arange(EXG, dtype=jnp.int32))
    return accumulated[:, 1:-1, 1:-1, 1:-1]


def gather_rows(numbers_row, panel_row):
    return jnp.take_along_axis(panel_row.transpose(1, 0, 2), numbers_row[:, :, None], axis=1)


def coarse_part(residual, vertex_number, panels):
    weights = hat_table()
    nodes = residual.reshape(NRHS, EXG, NPR, EYG, NPR, EZ, NPR)
    corner = jnp.einsum('rxiyjzk,ai,bj,ck->rxyzabc', nodes, weights, weights, weights, precision=precise)
    corner = corner.reshape(NRHS, N_GX, EX, N_GY, EY, EZ, 2, 2, 2)
    vertex_res = jnp.zeros((NRHS, N_GX, EX + 1, N_GY, EY + 1, EZ + 1), jnp.float32)
    for shift_a in (0, 1):
        for shift_b in (0, 1):
            for shift_c in (0, 1):
                vertex_res = vertex_res + jnp.pad(corner[..., shift_a, shift_b, shift_c], ((0, 0), (0, 0), (shift_a, 1 - shift_a), (0, 0), (shift_b, 1 - shift_b), (shift_c, 1 - shift_c)))
    vertex_res = vertex_res.transpose(1, 3, 0, 2, 4, 5).reshape(N_GX, N_GY, NRHS, V)
    numbers = vertex_number.reshape(N_GX, EX + 1, N_GY, EY + 1, EZ + 1).transpose(0, 2, 1, 3, 4).reshape(N_GX, N_GY, V)
    panel_rows = panels.reshape(N_GX, V, N_GY, KTOT)

    def first_pass(items):
        numbers_row, panel_row, residual_row = items
        chosen = gather_rows(numbers_row, panel_row)
        return jnp.einsum('qrv,qvk->qrk', residual_row, chosen, precision=precise)

    parts = lax.map(first_pass, (numbers, panel_rows, vertex_res))
    block_count = N_GX * N_GY
    flat_parts = parts.reshape(block_count, NRHS, KTOT).transpose(1, 0, 2)
    collected = [flat_parts[:, :, :V]]
    offset = V
    for level in range(1, LY + LX + 1):
        width = KY if level <= LY else KX
        segment = flat_parts[:, :, offset:offset + width]
        group = 2 ** level
        grouped = segment.reshape(NRHS, block_count // group, group, width).sum(axis=2, keepdims=True)
        collected.append(jnp.broadcast_to(grouped, (NRHS, block_count // group, group, width)).reshape(NRHS, block_count, width))
        offset = offset + width
    coeff = jnp.concatenate(collected, axis=2)
    coeff_blocks = coeff.transpose(1, 0, 2).reshape(N_GX, N_GY, NRHS, KTOT)

    def second_pass(items):
        numbers_row, panel_row, coeff_row = items
        chosen = gather_rows(numbers_row, panel_row)
        return jnp.einsum('qrk,qvk->qrv', coeff_row, chosen, precision=precise)

    coarse_vertex = lax.map(second_pass, (numbers, panel_rows, coeff_blocks))
    coarse_vertex = coarse_vertex.reshape(N_GX, N_GY, NRHS, EX + 1, EY + 1, EZ + 1)
    gathered = []
    for shift_a in (0, 1):
        for shift_b in (0, 1):
            for shift_c in (0, 1):
                gathered.append(coarse_vertex[:, :, :, shift_a:shift_a + EX, shift_b:shift_b + EY, shift_c:shift_c + EZ])
    corners = jnp.stack(gathered, axis=3).reshape(N_GX, N_GY, NRHS, 2, 2, 2, EX, EY, EZ)
    points = jnp.einsum('pqrabcxyz,ai,bj,ck->rpxiqyjzk', corners, weights, weights, weights, precision=precise)
    return points.reshape(NRHS, NX, NY, NZ)


def reference(residual, elem_class, basis, eigenvalues, vertex_number, panels):
    fine = fine_part(residual, elem_class, basis, eigenvalues)
    coarse = coarse_part(residual, vertex_number, panels)
    return fine + coarse
```

```python
import functools

import jax
import jax.numpy as jnp
from jax import lax
from jax.experimental import pallas as pl
from jax.experimental.pallas import tpu as pltpu
from jax.sharding import PartitionSpec as P

NPR = 8
NEXT = 10
NCLASS = 8
LANES = 128
HALO = NPR + 1
F32 = jnp.float32
exact = lax.Precision.HIGHEST
ORDER = (1, 2, 3, 4, 5, 6, 7, 8, 0, 9)


def iota(shape, axis):
    return lax.broadcasted_iota(jnp.int32, shape, axis)


def hat(point, vertex):
    place = (point.astype(F32) + 0.5) / NPR
    return jnp.maximum(0.0, 1.0 - jnp.abs(place - vertex.astype(F32)))


def plane_hat(point, vertex):
    third = (vertex.astype(F32) + 0.5) / 3.0
    big = third.astype(jnp.int32)
    return hat(point >> 4, big) * hat(point & 15, vertex - 3 * big)


def down_kernel(res_ref, num_ref, pan_ref, pay_ref, own_ref, line_ref):
    q = lax.axis_index("gy")
    plane = plane_hat(iota((16, 512), 1), iota((16, 512), 0))
    depth = hat(iota((128, 17), 0), iota((128, 17), 1))
    half = jnp.dot(plane, res_ref[...], precision=exact)
    vertex = jnp.dot(half, depth, precision=exact)
    rows = iota((256, 17), 0)
    spread = jnp.zeros((256, 17), F32)
    for i in range(5):
        for j in range(3):
            k = 3 * i + j
            spread = spread + jnp.where(num_ref[i, j : j + 1, :] == rows, vertex[k : k + 1, :], 0.0)
    ordered = jnp.broadcast_to(jnp.sum(spread, axis=1, keepdims=True), (256, LANES))
    line_ref[...] = jnp.zeros((40, LANES), F32)
    for c in range(23):
        low = c * LANES
        width = min(LANES, 2943 - low)
        piece = jnp.sum(pan_ref[:, low : low + width] * ordered[:255, :width], axis=0, keepdims=True)
        line_ref[8 + c : 9 + c, :width] = piece
    here = pltpu.roll(line_ref[8:32], 1, 1)
    before = pltpu.roll(line_ref[7:31], 1, 1)
    own_ref[...] = jnp.where(iota((24, LANES), 1) == 0, before, here)
    low_face = res_ref[pl.ds(0, 32, stride=16), :]
    high_face = res_ref[pl.ds(15, 32, stride=16), :]
    for peer in range(8):
        pay_ref[peer, 0:32, :] = jnp.where(peer < q, low_face, high_face)
        pay_ref[peer, 32:35, :] = own_ref[2:5, :]
        if peer < 6:
            pay_ref[peer, 35:38, :] = own_ref[5 + 3 * peer : 8 + 3 * peer, :]
            pay_ref[peer, 38:40, :] = jnp.zeros((2, LANES), F32)
        else:
            pay_ref[peer, 35:40, :] = jnp.zeros((5, LANES), F32)


def share_kernel(got_ref, res_ref, cls_ref, right_ref, left_ref, tree_ref, face_ref):
    q = lax.axis_index("gy")
    face_ref[0:32, :] = jnp.where(q > 0, got_ref[jnp.maximum(q - 1, 0), 0:32, :], 0.0)
    face_ref[32:64, :] = jnp.where(q < 7, got_ref[jnp.minimum(q + 1, 7), 0:32, :], 0.0)
    for ref, column, first in ((right_ref, 3, 23), (left_ref, 0, 0)):
        ref[0:144, :] = res_ref[16 * first : 16 * first + 144, :]
        ref[144:153, :] = face_ref[first : first + 9, :]
        ref[153:162, :] = face_ref[32 + first : 41 + first, :]
        ref[162:168, :] = jnp.zeros((6, LANES), F32)
        ref[162:164, 0:16] = (cls_ref[column] + 1).astype(F32)
    total = got_ref[0, 35:38, :]
    for peer in range(1, 8):
        total = total + got_ref[peer, 35:38, :]
    line = jnp.concatenate([total[0:1], total[1:2], total[2:3]], axis=1)
    for t in range(64):
        tree_ref[t] = line


def shuffled(tile, first, second, third):
    tile = jnp.take_along_axis(tile, first, axis=1, mode="promise_in_bounds")
    tile = jnp.take_along_axis(tile, second, axis=0, mode="promise_in_bounds")
    return jnp.take_along_axis(tile, third, axis=1, mode="promise_in_bounds")


def fine_kernel(
    res_ref, face_ref, from_left, from_right, cls_ref, basis_ref, value_ref,
    fine_ref, rim_ref,
    rows_m, rows_e, win_m, win_e, pick_m, pick_e, eig_m, eig_e, zfwd_m, zback_m, zfwd_e, zback_e,
    half_e, lxe, work, tmp_a, tmp_b, tmp_c, edge, out_rows, rim_rows,
):
    sub = iota((8, LANES), 0)
    lane = iota((8, LANES), 1)
    wide = iota((16, LANES), 1)
    kz = lane & 15

    for ix in range(4):
        for jy in range(2):
            r = 2 * ix + jy
            for i in range(8):
                rows_m[pl.ds(i * 8 + r, 8, stride=64), :] = res_ref[pl.ds(128 * ix + 16 * i + 8 * jy, 8), :]
            rows_m[pl.ds(512 + r, 8, stride=8), :] = face_ref[pl.ds(32 * jy + 8 * ix, 8), :]
    for side, ref in ((0, from_left), (1, from_right)):
        for layer in range(9):
            i = (layer + 8) % 9 if side == 0 else layer
            for jy in range(2):
                part = ref[pl.ds(16 * layer + 8 * jy, 8), :]
                outer = ref[pl.ds(144 + 9 * jy + layer, 1), :]
                for r in (2 * side + jy, 4 + 2 * side + jy):
                    rows_e[pl.ds(i * 8 + r, 8, stride=72), :] = part
                    rows_e[pl.ds((72 + i) * 8 + r, 1), :] = outer

    group = iota((8, LANES), 0)
    spread = (iota((16, LANES), 0) == (iota((16, LANES), 1) & 15)).astype(F32)
    kinds = jnp.concatenate([cls_ref[ix].astype(F32) + 1.0 for ix in range(4)], axis=0)
    near = [from_left[162:164, 0:16], from_right[162:164, 0:16]]
    kinds_e = jnp.concatenate(near + near, axis=0)
    for kind, pick, eig in ((kinds, pick_m, eig_m), (kinds_e, pick_e, eig_e)):
        laid = jnp.dot(kind, spread, precision=exact)
        laid = jnp.sum(jnp.where(group == (lane >> 4), laid, 0.0), axis=0, keepdims=True)
        onehot = (laid == (group + 1).astype(F32)).astype(F32)
        dims = (((0,), (0,)), ((), ()))
        pick[0:300, :] = lax.dot_general(basis_ref[...], onehot, dims, precision=exact, preferred_element_type=F32)
        eig[0:30, :] = lax.dot_general(value_ref[...], onehot, dims, precision=exact, preferred_element_type=F32)
        empty = jnp.where(laid == 0.0, 1.0, 0.0)
        eig[20:30, :] = eig[20:30, :] + empty
        eig[30:36, :] = jnp.ones((6, LANES), F32)
    for pick, zfwd, zback in ((pick_m, zfwd_m, zback_m), (pick_e, zfwd_e, zback_e)):
        for n, k in enumerate(ORDER):
            zfwd[n, 0:10, :] = pick[200 + 10 * k : 210 + 10 * k, :]
            zfwd[n, 10:16, :] = jnp.zeros((6, LANES), F32)
        for c in range(10):
            zback[c, 0:8, :] = pick[pl.ds(210 + c, 8, stride=10), :]
            zback[c, 8:16, :] = jnp.zeros((8, LANES), F32)
            zback[c, 8:9, :] = pick[200 + c : 201 + c, :]
            zback[c, 9:10, :] = pick[290 + c : 291 + c, :]
    low_half = iota((5, LANES), 1) < 64
    for i in range(10):
        half_e[5 * i : 5 * i + 5, :] = jnp.where(low_half, pick_e[10 * i : 10 * i + 5, :], pick_e[10 * i + 5 : 10 * i + 10, :])
    half_e[50:55, :] = jnp.where((iota((5, LANES), 1) & 32) == 0, half_e[45:50, :], half_e[0:5, :])
    lxe[0:5, :] = jnp.where(low_half, eig_e[0:5, :], eig_e[5:10, :])

    turn_a = (lane & ~7) | ((lane - sub) & 7)
    turn_b = (lane - sub) & 7
    turn_c = ((lane & 15) << 3) | ((sub + (lane >> 4)) & 7)

    def place(tile):
        main = shuffled(tile, turn_a, turn_b, turn_c)
        before = jnp.where(kz == 0, 0.0, pltpu.roll(main, 1, 1))
        after = jnp.where(kz == 15, 0.0, pltpu.roll(main, 127, 1))
        tail = pltpu.roll(jnp.where(sub == 7, before, after), 1, 0)
        return main, jnp.where(sub < 2, tail, 0.0)

    def fill(rows, win, count):
        def step(j, _):
            for i in range(count):
                tile = rows[pl.ds(pl.multiple_of((j * count + i) * 8, 8), 8), :]
                main, tail = place(tile)
                dest = jnp.where(j == 8, 10, j + 1)
                win[i + 1, dest, 0:8, :] = main
                win[i + 1, dest, 8:16, :] = tail
            return 0
        lax.fori_loop(0, 9, step, 0)

    fill(rows_m, win_m, 8)
    fill(rows_e, win_e, 9)

    def x_halo(j, _):
        ahead = win_m[8, j]
        back = win_m[1, j]
        extra = win_e[9, j]
        win_m[0, j] = jnp.where(wide >= 32, pltpu.roll(ahead, 32, 1), win_e[8, j])
        win_m[9, j] = jnp.where(wide < 96, pltpu.roll(back, 96, 1), win_e[1, j])
        ahead = jnp.where(wide >= 64, ahead, pltpu.roll(ahead, 64, 1))
        back = jnp.where(wide < 64, back, pltpu.roll(back, 64, 1))
        second = (wide & 32) != 0
        win_e[0, j] = jnp.where(second, ahead, extra)
        win_e[9, j] = jnp.where(second, extra, back)
        return 0

    lax.fori_loop(1, 11, x_halo, 0)

    def y_halo(i, _):
        for win in (win_m, win_e):
            outer = win[i, 10]
            upper = (wide & 16) != 0
            win[i, 0] = jnp.where(upper, pltpu.roll(win[i, 8], 16, 1), outer)
            win[i, 9] = jnp.where(upper, outer, pltpu.roll(win[i, 1], 112, 1))
        return 0

    lax.fori_loop(0, 10, y_halo, 0)

    def row(ref, n):
        return jnp.broadcast_to(ref[pl.ds(n, 1), :], (16, LANES))

    def dot_rows(pairs):
        total = None
        for a, b in pairs:
            total = a * b if total is None else total + a * b
        return total

    def x_forward(win, table, count):
        def step(j, _):
            column = [win[i, j] for i in range(10)]
            for a in range(count):
                work[a, j] = dot_rows([(row(table, count * i + a), column[i]) for i in range(10)])
            return 0
        lax.fori_loop(0, 10, step, 0)

    def through_z(source, target, zfwd):
        table = [zfwd[k] for k in range(10)]
        for b in range(10):
            target[b] = dot_rows([(table[k], jnp.broadcast_to(source[b, k : k + 1, :], (16, LANES))) for k in range(10)])

    def y_forward(a, pick):
        column = [work[a, j] for j in range(10)]
        for b in range(10):
            tmp_a[b] = dot_rows([(row(pick, 100 + 10 * j + b), column[j]) for j in range(10)])

    def scale(a, eig, lx):
        level = row(lx, a) + eig[20:36, :]
        for b in range(10):
            tmp_b[b] = tmp_b[b] / (level + row(eig, 10 + b))

    def y_back(source, pick, store):
        column = [source[b] for b in range(10)]
        for j in range(10):
            store(j, dot_rows([(row(pick, 100 + 10 * j + b), column[b]) for b in range(10)]))

    x_forward(win_e, half_e, 5)
    for b in range(10):
        edge[b] = jnp.zeros((16, LANES), F32)

    def edge_step(a, _):
        y_forward(a, pick_e)
        through_z(tmp_a, tmp_b, zfwd_e)
        scale(a, eig_e, lxe)
        weight = row(half_e, 50 + a)
        for b in range(10):
            edge[b] = edge[b] + weight * tmp_b[b]
        return 0

    lax.fori_loop(0, 5, edge_step, 0)
    for b in range(10):
        tmp_b[b] = edge[b] + pltpu.roll(edge[b], 64, 1)
    through_z(tmp_b, tmp_c, zback_e)

    def put_edge(j, value):
        edge[j] = value

    y_back(tmp_c, pick_e, put_edge)

    x_forward(win_m, pick_m, 10)

    def main_step(a, _):
        y_forward(a, pick_m)
        through_z(tmp_a, tmp_b, zfwd_m)
        scale(a, eig_m, eig_m)
        through_z(tmp_b, tmp_c, zback_m)

        def put(j, value):
            work[a, j] = value

        y_back(tmp_c, pick_m, put)
        return 0

    lax.fori_loop(0, 10, main_step, 0)

    def x_back(j, _):
        column = [work[a, j] for a in range(10)]
        first = dot_rows([(row(pick_m, a), column[a]) for a in range(10)])
        last = dot_rows([(row(pick_m, 90 + a), column[a]) for a in range(10)])
        side = edge[j]
        for i in range(1, 9):
            total = dot_rows([(row(pick_m, 10 * i + a), column[a]) for a in range(10)])
            if i == 1:
                total = total + jnp.where(wide >= 32, pltpu.roll(last, 32, 1), side)
            if i == 8:
                total = total + jnp.where(wide < 96, pltpu.roll(first, 96, 1), side)
            main = total[0:8]
            tail = pltpu.roll(total[8:16], 7, 0)
            main = main + jnp.where(
                sub == 7,
                jnp.where(kz == 15, 0.0, pltpu.roll(tail, 127, 1)),
                jnp.where((sub == 0) & (kz != 0), pltpu.roll(tail, 1, 1), 0.0),
            )
            win_m[i, j, 0:8, :] = main
        return 0

    lax.fori_loop(0, 10, x_back, 0)

    back_a = (((lane - sub) & 7) << 4) | (lane >> 3)
    back_c = (lane & ~7) | ((lane + sub) & 7)
    upper = (lane & 16) != 0

    def unplace(i, _):
        first = win_m[i + 1, 0, 0:8, :]
        last = win_m[i + 1, 9, 0:8, :]
        for j in range(8):
            tile = win_m[i + 1, j + 1, 0:8, :]
            if j == 0:
                tile = tile + jnp.where(upper, pltpu.roll(last, 16, 1), 0.0)
            if j == 7:
                tile = tile + jnp.where(upper, 0.0, pltpu.roll(first, 112, 1))
            out_rows[pl.ds(pl.multiple_of((i * 8 + j) * 8, 8), 8), :] = shuffled(tile, back_a, turn_b, back_c)
        tile = jnp.where(upper, last, first)
        rim_rows[pl.ds(pl.multiple_of(i * 8, 8), 8), :] = shuffled(tile, back_a, turn_b, back_c)
        return 0

    lax.fori_loop(0, 8, unplace, 0)

    for ix in range(4):
        for jy in range(2):
            r = 2 * ix + jy
            for i in range(8):
                fine_ref[pl.ds(128 * ix + 16 * i + 8 * jy, 8), :] = out_rows[pl.ds(64 * i + r, 8, stride=8), :]
            rim_ref[pl.ds(32 * jy + 8 * ix, 8), :] = rim_rows[pl.ds(r, 8, stride=8), :]


def tree_kernel(got_ref, rim_ref, pay_ref):
    p = lax.axis_index("gx")
    q = lax.axis_index("gy")
    bits = q + 1
    total = jnp.zeros((1, 384), F32)
    for t in range(64):
        inside = (t >> bits) == (p >> bits)
        total = total + jnp.where(inside, got_ref[t], 0.0)
    for peer in range(8):
        pay_ref[peer, 0:32, :] = jnp.where(peer < q, rim_ref[0:32, :], rim_ref[32:64, :])
        for n in range(3):
            pay_ref[peer, 32 + n : 33 + n, :] = total[:, LANES * n : LANES * (n + 1)]
        pay_ref[peer, 35:40, :] = jnp.zeros((5, LANES), F32)


def up_kernel(first_ref, own_ref, got_ref, pan_ref, num_ref, fine_ref, out_ref, line_ref, value_ref, vertex_ref):
    q = lax.axis_index("gy")
    line_ref[...] = jnp.zeros((32, LANES), F32)
    line_ref[0:2, :] = own_ref[0:2, :]
    for level in range(1, 4):
        total = jnp.zeros((1, LANES), F32)
        for peer in range(8):
            inside = (peer >> level) == (q >> level)
            total = total + jnp.where(inside, first_ref[peer, 31 + level : 32 + level, :], 0.0)
        line_ref[1 + level : 2 + level, :] = total
    for peer in range(6):
        line_ref[5 + 3 * peer : 8 + 3 * peer, :] = got_ref[peer, 32:35, :]
    here = pltpu.roll(line_ref[0:24], 127, 1)
    after = pltpu.roll(line_ref[1:25], 127, 1)
    coeff = jnp.where(iota((24, LANES), 1) == 127, after, here)
    for low in range(0, 255, 64):
        high = min(low + 64, 255)
        total = pan_ref[low:high, 0:LANES] * coeff[0:1]
        for c in range(1, 22):
            total = total + pan_ref[low:high, c * LANES : (c + 1) * LANES] * coeff[c : c + 1]
        value = jnp.sum(total, axis=1, keepdims=True)
        value = value + jnp.sum(pan_ref[low:high, 2816:2943] * coeff[22:23, 0:127], axis=1, keepdims=True)
        value_ref[low:high, :] = jnp.broadcast_to(value, (high - low, LANES))
    value_ref[255:256, :] = jnp.zeros((1, LANES), F32)
    vertex_ref[...] = jnp.zeros((16, LANES), F32)
    rows = iota((256, 17), 0)
    values = value_ref[:, 0:17]
    for i in range(5):
        for j in range(3):
            k = 3 * i + j
            vertex_ref[k : k + 1, 0:17] = jnp.sum(jnp.where(num_ref[i, j : j + 1, :] == rows, values, 0.0), axis=0, keepdims=True)
    depth = hat(iota((LANES, LANES), 1), iota((LANES, LANES), 0))
    plane = plane_hat(iota((512, 16), 0), iota((512, 16), 1))
    half = jnp.dot(vertex_ref[...], depth, precision=exact)
    out_ref[...] = fine_ref[...] + jnp.dot(plane, half, precision=exact)
    low_face = jnp.where(q > 0, got_ref[jnp.maximum(q - 1, 0), 0:32, :], 0.0)
    high_face = jnp.where(q < 7, got_ref[jnp.minimum(q + 1, 7), 0:32, :], 0.0)
    out_ref[pl.ds(0, 32, stride=16), :] = out_ref[pl.ds(0, 32, stride=16), :] + low_face
    out_ref[pl.ds(15, 32, stride=16), :] = out_ref[pl.ds(15, 32, stride=16), :] + high_face


def call(kernel, outs, scratch=(), flops=0, bytes_accessed=0, limit=40):
    shapes = [jax.ShapeDtypeStruct(s, F32) for s in outs]
    return pl.pallas_call(
        kernel,
        out_shape=shapes,
        scratch_shapes=[pltpu.VMEM(s, F32) for s in scratch],
        compiler_params=pltpu.CompilerParams(vmem_limit_bytes=limit << 20),
        cost_estimate=pl.CostEstimate(flops=flops, bytes_accessed=bytes_accessed, transcendentals=0),
    )


def spread_to(block, axis):
    return lax.all_to_all(block, axis, 0, 0, tiled=True)


FINE_SCRATCH = (
    (576, 128), (648, 128), (10, 11, 16, 128), (10, 11, 16, 128),
    (304, 128), (304, 128), (40, 128), (40, 128),
    (10, 16, 128), (10, 16, 128), (10, 16, 128), (10, 16, 128),
    (56, 128), (8, 128), (10, 10, 16, 128),
    (10, 16, 128), (10, 16, 128), (10, 16, 128), (10, 16, 128),
    (512, 128), (64, 128),
)


def shards(residual, elem_class, basis, eigenvalues, vertex_number, panels):
    field = residual.reshape(512, LANES)
    table = basis.reshape(NCLASS, 3 * NEXT * NEXT)
    values = eigenvalues.reshape(NCLASS, 3 * NEXT)
    pay, own = call(down_kernel, [(8, 40, 128), (24, 128)], [(40, 128)])(field, vertex_number, panels)
    first = spread_to(pay, "gy")
    right, left, tree, face = call(
        share_kernel, [(168, 128), (168, 128), (64, 1, 384), (64, 128)]
    )(first, field, elem_class)
    from_left = lax.ppermute(right, "gx", [(i, i + 1) for i in range(63)])
    from_right = lax.ppermute(left, "gx", [(i + 1, i) for i in range(63)])
    summed = spread_to(tree, "gx")
    fine, rim = call(fine_kernel, [(512, 128), (64, 128)], FINE_SCRATCH, flops=8_000_000_000, bytes_accessed=20_000_000)(
        field, face, from_left, from_right, elem_class, table, values
    )
    (pay,) = call(tree_kernel, [(8, 40, 128)])(summed, rim)
    second = spread_to(pay, "gy")
    (out,) = call(up_kernel, [(512, 128)], [(32, 128), (256, 128), (16, 128)])(
        first, own, second, panels, vertex_number, fine
    )
    return out.reshape(residual.shape)


def solution(mesh):
    return jax.shard_map(
        shards,
        mesh=mesh,
        in_specs=(
            P(None, "gx", "gy", None),
            P("gx", "gy", None),
            P(),
            P(),
            P("gx", "gy", None),
            P("gx", "gy"),
        ),
        out_specs=P(None, "gx", "gy", None),
        check_vma=False,
    )
```

```python
import functools

import jax
import jax.numpy as jnp
from jax import lax
from jax.experimental import pallas as pl
from jax.experimental.pallas import tpu as pltpu
from jax.sharding import PartitionSpec as P

NPR = 8
NEXT = 10
NCLASS = 8
LANES = 128
HALO = NPR + 1
F32 = jnp.float32
exact = lax.Precision.HIGHEST
ORDER = (1, 2, 3, 4, 5, 6, 7, 8, 0, 9)


def iota(shape, axis):
    return lax.broadcasted_iota(jnp.int32, shape, axis)


def hat(point, vertex):
    place = (point.astype(F32) + 0.5) / NPR
    return jnp.maximum(0.0, 1.0 - jnp.abs(place - vertex.astype(F32)))


def plane_hat(point, vertex):
    third = (vertex.astype(F32) + 0.5) / 3.0
    big = third.astype(jnp.int32)
    return hat(point >> 4, big) * hat(point & 15, vertex - 3 * big)


def down_kernel(
    res_hbm, num_hbm, pan_hbm, cls_hbm, basis_hbm, value_hbm,
    pay_ref, own_ref, res_ref, num_ref, cls_ref, basis_ref, value_ref,
    line_ref, pan_ref, sems,
):
    q = lax.axis_index("gy")
    pairs = (
        (res_hbm, res_ref), (num_hbm, num_ref), (pan_hbm, pan_ref),
        (cls_hbm, cls_ref), (basis_hbm, basis_ref), (value_hbm, value_ref),
    )
    copies = [pltpu.make_async_copy(source, target, sems.at[n]) for n, (source, target) in enumerate(pairs)]
    for copy in copies:
        copy.start()
    plane = plane_hat(iota((16, 512), 1), iota((16, 512), 0))
    depth = hat(iota((128, 17), 0), iota((128, 17), 1))
    line_ref[...] = jnp.zeros((40, LANES), F32)
    copies[0].wait()
    half = jnp.dot(plane, res_ref[...], precision=exact)
    vertex = jnp.dot(half, depth, precision=exact)
    low_face = res_ref[pl.ds(0, 32, stride=16), :]
    high_face = res_ref[pl.ds(15, 32, stride=16), :]
    for peer in range(8):
        pay_ref[peer, 0:32, :] = jnp.where(peer < q, low_face, high_face)
    copies[1].wait()
    rows = iota((256, 17), 0)
    spread = jnp.zeros((256, 17), F32)
    for i in range(5):
        for j in range(3):
            k = 3 * i + j
            spread = spread + jnp.where(num_ref[i, j : j + 1, :] == rows, vertex[k : k + 1, :], 0.0)
    ordered = jnp.broadcast_to(jnp.sum(spread, axis=1, keepdims=True), (256, LANES))
    for copy in copies[2:]:
        copy.wait()
    for c in range(23):
        low = c * LANES
        width = min(LANES, 2943 - low)
        piece = jnp.sum(pan_ref[:, low : low + width] * ordered[:255, :width], axis=0, keepdims=True)
        line_ref[8 + c : 9 + c, :width] = piece
    here = pltpu.roll(line_ref[8:32], 1, 1)
    before = pltpu.roll(line_ref[7:31], 1, 1)
    own_ref[...] = jnp.where(iota((24, LANES), 1) == 0, before, here)
    for peer in range(8):
        pay_ref[peer, 32:35, :] = own_ref[2:5, :]
        if peer < 6:
            pay_ref[peer, 35:38, :] = own_ref[5 + 3 * peer : 8 + 3 * peer, :]
            pay_ref[peer, 38:40, :] = jnp.zeros((2, LANES), F32)
        else:
            pay_ref[peer, 35:40, :] = jnp.zeros((5, LANES), F32)


def share_kernel(got_ref, res_ref, cls_ref, right_ref, left_ref, tree_ref, face_ref):
    q = lax.axis_index("gy")
    face_ref[0:32, :] = jnp.where(q > 0, got_ref[jnp.maximum(q - 1, 0), 0:32, :], 0.0)
    face_ref[32:64, :] = jnp.where(q < 7, got_ref[jnp.minimum(q + 1, 7), 0:32, :], 0.0)
    for ref, column, first in ((right_ref, 3, 23), (left_ref, 0, 0)):
        ref[0:144, :] = res_ref[16 * first : 16 * first + 144, :]
        ref[144:153, :] = face_ref[first : first + 9, :]
        ref[153:162, :] = face_ref[32 + first : 41 + first, :]
        ref[162:168, :] = jnp.zeros((6, LANES), F32)
        ref[162:164, 0:16] = (cls_ref[column] + 1).astype(F32)
    total = got_ref[0, 35:38, :]
    for peer in range(1, 8):
        total = total + got_ref[peer, 35:38, :]
    line = jnp.concatenate([total[0:1], total[1:2], total[2:3]], axis=1)
    for t in range(64):
        tree_ref[t] = line


def shuffled(tile, first, second, third):
    tile = jnp.take_along_axis(tile, first, axis=1, mode="promise_in_bounds")
    tile = jnp.take_along_axis(tile, second, axis=0, mode="promise_in_bounds")
    return jnp.take_along_axis(tile, third, axis=1, mode="promise_in_bounds")


def grids():
    sub = iota((8, LANES), 0)
    lane = iota((8, LANES), 1)
    return sub, lane, lane & 15


def place(tile, sub, lane, kz):
    turn_a = (lane & ~7) | ((lane - sub) & 7)
    turn_b = (lane - sub) & 7
    turn_c = ((lane & 15) << 3) | ((sub + (lane >> 4)) & 7)
    main = shuffled(tile, turn_a, turn_b, turn_c)
    before = jnp.where(kz == 0, 0.0, pltpu.roll(main, 1, 1))
    after = jnp.where(kz == 15, 0.0, pltpu.roll(main, 127, 1))
    tail = pltpu.roll(jnp.where(sub == 7, before, after), 1, 0)
    return main, jnp.where(sub < 2, tail, 0.0)


def unplace(tile, sub, lane):
    back_a = (((lane - sub) & 7) << 4) | (lane >> 3)
    back_c = (lane & ~7) | ((lane + sub) & 7)
    return shuffled(tile, back_a, (lane - sub) & 7, back_c)


def join_z(total, sub, kz):
    main = total[0:8]
    tail = pltpu.roll(total[8:16], 7, 0)
    return main + jnp.where(
        sub == 7,
        jnp.where(kz == 15, 0.0, pltpu.roll(tail, 127, 1)),
        jnp.where((sub == 0) & (kz != 0), pltpu.roll(tail, 1, 1), 0.0),
    )


def row(ref, n):
    return jnp.broadcast_to(ref[pl.ds(n, 1), :], (16, LANES))


def dot_rows(pairs):
    total = None
    for a, b in pairs:
        total = a * b if total is None else total + a * b
    return total


def pick_tables(kind, table_ref, eigen_ref, pick, eig, zfwd, zback):
    group = iota((8, LANES), 0)
    lane = iota((8, LANES), 1)
    spread = (iota((16, LANES), 0) == (iota((16, LANES), 1) & 15)).astype(F32)
    laid = jnp.dot(kind, spread, precision=exact)
    laid = jnp.sum(jnp.where(group == (lane >> 4), laid, 0.0), axis=0, keepdims=True)
    onehot = (laid == (group + 1).astype(F32)).astype(F32)
    dims = (((0,), (0,)), ((), ()))
    pick[0:300, :] = lax.dot_general(table_ref[:, 0:300], onehot, dims, precision=exact, preferred_element_type=F32)
    eig[0:30, :] = lax.dot_general(eigen_ref[:, 0:30], onehot, dims, precision=exact, preferred_element_type=F32)
    eig[20:30, :] = eig[20:30, :] + jnp.where(laid == 0.0, 1.0, 0.0)
    eig[30:40, :] = jnp.ones((10, LANES), F32)
    for n, k in enumerate(ORDER):
        zfwd[n, 0:10, :] = pick[200 + 10 * k : 210 + 10 * k, :]
        zfwd[n, 10:16, :] = jnp.zeros((6, LANES), F32)
    for c in range(10):
        zback[c, 0:8, :] = pick[pl.ds(210 + c, 8, stride=10), :]
        zback[c, 8:16, :] = jnp.zeros((8, LANES), F32)
        zback[c, 8:9, :] = pick[200 + c : 201 + c, :]
        zback[c, 9:10, :] = pick[290 + c : 291 + c, :]


def tile_kernel(
    res_ref, cls_ref, basis_ref, value_ref,
    win, table_ref, eigen_ref, pick, eig, zfwd, zback,
    rows_m,
):
    sub, lane, kz = grids()
    for d in range(3):
        eigen_ref[:, 10 * d : 10 * d + 10] = value_ref[d]
        for i in range(10):
            low = 100 * d + 10 * i
            table_ref[:, low : low + 10] = basis_ref[d, i]
    kind = jnp.concatenate([cls_ref[ix].astype(F32) + 1.0 for ix in range(4)], axis=0)
    pick_tables(kind, table_ref, eigen_ref, pick, eig, zfwd, zback)
    for ix in range(4):
        for jy in range(2):
            r = 2 * ix + jy
            for i in range(8):
                rows_m[pl.ds(i * 8 + r, 8, stride=64), :] = res_ref[pl.ds(128 * ix + 16 * i + 8 * jy, 8), :]

    def step(j, _):
        for i in range(8):
            main, tail = place(rows_m[pl.ds(pl.multiple_of((j * 8 + i) * 8, 8), 8), :], sub, lane, kz)
            win[i + 1, j + 1, 0:8, :] = main
            win[i + 1, j + 1, 8:16, :] = tail
        return 0

    lax.fori_loop(0, 8, step, 0)


def solve_kernel(
    win_in, table_ref, eigen_ref, pick_m, eig_m, zfwd_m, zback_m, face_ref, from_left, from_right,
    win_m, work, edge, ends, rim_ref,
    rows_e, rows_f, win_e, pick_e, eig_e, zfwd_e, zback_e, half_e, lxe, work_e, tmp_a, tmp_b, tmp_c, rim_rows,
):
    del win_in
    sub, lane, kz = grids()
    wide = iota((16, LANES), 1)
    upper = (wide & 16) != 0

    for ix in range(4):
        for jy in range(2):
            rows_f[pl.ds(2 * ix + jy, 8, stride=8), :] = face_ref[pl.ds(32 * jy + 8 * ix, 8), :]
    for side, ref in ((0, from_left), (1, from_right)):
        for layer in range(9):
            i = (layer + 8) % 9 if side == 0 else layer
            for jy in range(2):
                part = ref[pl.ds(16 * layer + 8 * jy, 8), :]
                outer = ref[pl.ds(144 + 9 * jy + layer, 1), :]
                for r in (2 * side + jy, 4 + 2 * side + jy):
                    rows_e[pl.ds(i * 8 + r, 8, stride=72), :] = part
                    rows_e[pl.ds((72 + i) * 8 + r, 1), :] = outer
    near = [from_left[162:164, 0:16], from_right[162:164, 0:16]]
    pick_tables(jnp.concatenate(near + near, axis=0), table_ref, eigen_ref, pick_e, eig_e, zfwd_e, zback_e)
    low_half = iota((5, LANES), 1) < 64
    for i in range(10):
        half_e[5 * i : 5 * i + 5, :] = jnp.where(low_half, pick_e[10 * i : 10 * i + 5, :], pick_e[10 * i + 5 : 10 * i + 10, :])
    half_e[50:55, :] = jnp.where((iota((5, LANES), 1) & 32) == 0, half_e[45:50, :], half_e[0:5, :])
    lxe[0:5, :] = jnp.where(low_half, eig_e[0:5, :], eig_e[5:10, :])

    for i in range(8):
        main, tail = place(rows_f[8 * i : 8 * i + 8, :], sub, lane, kz)
        win_m[i + 1, 10, 0:8, :] = main
        win_m[i + 1, 10, 8:16, :] = tail

    def fill(j, _):
        for i in range(9):
            main, tail = place(rows_e[pl.ds(pl.multiple_of((j * 9 + i) * 8, 8), 8), :], sub, lane, kz)
            dest = jnp.where(j == 8, 10, j + 1)
            win_e[i + 1, dest, 0:8, :] = main
            win_e[i + 1, dest, 8:16, :] = tail
        return 0

    lax.fori_loop(0, 9, fill, 0)

    def x_halo(j):
        ahead = win_m[8, j]
        back = win_m[1, j]
        extra = win_e[9, j]
        win_m[0, j] = jnp.where(wide >= 32, pltpu.roll(ahead, 32, 1), win_e[8, j])
        win_m[9, j] = jnp.where(wide < 96, pltpu.roll(back, 96, 1), win_e[1, j])
        ahead = jnp.where(wide >= 64, ahead, pltpu.roll(ahead, 64, 1))
        back = jnp.where(wide < 64, back, pltpu.roll(back, 64, 1))
        second = (wide & 32) != 0
        win_e[0, j] = jnp.where(second, ahead, extra)
        win_e[9, j] = jnp.where(second, extra, back)

    for j in (1, 2, 3, 4, 5, 6, 7, 8, 10):
        x_halo(j)

    def y_halo(i, _):
        for win in (win_m, win_e):
            outer = win[i, 10]
            win[i, 0] = jnp.where(upper, pltpu.roll(win[i, 8], 16, 1), outer)
            win[i, 9] = jnp.where(upper, outer, pltpu.roll(win[i, 1], 112, 1))
        return 0

    lax.fori_loop(0, 10, y_halo, 0)

    def x_forward(win, table, target, count):
        def step(j, _):
            column = [win[i, j] for i in range(10)]
            for a in range(count):
                target[a, j] = dot_rows([(row(table, count * i + a), column[i]) for i in range(10)])
            return 0
        lax.fori_loop(0, 10, step, 0)

    def through_z(source, target, zfwd):
        table = [zfwd[k] for k in range(10)]
        for b in range(10):
            target[b] = dot_rows([(table[k], jnp.broadcast_to(source[b, k : k + 1, :], (16, LANES))) for k in range(10)])

    def y_forward(a, source, pick):
        column = [source[a, j] for j in range(10)]
        for b in range(10):
            tmp_a[b] = dot_rows([(row(pick, 100 + 10 * j + b), column[j]) for j in range(10)])

    def scale(a, eig, lx):
        level = row(lx, a) + eig[20:36, :]
        for b in range(10):
            tmp_b[b] = tmp_b[b] / (level + row(eig, 10 + b))

    def y_back(source, pick, store):
        column = [source[b] for b in range(10)]
        for j in range(10):
            store(j, dot_rows([(row(pick, 100 + 10 * j + b), column[b]) for b in range(10)]))

    x_forward(win_e, half_e, work_e, 5)
    for b in range(10):
        edge[b] = jnp.zeros((16, LANES), F32)

    def edge_step(a, _):
        y_forward(a, work_e, pick_e)
        through_z(tmp_a, tmp_b, zfwd_e)
        scale(a, eig_e, lxe)
        weight = row(half_e, 50 + a)
        for b in range(10):
            edge[b] = edge[b] + weight * tmp_b[b]
        return 0

    lax.fori_loop(0, 5, edge_step, 0)
    for b in range(10):
        tmp_b[b] = edge[b] + pltpu.roll(edge[b], 64, 1)
    through_z(tmp_b, tmp_c, zback_e)

    def put_edge(j, value):
        edge[j] = value

    y_back(tmp_c, pick_e, put_edge)

    x_forward(win_m, pick_m, work, 10)

    def main_step(a, _):
        y_forward(a, work, pick_m)
        through_z(tmp_a, tmp_b, zfwd_m)
        scale(a, eig_m, eig_m)
        through_z(tmp_b, tmp_c, zback_m)

        def put(j, value):
            work[a, j] = value

        y_back(tmp_c, pick_m, put)
        return 0

    lax.fori_loop(0, 10, main_step, 0)

    for n, j in ((0, 0), (1, 9)):
        def put_end(i, main, n=n):
            ends[n, i - 1] = main

        x_back(work, edge, pick_m, j, put_end)
    for i in range(8):
        tile = jnp.where(upper[0:8], ends[1, i], ends[0, i])
        rim_rows[8 * i : 8 * i + 8, :] = unplace(tile, sub, lane)
    for ix in range(4):
        for jy in range(2):
            rim_ref[pl.ds(32 * jy + 8 * ix, 8), :] = rim_rows[pl.ds(2 * ix + jy, 8, stride=8), :]


def x_back(work, edge, pick, j, put):
    sub, lane, kz = grids()
    wide = iota((16, LANES), 1)
    column = [work[a, j] for a in range(10)]
    first = dot_rows([(row(pick, a), column[a]) for a in range(10)])
    last = dot_rows([(row(pick, 90 + a), column[a]) for a in range(10)])
    side = edge[j]
    for i in range(1, 9):
        total = dot_rows([(row(pick, 10 * i + a), column[a]) for a in range(10)])
        if i == 1:
            total = total + jnp.where(wide >= 32, pltpu.roll(last, 32, 1), side)
        if i == 8:
            total = total + jnp.where(wide < 96, pltpu.roll(first, 96, 1), side)
        put(i, join_z(total, sub, kz))


def back_kernel(work, edge, ends, pick, fine_ref, out_rows):
    sub, lane, kz = grids()
    upper = (lane & 16) != 0

    def step(j, _):
        def put(i, tile):
            tile = tile + jnp.where(upper & (j == 1), pltpu.roll(ends[1, i - 1], 16, 1), 0.0)
            tile = tile + jnp.where(upper | (j != 8), 0.0, pltpu.roll(ends[0, i - 1], 112, 1))
            out_rows[pl.ds(pl.multiple_of(((i - 1) * 8 + j - 1) * 8, 8), 8), :] = unplace(tile, sub, lane)

        x_back(work, edge, pick, j, put)
        return 0

    lax.fori_loop(1, 9, step, 0)
    for ix in range(4):
        for jy in range(2):
            r = 2 * ix + jy
            for i in range(8):
                fine_ref[pl.ds(128 * ix + 16 * i + 8 * jy, 8), :] = out_rows[pl.ds(64 * i + r, 8, stride=8), :]


def tree_kernel(got_ref, rim_ref, pay_ref):
    p = lax.axis_index("gx")
    q = lax.axis_index("gy")
    bits = q + 1
    total = jnp.zeros((1, 384), F32)
    for t in range(64):
        inside = (t >> bits) == (p >> bits)
        total = total + jnp.where(inside, got_ref[t], 0.0)
    for peer in range(8):
        pay_ref[peer, 0:32, :] = jnp.where(peer < q, rim_ref[0:32, :], rim_ref[32:64, :])
        for n in range(3):
            pay_ref[peer, 32 + n : 33 + n, :] = total[:, LANES * n : LANES * (n + 1)]
        pay_ref[peer, 35:40, :] = jnp.zeros((5, LANES), F32)


def up_kernel(
    first_ref, own_ref, got_ref, pan_hbm, num_ref, fine_ref, out_ref, line_ref, value_ref, vertex_ref, pan_ref, sems
):
    q = lax.axis_index("gy")
    copies = []
    for n, low in enumerate(range(0, 255, 64)):
        part = pl.ds(low, min(64, 255 - low))
        copies.append(pltpu.make_async_copy(pan_hbm.at[part, :], pan_ref.at[part, :], sems.at[n]))
        copies[n].start()
    line_ref[...] = jnp.zeros((32, LANES), F32)
    line_ref[0:2, :] = own_ref[0:2, :]
    for level in range(1, 4):
        total = jnp.zeros((1, LANES), F32)
        for peer in range(8):
            inside = (peer >> level) == (q >> level)
            total = total + jnp.where(inside, first_ref[peer, 31 + level : 32 + level, :], 0.0)
        line_ref[1 + level : 2 + level, :] = total
    for peer in range(6):
        line_ref[5 + 3 * peer : 8 + 3 * peer, :] = got_ref[peer, 32:35, :]
    here = pltpu.roll(line_ref[0:24], 127, 1)
    after = pltpu.roll(line_ref[1:25], 127, 1)
    coeff = jnp.where(iota((24, LANES), 1) == 127, after, here)
    for n, low in enumerate(range(0, 255, 64)):
        high = min(low + 64, 255)
        copies[n].wait()
        total = pan_ref[low:high, 0:LANES] * coeff[0:1]
        for c in range(1, 22):
            total = total + pan_ref[low:high, c * LANES : (c + 1) * LANES] * coeff[c : c + 1]
        value = jnp.sum(total, axis=1, keepdims=True)
        value = value + jnp.sum(pan_ref[low:high, 2816:2943] * coeff[22:23, 0:127], axis=1, keepdims=True)
        value_ref[low:high, :] = jnp.broadcast_to(value, (high - low, LANES))
    value_ref[255:256, :] = jnp.zeros((1, LANES), F32)
    vertex_ref[...] = jnp.zeros((16, LANES), F32)
    rows = iota((256, 17), 0)
    values = value_ref[:, 0:17]
    for i in range(5):
        for j in range(3):
            k = 3 * i + j
            vertex_ref[k : k + 1, 0:17] = jnp.sum(jnp.where(num_ref[i, j : j + 1, :] == rows, values, 0.0), axis=0, keepdims=True)
    depth = hat(iota((LANES, LANES), 1), iota((LANES, LANES), 0))
    plane = plane_hat(iota((512, 16), 0), iota((512, 16), 1))
    half = jnp.dot(vertex_ref[...], depth, precision=exact)
    out_ref[...] = fine_ref[...] + jnp.dot(plane, half, precision=exact)
    low_face = jnp.where(q > 0, got_ref[jnp.maximum(q - 1, 0), 0:32, :], 0.0)
    high_face = jnp.where(q < 7, got_ref[jnp.minimum(q + 1, 7), 0:32, :], 0.0)
    out_ref[pl.ds(0, 32, stride=16), :] = out_ref[pl.ds(0, 32, stride=16), :] + low_face
    out_ref[pl.ds(15, 32, stride=16), :] = out_ref[pl.ds(15, 32, stride=16), :] + high_face


VM = pltpu.VMEM
ANYWHERE = None


def call(kernel, outs, scratch=(), ins=None, sems=0, cost=0, limit=24, aliases=None):
    shapes = [
        jax.ShapeDtypeStruct(o[0], o[2] if len(o) > 2 else F32) if o[1] is None else o[1](o[0], o[2] if len(o) > 2 else F32)
        for o in outs
    ]
    spaces = [pltpu.VMEM(s, F32) for s in scratch]
    if sems:
        spaces.append(pltpu.SemaphoreType.DMA((sems,)))
    run = pl.pallas_call(
        kernel,
        out_shape=shapes,
        in_specs=[pl.BlockSpec(memory_space=m or pltpu.VMEM) for m in ins],
        out_specs=[pl.BlockSpec(memory_space=pltpu.VMEM) for _ in outs],
        scratch_shapes=spaces,
        input_output_aliases=aliases or {},
        compiler_params=pltpu.CompilerParams(vmem_limit_bytes=limit << 20),
        cost_estimate=pl.CostEstimate(flops=cost, bytes_accessed=cost // 400, transcendentals=0),
    )

    def apply(*operands):
        held = [x if m is None else pltpu.with_memory_space_constraint(x, m) for x, m in zip(operands, ins, strict=True)]
        return run(*held)

    return apply


def spread_to(block, axis):
    return lax.all_to_all(block, axis, 0, 0, tiled=True)


def shards(residual, elem_class, basis, eigenvalues, vertex_number, panels):
    field = residual.reshape(512, LANES)
    I32 = jnp.int32
    pay, own, res, num, cls, table, eigen = call(
        down_kernel,
        [
            ((8, 40, 128), None), ((24, 128), VM), ((512, 128), VM), ((5, 3, 17), VM, I32),
            ((4, 2, 16), VM, I32), ((3, 10, 8, 10), VM), ((3, 8, 10), VM),
        ],
        [(40, 128), (255, 2943)], ins=[pltpu.HBM] * 6, sems=6,
    )(field, vertex_number, panels, elem_class, basis.transpose(1, 2, 0, 3), eigenvalues.transpose(1, 0, 2))
    first = spread_to(pay, "gy")
    win, basis2, eigen2, pick, eig, zfwd, zback = call(
        tile_kernel,
        [
            ((10, 11, 16, 128), VM), ((8, 300), VM), ((8, 30), VM), ((304, 128), VM), ((40, 128), VM),
            ((10, 16, 128), VM), ((10, 16, 128), VM),
        ],
        [(512, 128)], ins=[VM] * 4, cost=2_000_000_000,
    )(res, cls, table, eigen)
    right, left, tree, face = call(
        share_kernel, [((168, 128), None), ((168, 128), None), ((64, 1, 384), None), ((64, 128), VM)], ins=[None, VM, VM]
    )(first, res, cls)
    from_left = lax.ppermute(right, "gx", [(i, i + 1) for i in range(63)])
    from_right = lax.ppermute(left, "gx", [(i + 1, i) for i in range(63)])
    summed = spread_to(tree, "gx")
    win, work, edge, ends, rim = call(
        solve_kernel,
        [((10, 11, 16, 128), VM), ((10, 10, 16, 128), VM), ((10, 16, 128), VM), ((2, 8, 8, 128), VM), ((64, 128), VM)],
        [
            (648, 128), (64, 128), (10, 11, 16, 128), (304, 128), (40, 128), (10, 16, 128), (10, 16, 128),
            (56, 128), (8, 128), (5, 10, 16, 128), (10, 16, 128), (10, 16, 128), (10, 16, 128), (64, 128),
        ],
        ins=[VM] * 8 + [None, None], cost=8_000_000_000, aliases={0: 0},
    )(win, basis2, eigen2, pick, eig, zfwd, zback, face, from_left, from_right)
    (pay,) = call(tree_kernel, [((8, 40, 128), None)], ins=[None, VM])(summed, rim)
    second = spread_to(pay, "gy")
    (fine,) = call(back_kernel, [((512, 128), VM)], [(512, 128)], ins=[VM] * 4, cost=3_000_000_000)(work, edge, ends, pick)
    (out,) = call(up_kernel, [((512, 128), None)], [(32, 128), (256, 128), (16, 128), (255, 2943)], ins=[None, VM, None, pltpu.HBM, VM, VM], sems=4)(
        first, own, second, panels, num, fine
    )
    return out.reshape(residual.shape)


def solution(mesh):
    return jax.shard_map(
        shards,
        mesh=mesh,
        in_specs=(
            P(None, "gx", "gy", None),
            P("gx", "gy", None),
            P(),
            P(),
            P("gx", "gy", None),
            P("gx", "gy"),
        ),
        out_specs=P(None, "gx", "gy", None),
        check_vma=False,
    )
```

```python
import functools

import jax
import jax.numpy as jnp
from jax import lax
from jax.experimental import pallas as pl
from jax.experimental.pallas import tpu as pltpu
from jax.sharding import PartitionSpec as P

NPR = 8
NEXT = 10
NCLASS = 8
LANES = 128
TOP = 128
CUTS = [(slice(low, min(low + 128, 2943)), min(128, 2943 - low)) for low in range(0, 2943, 128)]
HALO = NPR + 1
F32 = jnp.float32
exact = lax.Precision.HIGHEST
ORDER = (1, 2, 3, 4, 5, 6, 7, 8, 0, 9)


def iota(shape, axis):
    return lax.broadcasted_iota(jnp.int32, shape, axis)


def hat(point, vertex):
    place = (point.astype(F32) + 0.5) / NPR
    return jnp.maximum(0.0, 1.0 - jnp.abs(place - vertex.astype(F32)))


def moved(rows, table):
    high = rows.astype(jnp.bfloat16)
    rest = rows - high.astype(F32)
    middle = rest.astype(jnp.bfloat16)
    low = (rest - middle.astype(F32)).astype(jnp.bfloat16)
    total = jnp.dot(low, table, preferred_element_type=F32)
    total = total + jnp.dot(middle, table, preferred_element_type=F32)
    return total + jnp.dot(high, table, preferred_element_type=F32)


def plane_hat(point, vertex):
    third = (vertex.astype(F32) + 0.5) / 3.0
    big = third.astype(jnp.int32)
    return hat(point >> 4, big) * hat(point & 15, vertex - 3 * big)


def down_kernel(
    res_hbm, num_hbm, pan_hbm, cls_hbm, basis_hbm, value_hbm,
    pay_ref, own_ref, num_ref, cls_ref, top_ref, win, table_ref, eigen_ref, pick, eig, zfwd, zback, rows_ref,
    res_ref, basis_ref, value_ref, line_ref, low_ref, sems,
):
    q = lax.axis_index("gy")
    pairs = [
        (res_hbm, res_ref), (num_hbm, num_ref), (cls_hbm, cls_ref), (basis_hbm, basis_ref), (value_hbm, value_ref),
        (pan_hbm.at[pl.ds(0, TOP), :], top_ref), (pan_hbm.at[pl.ds(TOP, 255 - TOP), :], low_ref),
    ]
    copies = [pltpu.make_async_copy(source, target, sems.at[n]) for n, (source, target) in enumerate(pairs)]
    for copy in copies:
        copy.start()
    plane = plane_hat(iota((16, 512), 1), iota((16, 512), 0))
    depth = hat(iota((128, 17), 0), iota((128, 17), 1))
    line_ref[...] = jnp.zeros((40, LANES), F32)
    copies[0].wait()
    half = jnp.dot(plane, res_ref[...], precision=exact)
    vertex = jnp.dot(half, depth, precision=exact)
    low_face = res_ref[pl.ds(0, 32, stride=16), :]
    high_face = res_ref[pl.ds(15, 32, stride=16), :]
    for peer in range(8):
        pay_ref[peer, 0:32, :] = jnp.where(peer < q, low_face, high_face)
    copies[1].wait()
    rows = iota((256, 17), 0)
    spread = jnp.zeros((256, 17), F32)
    for i in range(5):
        for j in range(3):
            k = 3 * i + j
            spread = spread + jnp.where(num_ref[i, j : j + 1, :] == rows, vertex[k : k + 1, :], 0.0)
    ordered = jnp.broadcast_to(jnp.sum(spread, axis=1, keepdims=True), (256, LANES))

    rows_ref[...] = split_z(res_ref[...])
    for copy in copies[2:5]:
        copy.wait()
    for d in range(3):
        eigen_ref[:, 10 * d : 10 * d + 10] = value_ref[d]
        for i in range(10):
            low = 100 * d + 10 * i
            table_ref[:, low : low + 10] = basis_ref[d, i]
    kind = jnp.concatenate([cls_ref[ix].astype(F32) + 1.0 for ix in range(4)], axis=0)
    pick_tables(kind, table_ref, eigen_ref, pick, eig, zfwd, zback)
    columns = range(8)
    groups = [[rows_ref[128 * (r // 2) + 16 * i + 8 * (r % 2) : 128 * (r // 2) + 16 * i + 8 * (r % 2) + 8, :] for r in range(8)] for i in columns]
    for i, parts in zip(columns, with_outer(exchange(groups)), strict=True):
        for k, part in enumerate(parts):
            win[pl.ds((i * 11 + 12) * 16 + k, 8, stride=16), :] = part

    for copy in copies[5:]:
        copy.wait()
    for c, (cut, width) in enumerate(CUTS):
        piece = jnp.sum(top_ref[:, cut] * ordered[:TOP, :width], axis=0, keepdims=True)
        piece = piece + jnp.sum(low_ref[:, cut] * ordered[TOP:255, :width], axis=0, keepdims=True)
        line_ref[8 + c : 9 + c, :width] = piece
    here = pltpu.roll(line_ref[8:32], 1, 1)
    before = pltpu.roll(line_ref[7:31], 1, 1)
    own_ref[...] = jnp.where(iota((24, LANES), 1) == 0, before, here)
    for peer in range(8):
        pay_ref[peer, 32:35, :] = own_ref[2:5, :]
        pay_ref[peer, 35:37, :] = own_ref[8 + 2 * peer : 10 + 2 * peer, :]
        pay_ref[peer, 37:40, :] = own_ref[5:8, :] if peer == 7 else jnp.zeros((3, LANES), F32)


def share_kernel(got_ref, rows_ref, cls_ref, right_ref, left_ref, tree_ref, face_ref, four_ref):
    q = lax.axis_index("gy")
    face_ref[0:32, :] = jnp.where(q > 0, got_ref[jnp.maximum(q - 1, 0), 0:32, :], 0.0)
    face_ref[32:64, :] = jnp.where(q < 7, got_ref[jnp.minimum(q + 1, 7), 0:32, :], 0.0)
    total = got_ref[0, 35:40, :]
    for peer in range(1, 8):
        total = total + got_ref[peer, 35:40, :]
    four_ref[...] = jnp.zeros((8, LANES), F32)
    four_ref[0:3, :] = total[2:5]
    for level in range(1, 4):
        low = jnp.zeros((1, LANES), F32)
        for peer in range(8):
            inside = (peer >> level) == (q >> level)
            low = low + jnp.where(inside, got_ref[peer, 31 + level : 32 + level, :], 0.0)
        four_ref[2 + level : 3 + level, :] = low
    for ref, column, first in ((right_ref, 3, 23), (left_ref, 0, 0)):
        ref[0:144, :] = rows_ref[16 * first : 16 * first + 144, :]
        ref[144:153, :] = face_ref[first : first + 9, :]
        ref[153:162, :] = face_ref[32 + first : 41 + first, :]
        ref[162:168, :] = jnp.zeros((6, LANES), F32)
        ref[162:164, 0:16] = (cls_ref[column] + 1).astype(F32)
        ref[164:167, :] = total[2:5]
    line = jnp.concatenate([total[0:1], total[1:2]], axis=1)
    for t in range(64):
        tree_ref[t] = line


def grids():
    sub = iota((8, LANES), 0)
    lane = iota((8, LANES), 1)
    return sub, lane, lane & 15


def split_z(rows):
    lane = iota((LANES, LANES), 1)
    return moved(rows, (iota((LANES, LANES), 0) == (((lane & 15) << 3) | (lane >> 4))).astype(jnp.bfloat16))


def join_rows(rows):
    lane = iota((LANES, LANES), 0)
    return moved(rows, (iota((LANES, LANES), 1) == (((lane & 15) << 3) | (lane >> 4))).astype(jnp.bfloat16))


def exchange(groups):
    lane = iota((8, LANES), 1)
    groups = [list(parts) for parts in groups]
    for bit in (4, 2, 1):
        inside = (lane & (16 * bit)) != 0
        for parts in groups:
            for n in range(8):
                if n & bit:
                    continue
                low, high = parts[n], parts[n | bit]
                if bit == 4:
                    swap = pltpu.roll(jnp.where(inside, low, high), 64, 1)
                    parts[n] = jnp.where(inside, swap, low)
                    parts[n | bit] = jnp.where(inside, high, swap)
                else:
                    parts[n] = jnp.where(inside, pltpu.roll(high, 16 * bit, 1), low)
                    parts[n | bit] = jnp.where(inside, high, pltpu.roll(low, LANES - 16 * bit, 1))
    return groups


def with_outer(groups):
    kz = iota((8, LANES), 1) & 15
    before = [jnp.where(kz == 0, 0.0, pltpu.roll(parts[7], 1, 1)) for parts in groups]
    after = [jnp.where(kz == 15, 0.0, pltpu.roll(parts[0], 127, 1)) for parts in groups]
    return [parts + [b, a] for parts, b, a in zip(groups, before, after, strict=True)]


def at(i, j):
    return pl.ds(pl.multiple_of((i * 11 + j) * 16, 16), 16)


def join_z(total, sub, kz):
    main = total[0:8]
    tail = pltpu.roll(total[8:16], 7, 0)
    return main + jnp.where(
        sub == 7,
        jnp.where(kz == 15, 0.0, pltpu.roll(tail, 127, 1)),
        jnp.where((sub == 0) & (kz != 0), pltpu.roll(tail, 1, 1), 0.0),
    )


def row(ref, n):
    return jnp.broadcast_to(ref[pl.ds(n, 1), :], (16, LANES))


def dot_rows(pairs):
    total = None
    for a, b in pairs:
        total = a * b if total is None else total + a * b
    return total


def pick_tables(kind, table_ref, eigen_ref, pick, eig, zfwd, zback):
    group = iota((8, LANES), 0)
    lane = iota((8, LANES), 1)
    spread = (iota((16, LANES), 0) == (iota((16, LANES), 1) & 15)).astype(F32)
    laid = jnp.dot(kind, spread, precision=exact)
    laid = jnp.sum(jnp.where(group == (lane >> 4), laid, 0.0), axis=0, keepdims=True)
    onehot = (laid == (group + 1).astype(F32)).astype(F32)
    dims = (((0,), (0,)), ((), ()))
    pick[0:300, :] = lax.dot_general(table_ref[:, 0:300], onehot, dims, precision=exact, preferred_element_type=F32)
    eig[0:30, :] = lax.dot_general(eigen_ref[:, 0:30], onehot, dims, precision=exact, preferred_element_type=F32)
    eig[20:30, :] = eig[20:30, :] + jnp.where(laid == 0.0, 1.0, 0.0)
    eig[30:40, :] = jnp.ones((10, LANES), F32)
    for n, k in enumerate(ORDER):
        zfwd[n, 0:10, :] = pick[200 + 10 * k : 210 + 10 * k, :]
        zfwd[n, 10:16, :] = jnp.zeros((6, LANES), F32)
    for c in range(10):
        zback[c, 0:8, :] = pick[pl.ds(210 + c, 8, stride=10), :]
        zback[c, 8:16, :] = jnp.zeros((8, LANES), F32)
        zback[c, 8:9, :] = pick[200 + c : 201 + c, :]
        zback[c, 9:10, :] = pick[290 + c : 291 + c, :]


def solve_kernel(
    win_in, table_ref, eigen_ref, pick_m, eig_m, zfwd_m, zback_m, face_ref, from_left, from_right,
    win_m, fine_ref, rim_ref,
    work, edge, ends, tiles, rows_ref, rows_f, win_e, pick_e, eig_e, zfwd_e, zback_e, half_e, lxe, work_e, tmp_a, tmp_b, tmp_c, rim_rows,
):
    del win_in
    sub, lane, kz = grids()
    wide = iota((16, LANES), 1)
    upper = (wide & 16) != 0

    rows_f[0:64, :] = face_ref[...]
    rows_f[64:88, :] = from_left[144:168, :]
    rows_f[88:112, :] = from_right[144:168, :]
    rows_f[...] = split_z(rows_f[...])
    outer = [rows_f[32 * (r % 2) + 8 * (r // 2) : 32 * (r % 2) + 8 * (r // 2) + 8, :] for r in range(8)]
    beside = [rows_f[first : first + 8, :] for first in (65, 74, 88, 97)]
    corner = [jnp.broadcast_to(rows_f[n : n + 1, :], (8, LANES)) for n in (64, 73, 96, 105)]
    outer, beside, corner = with_outer(exchange([outer, beside + beside, corner + corner]))
    for k in range(10):
        win_m[pl.ds(21 * 16 + k, 8, stride=176), :] = outer[k]
        win_e[pl.ds(21 * 16 + k, 8, stride=176), :] = beside[k]
        win_e[109 * 16 + k : 109 * 16 + k + 1, :] = corner[k][0:1]

    def fill(n, _):
        columns = [9 * n + m for m in range(9)]
        groups = []
        for i in columns:
            layer = jnp.where(i == 8, 0, i + 1)
            parts = [from_left[pl.ds(pl.multiple_of(16 * layer + 8 * jy, 8), 8), :] for jy in range(2)]
            parts += [from_right[pl.ds(pl.multiple_of(16 * i + 8 * jy, 8), 8), :] for jy in range(2)]
            groups.append(parts + parts)
        for i, parts in zip(columns, with_outer(exchange(groups)), strict=True):
            for k, part in enumerate(parts):
                win_e[pl.ds((i * 11 + 12) * 16 + k, 8, stride=16), :] = part
        return 0

    lax.fori_loop(0, 1, fill, 0)

    near = [from_left[162:164, 0:16], from_right[162:164, 0:16]]
    pick_tables(jnp.concatenate(near + near, axis=0), table_ref, eigen_ref, pick_e, eig_e, zfwd_e, zback_e)
    low_half = iota((5, LANES), 1) < 64
    for i in range(10):
        half_e[5 * i : 5 * i + 5, :] = jnp.where(low_half, pick_e[10 * i : 10 * i + 5, :], pick_e[10 * i + 5 : 10 * i + 10, :])
    half_e[50:55, :] = jnp.where((iota((5, LANES), 1) & 32) == 0, half_e[45:50, :], half_e[0:5, :])
    lxe[0:5, :] = jnp.where(low_half, eig_e[0:5, :], eig_e[5:10, :])

    second = (wide & 32) != 0

    def x_halo(lines):
        ahead = [win_m[at(8, j), :] for j in lines]
        back = [win_m[at(1, j), :] for j in lines]
        extra = [win_e[at(9, j), :] for j in lines]
        near = [win_e[at(8, j), :] for j in lines]
        far = [win_e[at(1, j), :] for j in lines]
        for n, j in enumerate(lines):
            win_m[at(0, j), :] = jnp.where(wide >= 32, pltpu.roll(ahead[n], 32, 1), near[n])
            win_m[at(9, j), :] = jnp.where(wide < 96, pltpu.roll(back[n], 96, 1), far[n])
            both = pltpu.roll(jnp.where(wide < 64, back[n], ahead[n]), 64, 1)
            win_e[at(0, j), :] = jnp.where(second, jnp.where(wide >= 64, ahead[n], both), extra[n])
            win_e[at(9, j), :] = jnp.where(second, extra[n], jnp.where(wide < 64, back[n], both))

    def x_halos(n, _):
        x_halo([1 + 8 * n + m for m in range(8)])
        return 0

    lax.fori_loop(0, 1, x_halos, 0)
    x_halo([10])

    def y_halo(n, _):
        columns = [(win, 10 * n + m) for m in range(10) for win in (win_m, win_e)]
        outer = [win[at(i, 10), :] for win, i in columns]
        last = [pltpu.roll(win[at(i, 8), :], 16, 1) for win, i in columns]
        first = [pltpu.roll(win[at(i, 1), :], 112, 1) for win, i in columns]
        for m, (win, i) in enumerate(columns):
            win[at(i, 0), :] = jnp.where(upper, last[m], outer[m])
            win[at(i, 9), :] = jnp.where(upper, outer[m], first[m])
        return 0

    lax.fori_loop(0, 1, y_halo, 0)

    def x_forward(win, table, target, count):
        def step(j, _):
            column = [win[at(i, j), :] for i in range(10)]
            for a in range(count):
                target[a, j] = dot_rows([(row(table, count * i + a), column[i]) for i in range(10)])
            return 0
        lax.fori_loop(0, 10, step, 0)

    def through_z(source, target, zfwd):
        table = [zfwd[k] for k in range(10)]
        for b in range(10):
            target[b] = dot_rows([(table[k], jnp.broadcast_to(source[b, k : k + 1, :], (16, LANES))) for k in range(10)])

    def y_forward(a, source, pick):
        column = [source[a, j] for j in range(10)]
        for b in range(10):
            tmp_a[b] = dot_rows([(row(pick, 100 + 10 * j + b), column[j]) for j in range(10)])

    def scale(a, eig, lx):
        level = row(lx, a) + eig[20:36, :]
        for b in range(10):
            tmp_b[b] = tmp_b[b] / (level + row(eig, 10 + b))

    def y_back(source, pick, store):
        column = [source[b] for b in range(10)]
        for j in range(10):
            store(j, dot_rows([(row(pick, 100 + 10 * j + b), column[b]) for b in range(10)]))

    x_forward(win_e, half_e, work_e, 5)
    for b in range(10):
        edge[b] = jnp.zeros((16, LANES), F32)

    def edge_step(a, _):
        y_forward(a, work_e, pick_e)
        through_z(tmp_a, tmp_b, zfwd_e)
        scale(a, eig_e, lxe)
        weight = row(half_e, 50 + a)
        for b in range(10):
            edge[b] = edge[b] + weight * tmp_b[b]
        return 0

    lax.fori_loop(0, 5, edge_step, 0)
    for b in range(10):
        tmp_b[b] = edge[b] + pltpu.roll(edge[b], 64, 1)
    through_z(tmp_b, tmp_c, zback_e)

    def put_edge(j, value):
        edge[j] = value

    y_back(tmp_c, pick_e, put_edge)

    x_forward(win_m, pick_m, work, 10)

    def main_step(a, _):
        y_forward(a, work, pick_m)
        through_z(tmp_a, tmp_b, zfwd_m)
        scale(a, eig_m, eig_m)
        through_z(tmp_b, tmp_c, zback_m)

        def put(j, value):
            work[a, j] = value

        y_back(tmp_c, pick_m, put)
        return 0

    lax.fori_loop(0, 10, main_step, 0)

    for n, j in ((0, 0), (1, 9)):
        def put_end(i, main, n=n):
            ends[n, i - 1] = main

        x_back(work, edge, pick_m, j, put_end)
    for i in range(8):
        rim_rows[8 * i : 8 * i + 8, :] = jnp.where(upper[0:8], ends[1, i], ends[0, i])
    (parts,) = exchange([[rim_rows[pl.ds(k, 8, stride=8), :] for k in range(8)]])
    for r in range(8):
        rows_f[32 * (r % 2) + 8 * (r // 2) : 32 * (r % 2) + 8 * (r // 2) + 8, :] = parts[r]
    rim_ref[...] = join_rows(rows_f[0:64, :])
    inner = upper[0:8]

    def solve(j, _):
        def put(i, tile):
            tile = tile + jnp.where(inner & (j == 1), pltpu.roll(ends[1, i - 1], 16, 1), 0.0)
            tile = tile + jnp.where(inner | (j != 8), 0.0, pltpu.roll(ends[0, i - 1], 112, 1))
            tiles[pl.ds(pl.multiple_of(((i - 1) * 8 + j - 1) * 8, 8), 8), :] = tile

        x_back(work, edge, pick_m, j, put)
        return 0

    lax.fori_loop(1, 9, solve, 0)

    def step(n, _):
        columns = [8 * n + m for m in range(8)]
        groups = exchange([[tiles[pl.ds(i * 64 + k, 8, stride=8), :] for k in range(8)] for i in columns])
        for i, parts in zip(columns, groups, strict=True):
            for r in range(8):
                rows_ref[pl.ds(pl.multiple_of(128 * (r // 2) + 16 * i + 8 * (r % 2), 8), 8), :] = parts[r]
        return 0

    lax.fori_loop(0, 1, step, 0)
    fine_ref[...] = join_rows(rows_ref[...])


def x_back(work, edge, pick, j, put):
    sub, lane, kz = grids()
    wide = iota((16, LANES), 1)
    column = [work[a, j] for a in range(10)]
    first = dot_rows([(row(pick, a), column[a]) for a in range(10)])
    last = dot_rows([(row(pick, 90 + a), column[a]) for a in range(10)])
    side = edge[j]
    for i in range(1, 9):
        total = dot_rows([(row(pick, 10 * i + a), column[a]) for a in range(10)])
        if i == 1:
            total = total + jnp.where(wide >= 32, pltpu.roll(last, 32, 1), side)
        if i == 8:
            total = total + jnp.where(wide < 96, pltpu.roll(first, 96, 1), side)
        put(i, join_z(total, sub, kz))


def tree_kernel(got_ref, rim_ref, four_ref, from_left, from_right, pay_ref):
    p = lax.axis_index("gx")
    q = lax.axis_index("gy")
    totals = []
    for n in range(2):
        bits = 2 + (2 * q + n) // 3
        total = jnp.zeros((1, LANES), F32)
        for t in range(64):
            inside = (t >> bits) == (p >> bits)
            total = total + jnp.where(inside, got_ref[t, :, LANES * n : LANES * (n + 1)], 0.0)
        totals.append(total)
    four = four_ref[0:3, :] + jnp.where((p & 1) == 0, from_right[164:167, :], from_left[164:167, :])
    for peer in range(8):
        pay_ref[peer, 0:32, :] = jnp.where(peer < q, rim_ref[0:32, :], rim_ref[32:64, :])
        pay_ref[peer, 32:33, :] = totals[0]
        pay_ref[peer, 33:34, :] = totals[1]
        pay_ref[peer, 34:37, :] = four
        pay_ref[peer, 37:40, :] = jnp.zeros((3, LANES), F32)


def up_kernel(
    four_ref, own_ref, got_ref, pan_hbm, num_ref, top_ref, fine_ref, out_ref, line_ref, coeff_ref, sums_ref, vertex_ref, low_ref, sems
):
    q = lax.axis_index("gy")
    copies = []
    for n, (low, high) in enumerate(((0, 64), (64, 255 - TOP))):
        part = pl.ds(low, high - low)
        copies.append(pltpu.make_async_copy(pan_hbm.at[pl.ds(TOP + low, high - low), :], low_ref.at[part, :], sems.at[n]))
        copies[n].start()
    line_ref[...] = jnp.zeros((32, LANES), F32)
    line_ref[0:2, :] = own_ref[0:2, :]
    line_ref[2:5, :] = four_ref[3:6, :]
    line_ref[5:8, :] = got_ref[7, 34:37, :]
    for peer in range(8):
        line_ref[8 + 2 * peer : 10 + 2 * peer, :] = got_ref[peer, 32:34, :]
    here = pltpu.roll(line_ref[0:24], 127, 1)
    after = pltpu.roll(line_ref[1:25], 127, 1)
    coeff_ref[...] = jnp.where(iota((24, LANES), 1) == 127, after, here)
    weights = [jnp.broadcast_to(coeff_ref[c : c + 1, :width], (8, width)) for c, (_, width) in enumerate(CUTS)]

    def product(ref, first, place, count):
        total = ref[place, CUTS[0][0]] * weights[0][:count]
        for weight, (cut, _) in zip(weights[1:22], CUTS[1:22], strict=True):
            total = total + ref[place, cut] * weight[:count]
        end = ref[place, CUTS[22][0]] * weights[22][:count]
        sums_ref[pl.ds(first, count), :] = total
        sums_ref[pl.ds(first, count), 0:127] = total[:, 0:127] + end

    def top_step(g, _):
        first = pl.multiple_of(8 * g, 8)
        product(top_ref, first, pl.ds(first, 8), 8)
        return 0

    def low_step(g, _):
        first = pl.multiple_of(8 * g, 8)
        product(low_ref, TOP + first, pl.ds(first, 8), 8)
        return 0

    lax.fori_loop(0, TOP // 8, top_step, 0, unroll=4)
    copies[0].wait()
    lax.fori_loop(0, 8, low_step, 0, unroll=4)
    copies[1].wait()
    lax.fori_loop(8, (255 - TOP) // 8, low_step, 0, unroll=7)
    product(low_ref, 248, pl.ds(248 - TOP, 7), 7)
    sums_ref[255:256, :] = jnp.zeros((1, LANES), F32)
    values = jnp.broadcast_to(jnp.sum(sums_ref[...], axis=1, keepdims=True), (256, 17))
    vertex_ref[...] = jnp.zeros((16, LANES), F32)
    rows = iota((256, 17), 0)
    for i in range(5):
        for j in range(3):
            k = 3 * i + j
            vertex_ref[k : k + 1, 0:17] = jnp.sum(jnp.where(num_ref[i, j : j + 1, :] == rows, values, 0.0), axis=0, keepdims=True)
    depth = hat(iota((LANES, LANES), 1), iota((LANES, LANES), 0)).astype(jnp.bfloat16)
    vertex_ref[...] = moved(vertex_ref[...], depth)
    rise = (2.0 * iota((8, LANES), 0).astype(F32) + 1.0) / 16.0
    planes = []
    for i in range(5):
        three = [jnp.broadcast_to(vertex_ref[3 * i + j : 3 * i + j + 1, :], (8, LANES)) for j in range(3)]
        planes.append([three[jy] * (1.0 - rise) + three[jy + 1] * rise for jy in range(2)])
    faces = (
        jnp.where(q > 0, got_ref[jnp.maximum(q - 1, 0), 0:32, :], 0.0),
        jnp.where(q < 7, got_ref[jnp.minimum(q + 1, 7), 0:32, :], 0.0),
    )
    edges = (iota((8, LANES), 0) == 0, iota((8, LANES), 0) == 7)
    for ix in range(4):
        for i in range(8):
            x = 8 * ix + i
            far = (2 * i + 1) / 16.0
            for jy in range(2):
                place = slice(16 * x + 8 * jy, 16 * x + 8 * jy + 8)
                value = fine_ref[place, :] + planes[ix][jy] * (1.0 - far) + planes[ix + 1][jy] * far
                out_ref[place, :] = value + jnp.where(edges[jy], faces[jy][x : x + 1, :], 0.0)


VM = pltpu.VMEM
ANYWHERE = None


def call(kernel, outs, scratch=(), ins=None, sems=0, cost=0, limit=24, aliases=None):
    shapes = [
        jax.ShapeDtypeStruct(o[0], o[2] if len(o) > 2 else F32) if o[1] is None else o[1](o[0], o[2] if len(o) > 2 else F32)
        for o in outs
    ]
    spaces = [pltpu.VMEM(s, F32) for s in scratch]
    if sems:
        spaces.append(pltpu.SemaphoreType.DMA((sems,)))
    run = pl.pallas_call(
        kernel,
        out_shape=shapes,
        in_specs=[pl.BlockSpec(memory_space=m or pltpu.VMEM) for m in ins],
        out_specs=[pl.BlockSpec(memory_space=pltpu.VMEM) for _ in outs],
        scratch_shapes=spaces,
        input_output_aliases=aliases or {},
        compiler_params=pltpu.CompilerParams(vmem_limit_bytes=limit << 20),
        cost_estimate=pl.CostEstimate(flops=cost, bytes_accessed=cost // 400, transcendentals=0),
    )

    def apply(*operands):
        held = [x if m is None else pltpu.with_memory_space_constraint(x, m) for x, m in zip(operands, ins, strict=True)]
        return run(*held)

    return apply


def spread_to(block, axis):
    return lax.all_to_all(block, axis, 0, 0, tiled=True)


def shards(residual, elem_class, basis, eigenvalues, vertex_number, panels):
    field = residual.reshape(512, LANES)
    I32 = jnp.int32
    pay, own, num, cls, top, win, basis2, eigen2, pick, eig, zfwd, zback, rows = call(
        down_kernel,
        [
            ((8, 40, 128), VM), ((24, 128), VM), ((5, 3, 17), VM, I32), ((4, 2, 16), VM, I32), ((TOP, 2943), VM),
            ((1760, 128), VM), ((8, 300), VM), ((8, 30), VM), ((304, 128), VM), ((40, 128), VM),
            ((10, 16, 128), VM), ((10, 16, 128), VM), ((512, 128), VM),
        ],
        [(512, 128), (3, 10, 8, 10), (3, 8, 10), (40, 128), (255 - TOP, 2943)], ins=[pltpu.HBM] * 6, sems=7,
    )(field, vertex_number, panels, elem_class, basis.transpose(1, 2, 0, 3), eigenvalues.transpose(1, 0, 2))
    first = spread_to(pay, "gy")
    right, left, tree, face, four = call(
        share_kernel,
        [((168, 128), VM), ((168, 128), VM), ((64, 1, 256), VM), ((64, 128), VM), ((8, 128), VM)],
        ins=[None, VM, VM],
    )(first, rows, cls)
    from_left = lax.ppermute(right, "gx", [(i, i + 1) for i in range(63)])
    from_right = lax.ppermute(left, "gx", [(i + 1, i) for i in range(63)])
    summed = spread_to(tree, "gx")
    win, fine, rim = call(
        solve_kernel,
        [((1760, 128), VM), ((512, 128), VM), ((64, 128), VM)],
        [
            (10, 10, 16, 128), (10, 16, 128), (2, 8, 8, 128), (512, 128), (512, 128),
            (112, 128), (1760, 128), (304, 128), (40, 128), (10, 16, 128), (10, 16, 128),
            (56, 128), (8, 128), (5, 10, 16, 128), (10, 16, 128), (10, 16, 128), (10, 16, 128), (64, 128),
        ],
        ins=[VM] * 8 + [None, None], cost=8_000_000_000, aliases={0: 0},
    )(win, basis2, eigen2, pick, eig, zfwd, zback, face, from_left, from_right)
    (pay,) = call(tree_kernel, [((8, 40, 128), VM)], ins=[None, VM, VM, None, None])(summed, rim, four, from_left, from_right)
    second = spread_to(pay, "gy")
    (out,) = call(
        up_kernel, [((512, 128), None)], [(32, 128), (24, 128), (256, 128), (16, 128), (255 - TOP, 2943)],
        ins=[VM, VM, None, pltpu.HBM, VM, VM, VM], sems=2,
    )(four, own, second, panels, num, top, fine)
    return out.reshape(residual.shape)


def solution(mesh):
    return jax.shard_map(
        shards,
        mesh=mesh,
        in_specs=(
            P(None, "gx", "gy", None),
            P("gx", "gy", None),
            P(),
            P(),
            P("gx", "gy", None),
            P("gx", "gy"),
        ),
        out_specs=P(None, "gx", "gy", None),
        check_vma=False,
    )
```

```python
import functools

import jax
import jax.numpy as jnp
from jax import lax
from jax.experimental import pallas as pl
from jax.experimental.pallas import tpu as pltpu
from jax.sharding import PartitionSpec as P

NPR = 8
NEXT = 10
NCLASS = 8
LANES = 128
TOP = 128
CUTS = [(slice(low, min(low + 128, 2943)), min(128, 2943 - low)) for low in range(0, 2943, 128)]
HALO = NPR + 1
F32 = jnp.float32
exact = lax.Precision.HIGHEST
ORDER = (1, 2, 3, 4, 5, 6, 7, 8, 0, 9)


def iota(shape, axis):
    return lax.broadcasted_iota(jnp.int32, shape, axis)


def hat(point, vertex):
    place = (point.astype(F32) + 0.5) / NPR
    return jnp.maximum(0.0, 1.0 - jnp.abs(place - vertex.astype(F32)))


def moved(rows, table):
    high = rows.astype(jnp.bfloat16)
    rest = rows - high.astype(F32)
    middle = rest.astype(jnp.bfloat16)
    low = (rest - middle.astype(F32)).astype(jnp.bfloat16)
    total = jnp.dot(low, table, preferred_element_type=F32)
    total = total + jnp.dot(middle, table, preferred_element_type=F32)
    return total + jnp.dot(high, table, preferred_element_type=F32)


def plane_hat(point, vertex):
    third = (vertex.astype(F32) + 0.5) / 3.0
    big = third.astype(jnp.int32)
    return hat(point >> 4, big) * hat(point & 15, vertex - 3 * big)


def down_kernel(
    res_hbm, num_hbm, pan_hbm, cls_hbm, basis_hbm, value_hbm,
    pay_ref, own_ref, num_ref, cls_ref, top_ref, res_ref, basis_ref, value_ref,
    line_ref, low_ref, sems,
):
    q = lax.axis_index("gy")
    pairs = [
        (res_hbm, res_ref), (num_hbm, num_ref), (cls_hbm, cls_ref), (basis_hbm, basis_ref), (value_hbm, value_ref),
        (pan_hbm.at[pl.ds(0, TOP), :], top_ref), (pan_hbm.at[pl.ds(TOP, 255 - TOP), :], low_ref),
    ]
    copies = [pltpu.make_async_copy(source, target, sems.at[n]) for n, (source, target) in enumerate(pairs)]
    for copy in copies:
        copy.start()
    plane = plane_hat(iota((16, 512), 1), iota((16, 512), 0))
    depth = hat(iota((128, 17), 0), iota((128, 17), 1))
    line_ref[...] = jnp.zeros((40, LANES), F32)
    copies[0].wait()
    half = jnp.dot(plane, res_ref[...], precision=exact)
    vertex = jnp.dot(half, depth, precision=exact)
    low_face = res_ref[pl.ds(0, 32, stride=16), :]
    high_face = res_ref[pl.ds(15, 32, stride=16), :]
    for peer in range(8):
        pay_ref[peer, 0:32, :] = jnp.where(peer < q, low_face, high_face)
    copies[1].wait()
    rows = iota((256, 17), 0)
    spread = jnp.zeros((256, 17), F32)
    for i in range(5):
        for j in range(3):
            k = 3 * i + j
            spread = spread + jnp.where(num_ref[i, j : j + 1, :] == rows, vertex[k : k + 1, :], 0.0)
    ordered = jnp.broadcast_to(jnp.sum(spread, axis=1, keepdims=True), (256, LANES))

    for copy in copies[2:]:
        copy.wait()
    for c, (cut, width) in enumerate(CUTS):
        piece = jnp.sum(top_ref[:, cut] * ordered[:TOP, :width], axis=0, keepdims=True)
        piece = piece + jnp.sum(low_ref[:, cut] * ordered[TOP:255, :width], axis=0, keepdims=True)
        line_ref[8 + c : 9 + c, :width] = piece
    here = pltpu.roll(line_ref[8:32], 1, 1)
    before = pltpu.roll(line_ref[7:31], 1, 1)
    own_ref[...] = jnp.where(iota((24, LANES), 1) == 0, before, here)
    for peer in range(8):
        pay_ref[peer, 32:35, :] = own_ref[2:5, :]
        pay_ref[peer, 35:37, :] = own_ref[8 + 2 * peer : 10 + 2 * peer, :]
        pay_ref[peer, 37:40, :] = own_ref[5:8, :] if peer == 7 else jnp.zeros((3, LANES), F32)


def sum_kernel(got_ref, tree_ref, four_ref):
    q = lax.axis_index("gy")
    total = got_ref[0, 35:40, :]
    for peer in range(1, 8):
        total = total + got_ref[peer, 35:40, :]
    four_ref[...] = jnp.zeros((8, LANES), F32)
    four_ref[0:3, :] = total[2:5]
    for level in range(1, 4):
        low = jnp.zeros((1, LANES), F32)
        for peer in range(8):
            inside = (peer >> level) == (q >> level)
            low = low + jnp.where(inside, got_ref[peer, 31 + level : 32 + level, :], 0.0)
        four_ref[2 + level : 3 + level, :] = low
    line = jnp.concatenate([total[0:1], total[1:2]], axis=1)
    for t in range(64):
        tree_ref[t] = line


def pack_kernel(got_ref, res_ref, cls_ref, four_ref, right_ref, left_ref, face_ref):
    q = lax.axis_index("gy")
    face_ref[0:32, :] = jnp.where(q > 0, got_ref[jnp.maximum(q - 1, 0), 0:32, :], 0.0)
    face_ref[32:64, :] = jnp.where(q < 7, got_ref[jnp.minimum(q + 1, 7), 0:32, :], 0.0)
    for ref, column, first in ((right_ref, 3, 23), (left_ref, 0, 0)):
        ref[0:144, :] = res_ref[16 * first : 16 * first + 144, :]
        ref[144:153, :] = face_ref[first : first + 9, :]
        ref[153:162, :] = face_ref[32 + first : 41 + first, :]
        ref[162:168, :] = jnp.zeros((6, LANES), F32)
        ref[162:164, 0:16] = (cls_ref[column] + 1).astype(F32)
        ref[164:167, :] = four_ref[0:3, :]


def grids():
    sub = iota((8, LANES), 0)
    lane = iota((8, LANES), 1)
    return sub, lane, lane & 15


def split_z(rows):
    lane = iota((LANES, LANES), 1)
    return moved(rows, (iota((LANES, LANES), 0) == (((lane & 15) << 3) | (lane >> 4))).astype(jnp.bfloat16))


def join_rows(rows):
    lane = iota((LANES, LANES), 0)
    return moved(rows, (iota((LANES, LANES), 1) == (((lane & 15) << 3) | (lane >> 4))).astype(jnp.bfloat16))


def exchange(groups):
    lane = iota((8, LANES), 1)
    groups = [list(parts) for parts in groups]
    for bit in (4, 2, 1):
        inside = (lane & (16 * bit)) != 0
        for parts in groups:
            for n in range(8):
                if n & bit:
                    continue
                low, high = parts[n], parts[n | bit]
                if bit == 4:
                    swap = pltpu.roll(jnp.where(inside, low, high), 64, 1)
                    parts[n] = jnp.where(inside, swap, low)
                    parts[n | bit] = jnp.where(inside, high, swap)
                else:
                    parts[n] = jnp.where(inside, pltpu.roll(high, 16 * bit, 1), low)
                    parts[n | bit] = jnp.where(inside, high, pltpu.roll(low, LANES - 16 * bit, 1))
    return groups


def with_outer(groups):
    kz = iota((8, LANES), 1) & 15
    before = [jnp.where(kz == 0, 0.0, pltpu.roll(parts[7], 1, 1)) for parts in groups]
    after = [jnp.where(kz == 15, 0.0, pltpu.roll(parts[0], 127, 1)) for parts in groups]
    return [parts + [b, a] for parts, b, a in zip(groups, before, after, strict=True)]


def at(i, j):
    return pl.ds(pl.multiple_of((i * 11 + j) * 16, 16), 16)


def join_z(total, sub, kz):
    main = total[0:8]
    tail = pltpu.roll(total[8:16], 7, 0)
    return main + jnp.where(
        sub == 7,
        jnp.where(kz == 15, 0.0, pltpu.roll(tail, 127, 1)),
        jnp.where((sub == 0) & (kz != 0), pltpu.roll(tail, 1, 1), 0.0),
    )


def row(ref, n):
    return jnp.broadcast_to(ref[pl.ds(n, 1), :], (16, LANES))


def dot_rows(pairs):
    total = None
    for a, b in pairs:
        total = a * b if total is None else total + a * b
    return total


def pick_tables(kind, table_ref, eigen_ref, pick, eig, zfwd, zback):
    group = iota((8, LANES), 0)
    lane = iota((8, LANES), 1)
    spread = (iota((16, LANES), 0) == (iota((16, LANES), 1) & 15)).astype(F32)
    laid = jnp.dot(kind, spread, precision=exact)
    laid = jnp.sum(jnp.where(group == (lane >> 4), laid, 0.0), axis=0, keepdims=True)
    onehot = (laid == (group + 1).astype(F32)).astype(F32)
    dims = (((0,), (0,)), ((), ()))
    pick[0:300, :] = lax.dot_general(table_ref[:, 0:300], onehot, dims, precision=exact, preferred_element_type=F32)
    eig[0:30, :] = lax.dot_general(eigen_ref[:, 0:30], onehot, dims, precision=exact, preferred_element_type=F32)
    eig[20:30, :] = eig[20:30, :] + jnp.where(laid == 0.0, 1.0, 0.0)
    eig[30:40, :] = jnp.ones((10, LANES), F32)
    for n, k in enumerate(ORDER):
        zfwd[n, 0:10, :] = pick[200 + 10 * k : 210 + 10 * k, :]
        zfwd[n, 10:16, :] = jnp.zeros((6, LANES), F32)
    for c in range(10):
        zback[c, 0:8, :] = pick[pl.ds(210 + c, 8, stride=10), :]
        zback[c, 8:16, :] = jnp.zeros((8, LANES), F32)
        zback[c, 8:9, :] = pick[200 + c : 201 + c, :]
        zback[c, 9:10, :] = pick[290 + c : 291 + c, :]


def tile_kernel(
    res_ref, cls_ref, basis_ref, value_ref,
    win, table_ref, eigen_ref, pick, eig, zfwd, zback,
    rows_ref,
):
    rows_ref[...] = split_z(res_ref[...])
    for d in range(3):
        eigen_ref[:, 10 * d : 10 * d + 10] = value_ref[d]
        for i in range(10):
            low = 100 * d + 10 * i
            table_ref[:, low : low + 10] = basis_ref[d, i]
    kind = jnp.concatenate([cls_ref[ix].astype(F32) + 1.0 for ix in range(4)], axis=0)
    pick_tables(kind, table_ref, eigen_ref, pick, eig, zfwd, zback)
    columns = range(8)
    groups = [
        [rows_ref[128 * (r // 2) + 16 * i + 8 * (r % 2) : 128 * (r // 2) + 16 * i + 8 * (r % 2) + 8, :] for r in range(8)]
        for i in columns
    ]
    for i, parts in zip(columns, with_outer(exchange(groups)), strict=True):
        for k, part in enumerate(parts):
            win[pl.ds((i * 11 + 12) * 16 + k, 8, stride=16), :] = part


def solve_kernel(
    win_in, table_ref, eigen_ref, pick_m, eig_m, zfwd_m, zback_m, face_ref, from_left, from_right,
    win_m, fine_ref, rim_ref,
    work, edge, ends, tiles, rows_ref, rows_f, rows_e, win_e, pick_e, eig_e, zfwd_e, zback_e, half_e, lxe, work_e, tmp_a, tmp_b, tmp_c, rim_rows,
):
    del win_in
    sub, lane, kz = grids()
    wide = iota((16, LANES), 1)
    upper = (wide & 16) != 0

    rows_f[0:64, :] = face_ref[...]
    rows_f[64:88, :] = from_left[144:168, :]
    rows_f[88:112, :] = from_right[144:168, :]
    rows_f[...] = split_z(rows_f[...])
    rows_e[0:144, :] = from_left[0:144, :]
    rows_e[144:288, :] = from_right[0:144, :]
    rows_e[...] = split_z(rows_e[...])
    outer = [rows_f[32 * (r % 2) + 8 * (r // 2) : 32 * (r % 2) + 8 * (r // 2) + 8, :] for r in range(8)]
    beside = [rows_f[first : first + 8, :] for first in (65, 74, 88, 97)]
    corner = [jnp.broadcast_to(rows_f[n : n + 1, :], (8, LANES)) for n in (64, 73, 96, 105)]
    outer, beside, corner = with_outer(exchange([outer, beside + beside, corner + corner]))
    for k in range(10):
        win_m[pl.ds(21 * 16 + k, 8, stride=176), :] = outer[k]
        win_e[pl.ds(21 * 16 + k, 8, stride=176), :] = beside[k]
        win_e[109 * 16 + k : 109 * 16 + k + 1, :] = corner[k][0:1]

    def fill(n, _):
        columns = [9 * n + m for m in range(9)]
        groups = []
        for i in columns:
            layer = jnp.where(i == 8, 0, i + 1)
            parts = [rows_e[pl.ds(pl.multiple_of(16 * layer + 8 * jy, 8), 8), :] for jy in range(2)]
            parts += [rows_e[pl.ds(pl.multiple_of(144 + 16 * i + 8 * jy, 8), 8), :] for jy in range(2)]
            groups.append(parts + parts)
        for i, parts in zip(columns, with_outer(exchange(groups)), strict=True):
            for k, part in enumerate(parts):
                win_e[pl.ds((i * 11 + 12) * 16 + k, 8, stride=16), :] = part
        return 0

    lax.fori_loop(0, 1, fill, 0)

    near = [from_left[162:164, 0:16], from_right[162:164, 0:16]]
    pick_tables(jnp.concatenate(near + near, axis=0), table_ref, eigen_ref, pick_e, eig_e, zfwd_e, zback_e)
    low_half = iota((5, LANES), 1) < 64
    for i in range(10):
        half_e[5 * i : 5 * i + 5, :] = jnp.where(low_half, pick_e[10 * i : 10 * i + 5, :], pick_e[10 * i + 5 : 10 * i + 10, :])
    half_e[50:55, :] = jnp.where((iota((5, LANES), 1) & 32) == 0, half_e[45:50, :], half_e[0:5, :])
    lxe[0:5, :] = jnp.where(low_half, eig_e[0:5, :], eig_e[5:10, :])

    second = (wide & 32) != 0

    def x_halo(lines):
        ahead = [win_m[at(8, j), :] for j in lines]
        back = [win_m[at(1, j), :] for j in lines]
        extra = [win_e[at(9, j), :] for j in lines]
        near = [win_e[at(8, j), :] for j in lines]
        far = [win_e[at(1, j), :] for j in lines]
        for n, j in enumerate(lines):
            win_m[at(0, j), :] = jnp.where(wide >= 32, pltpu.roll(ahead[n], 32, 1), near[n])
            win_m[at(9, j), :] = jnp.where(wide < 96, pltpu.roll(back[n], 96, 1), far[n])
            both = pltpu.roll(jnp.where(wide < 64, back[n], ahead[n]), 64, 1)
            win_e[at(0, j), :] = jnp.where(second, jnp.where(wide >= 64, ahead[n], both), extra[n])
            win_e[at(9, j), :] = jnp.where(second, extra[n], jnp.where(wide < 64, back[n], both))

    def x_halos(n, _):
        x_halo([1 + 8 * n + m for m in range(8)])
        return 0

    lax.fori_loop(0, 1, x_halos, 0)
    x_halo([10])

    def y_halo(n, _):
        columns = [(win, 10 * n + m) for m in range(10) for win in (win_m, win_e)]
        outer = [win[at(i, 10), :] for win, i in columns]
        last = [pltpu.roll(win[at(i, 8), :], 16, 1) for win, i in columns]
        first = [pltpu.roll(win[at(i, 1), :], 112, 1) for win, i in columns]
        for m, (win, i) in enumerate(columns):
            win[at(i, 0), :] = jnp.where(upper, last[m], outer[m])
            win[at(i, 9), :] = jnp.where(upper, outer[m], first[m])
        return 0

    lax.fori_loop(0, 1, y_halo, 0)

    def x_forward(win, table, target, count):
        def step(j, _):
            column = [win[at(i, j), :] for i in range(10)]
            for a in range(count):
                target[a, j] = dot_rows([(row(table, count * i + a), column[i]) for i in range(10)])
            return 0
        lax.fori_loop(0, 10, step, 0)

    def through_z(source, target, zfwd):
        table = [zfwd[k] for k in range(10)]
        for b in range(10):
            target[b] = dot_rows([(table[k], jnp.broadcast_to(source[b, k : k + 1, :], (16, LANES))) for k in range(10)])

    def y_forward(a, source, pick):
        column = [source[a, j] for j in range(10)]
        for b in range(10):
            tmp_a[b] = dot_rows([(row(pick, 100 + 10 * j + b), column[j]) for j in range(10)])

    def scale(a, eig, lx):
        level = row(lx, a) + eig[20:36, :]
        for b in range(10):
            tmp_b[b] = tmp_b[b] / (level + row(eig, 10 + b))

    def y_back(source, pick, store):
        column = [source[b] for b in range(10)]
        for j in range(10):
            store(j, dot_rows([(row(pick, 100 + 10 * j + b), column[b]) for b in range(10)]))

    x_forward(win_e, half_e, work_e, 5)
    for b in range(10):
        edge[b] = jnp.zeros((16, LANES), F32)

    def edge_step(a, _):
        y_forward(a, work_e, pick_e)
        through_z(tmp_a, tmp_b, zfwd_e)
        scale(a, eig_e, lxe)
        weight = row(half_e, 50 + a)
        for b in range(10):
            edge[b] = edge[b] + weight * tmp_b[b]
        return 0

    lax.fori_loop(0, 5, edge_step, 0)
    for b in range(10):
        tmp_b[b] = edge[b] + pltpu.roll(edge[b], 64, 1)
    through_z(tmp_b, tmp_c, zback_e)

    def put_edge(j, value):
        edge[j] = value

    y_back(tmp_c, pick_e, put_edge)

    x_forward(win_m, pick_m, work, 10)

    def main_step(a, _):
        y_forward(a, work, pick_m)
        through_z(tmp_a, tmp_b, zfwd_m)
        scale(a, eig_m, eig_m)
        through_z(tmp_b, tmp_c, zback_m)

        def put(j, value):
            work[a, j] = value

        y_back(tmp_c, pick_m, put)
        return 0

    lax.fori_loop(0, 10, main_step, 0)

    for n, j in ((0, 0), (1, 9)):
        def put_end(i, main, n=n):
            ends[n, i - 1] = main

        x_back(work, edge, pick_m, j, put_end)
    for i in range(8):
        rim_rows[8 * i : 8 * i + 8, :] = jnp.where(upper[0:8], ends[1, i], ends[0, i])
    (parts,) = exchange([[rim_rows[pl.ds(k, 8, stride=8), :] for k in range(8)]])
    for r in range(8):
        rows_f[32 * (r % 2) + 8 * (r // 2) : 32 * (r % 2) + 8 * (r // 2) + 8, :] = parts[r]
    rim_ref[...] = join_rows(rows_f[0:64, :])
    inner = upper[0:8]

    def solve(j, _):
        def put(i, tile):
            tile = tile + jnp.where(inner & (j == 1), pltpu.roll(ends[1, i - 1], 16, 1), 0.0)
            tile = tile + jnp.where(inner | (j != 8), 0.0, pltpu.roll(ends[0, i - 1], 112, 1))
            tiles[pl.ds(pl.multiple_of(((i - 1) * 8 + j - 1) * 8, 8), 8), :] = tile

        x_back(work, edge, pick_m, j, put)
        return 0

    lax.fori_loop(1, 9, solve, 0)

    def step(n, _):
        columns = [8 * n + m for m in range(8)]
        groups = exchange([[tiles[pl.ds(i * 64 + k, 8, stride=8), :] for k in range(8)] for i in columns])
        for i, parts in zip(columns, groups, strict=True):
            for r in range(8):
                rows_ref[pl.ds(pl.multiple_of(128 * (r // 2) + 16 * i + 8 * (r % 2), 8), 8), :] = parts[r]
        return 0

    lax.fori_loop(0, 1, step, 0)
    fine_ref[...] = join_rows(rows_ref[...])


def x_back(work, edge, pick, j, put):
    sub, lane, kz = grids()
    wide = iota((16, LANES), 1)
    column = [work[a, j] for a in range(10)]
    first = dot_rows([(row(pick, a), column[a]) for a in range(10)])
    last = dot_rows([(row(pick, 90 + a), column[a]) for a in range(10)])
    side = edge[j]
    for i in range(1, 9):
        total = dot_rows([(row(pick, 10 * i + a), column[a]) for a in range(10)])
        if i == 1:
            total = total + jnp.where(wide >= 32, pltpu.roll(last, 32, 1), side)
        if i == 8:
            total = total + jnp.where(wide < 96, pltpu.roll(first, 96, 1), side)
        put(i, join_z(total, sub, kz))


def tree_kernel(got_ref, rim_ref, four_ref, from_left, from_right, pay_ref):
    p = lax.axis_index("gx")
    q = lax.axis_index("gy")
    totals = []
    for n in range(2):
        bits = 2 + (2 * q + n) // 3
        total = jnp.zeros((1, LANES), F32)
        for t in range(64):
            inside = (t >> bits) == (p >> bits)
            total = total + jnp.where(inside, got_ref[t, :, LANES * n : LANES * (n + 1)], 0.0)
        totals.append(total)
    four = four_ref[0:3, :] + jnp.where((p & 1) == 0, from_right[164:167, :], from_left[164:167, :])
    for peer in range(8):
        pay_ref[peer, 0:32, :] = jnp.where(peer < q, rim_ref[0:32, :], rim_ref[32:64, :])
        pay_ref[peer, 32:33, :] = totals[0]
        pay_ref[peer, 33:34, :] = totals[1]
        pay_ref[peer, 34:37, :] = four
        pay_ref[peer, 37:40, :] = jnp.zeros((3, LANES), F32)


def up_kernel(
    four_ref, own_ref, got_ref, pan_hbm, num_ref, top_ref, fine_ref, out_ref, line_ref, coeff_ref, sums_ref, vertex_ref, low_ref, sems
):
    q = lax.axis_index("gy")
    copies = []
    for n, (low, high) in enumerate(((0, 64), (64, 255 - TOP))):
        part = pl.ds(low, high - low)
        copies.append(pltpu.make_async_copy(pan_hbm.at[pl.ds(TOP + low, high - low), :], low_ref.at[part, :], sems.at[n]))
        copies[n].start()
    line_ref[...] = jnp.zeros((32, LANES), F32)
    line_ref[0:2, :] = own_ref[0:2, :]
    line_ref[2:5, :] = four_ref[3:6, :]
    line_ref[5:8, :] = got_ref[7, 34:37, :]
    for peer in range(8):
        line_ref[8 + 2 * peer : 10 + 2 * peer, :] = got_ref[peer, 32:34, :]
    here = pltpu.roll(line_ref[0:24], 127, 1)
    after = pltpu.roll(line_ref[1:25], 127, 1)
    coeff_ref[...] = jnp.where(iota((24, LANES), 1) == 127, after, here)
    weights = [jnp.broadcast_to(coeff_ref[c : c + 1, :width], (8, width)) for c, (_, width) in enumerate(CUTS)]

    def product(ref, first, place, count):
        total = ref[place, CUTS[0][0]] * weights[0][:count]
        for weight, (cut, _) in zip(weights[1:22], CUTS[1:22], strict=True):
            total = total + ref[place, cut] * weight[:count]
        end = ref[place, CUTS[22][0]] * weights[22][:count]
        sums_ref[pl.ds(first, count), :] = total
        sums_ref[pl.ds(first, count), 0:127] = total[:, 0:127] + end

    def top_step(g, _):
        first = pl.multiple_of(8 * g, 8)
        product(top_ref, first, pl.ds(first, 8), 8)
        return 0

    def low_step(g, _):
        first = pl.multiple_of(8 * g, 8)
        product(low_ref, TOP + first, pl.ds(first, 8), 8)
        return 0

    lax.fori_loop(0, TOP // 8, top_step, 0, unroll=4)
    copies[0].wait()
    lax.fori_loop(0, 8, low_step, 0, unroll=4)
    copies[1].wait()
    lax.fori_loop(8, (255 - TOP) // 8, low_step, 0, unroll=7)
    product(low_ref, 248, pl.ds(248 - TOP, 7), 7)
    sums_ref[255:256, :] = jnp.zeros((1, LANES), F32)
    values = jnp.broadcast_to(jnp.sum(sums_ref[...], axis=1, keepdims=True), (256, 17))
    vertex_ref[...] = jnp.zeros((16, LANES), F32)
    rows = iota((256, 17), 0)
    for i in range(5):
        for j in range(3):
            k = 3 * i + j
            vertex_ref[k : k + 1, 0:17] = jnp.sum(jnp.where(num_ref[i, j : j + 1, :] == rows, values, 0.0), axis=0, keepdims=True)
    depth = hat(iota((LANES, LANES), 1), iota((LANES, LANES), 0)).astype(jnp.bfloat16)
    vertex_ref[...] = moved(vertex_ref[...], depth)
    rise = (2.0 * iota((8, LANES), 0).astype(F32) + 1.0) / 16.0
    planes = []
    for i in range(5):
        three = [jnp.broadcast_to(vertex_ref[3 * i + j : 3 * i + j + 1, :], (8, LANES)) for j in range(3)]
        planes.append([three[jy] * (1.0 - rise) + three[jy + 1] * rise for jy in range(2)])
    faces = (
        jnp.where(q > 0, got_ref[jnp.maximum(q - 1, 0), 0:32, :], 0.0),
        jnp.where(q < 7, got_ref[jnp.minimum(q + 1, 7), 0:32, :], 0.0),
    )
    edges = (iota((8, LANES), 0) == 0, iota((8, LANES), 0) == 7)
    for ix in range(4):
        for i in range(8):
            x = 8 * ix + i
            far = (2 * i + 1) / 16.0
            for jy in range(2):
                place = slice(16 * x + 8 * jy, 16 * x + 8 * jy + 8)
                value = fine_ref[place, :] + planes[ix][jy] * (1.0 - far) + planes[ix + 1][jy] * far
                out_ref[place, :] = value + jnp.where(edges[jy], faces[jy][x : x + 1, :], 0.0)


VM = pltpu.VMEM
ANYWHERE = None


def call(kernel, outs, scratch=(), ins=None, sems=0, cost=0, limit=24, aliases=None):
    shapes = [
        jax.ShapeDtypeStruct(o[0], o[2] if len(o) > 2 else F32) if o[1] is None else o[1](o[0], o[2] if len(o) > 2 else F32)
        for o in outs
    ]
    spaces = [pltpu.VMEM(s, F32) for s in scratch]
    if sems:
        spaces.append(pltpu.SemaphoreType.DMA((sems,)))
    run = pl.pallas_call(
        kernel,
        out_shape=shapes,
        in_specs=[pl.BlockSpec(memory_space=m or pltpu.VMEM) for m in ins],
        out_specs=[pl.BlockSpec(memory_space=pltpu.VMEM) for _ in outs],
        scratch_shapes=spaces,
        input_output_aliases=aliases or {},
        compiler_params=pltpu.CompilerParams(vmem_limit_bytes=limit << 20),
        cost_estimate=pl.CostEstimate(flops=cost, bytes_accessed=cost // 400, transcendentals=0),
    )

    def apply(*operands):
        held = [x if m is None else pltpu.with_memory_space_constraint(x, m) for x, m in zip(operands, ins, strict=True)]
        return run(*held)

    return apply


def spread_to(block, axis):
    return lax.all_to_all(block, axis, 0, 0, tiled=True)


def shards(residual, elem_class, basis, eigenvalues, vertex_number, panels):
    field = residual.reshape(512, LANES)
    I32 = jnp.int32
    pay, own, num, cls, top, res, table, eigen = call(
        down_kernel,
        [
            ((8, 40, 128), VM), ((24, 128), VM), ((5, 3, 17), VM, I32), ((4, 2, 16), VM, I32), ((TOP, 2943), VM),
            ((512, 128), VM), ((3, 10, 8, 10), VM), ((3, 8, 10), VM),
        ],
        [(40, 128), (255 - TOP, 2943)], ins=[pltpu.HBM] * 6, sems=7,
    )(field, vertex_number, panels, elem_class, basis.transpose(1, 2, 0, 3), eigenvalues.transpose(1, 0, 2))
    first = spread_to(pay, "gy")
    tree, four = call(sum_kernel, [((64, 1, 256), VM), ((8, 128), VM)], ins=[None])(first)
    summed = spread_to(tree, "gx")
    right, left, face = call(
        pack_kernel, [((168, 128), VM), ((168, 128), VM), ((64, 128), VM)], ins=[None, VM, VM, VM], cost=2_000_000_000
    )(first, res, cls, four)
    from_left = lax.ppermute(right, "gx", [(i, i + 1) for i in range(63)])
    from_right = lax.ppermute(left, "gx", [(i + 1, i) for i in range(63)])
    win, basis2, eigen2, pick, eig, zfwd, zback = call(
        tile_kernel,
        [
            ((1760, 128), VM), ((8, 300), VM), ((8, 30), VM), ((304, 128), VM), ((40, 128), VM),
            ((10, 16, 128), VM), ((10, 16, 128), VM),
        ],
        [(512, 128)], ins=[VM] * 4, cost=2_000_000_000,
    )(res, cls, table, eigen)
    win, fine, rim = call(
        solve_kernel,
        [((1760, 128), VM), ((512, 128), VM), ((64, 128), VM)],
        [
            (10, 10, 16, 128), (10, 16, 128), (2, 8, 8, 128), (512, 128), (512, 128),
            (112, 128), (288, 128), (1760, 128), (304, 128), (40, 128), (10, 16, 128), (10, 16, 128),
            (56, 128), (8, 128), (5, 10, 16, 128), (10, 16, 128), (10, 16, 128), (10, 16, 128), (64, 128),
        ],
        ins=[VM] * 8 + [None, None], cost=1_000_000_000, aliases={0: 0},
    )(win, basis2, eigen2, pick, eig, zfwd, zback, face, from_left, from_right)
    (pay,) = call(tree_kernel, [((8, 40, 128), VM)], ins=[None, VM, VM, None, None])(summed, rim, four, from_left, from_right)
    second = spread_to(pay, "gy")
    (out,) = call(
        up_kernel, [((512, 128), None)], [(32, 128), (24, 128), (256, 128), (16, 128), (255 - TOP, 2943)],
        ins=[VM, VM, None, pltpu.HBM, VM, VM, VM], sems=2,
    )(four, own, second, panels, num, top, fine)
    return out.reshape(residual.shape)


def solution(mesh):
    return jax.shard_map(
        shards,
        mesh=mesh,
        in_specs=(
            P(None, "gx", "gy", None),
            P("gx", "gy", None),
            P(),
            P(),
            P("gx", "gy", None),
            P("gx", "gy"),
        ),
        out_specs=P(None, "gx", "gy", None),
        check_vma=False,
    )
```

```python
import functools

import jax
import jax.numpy as jnp
from jax import lax
from jax.experimental import pallas as pl
from jax.experimental.pallas import tpu as pltpu
from jax.sharding import PartitionSpec as P

NPR = 8
NEXT = 10
NCLASS = 8
LANES = 128
TOP = 208
CUTS = [(slice(low, min(low + 128, 2943)), min(128, 2943 - low)) for low in range(0, 2943, 128)]
HALO = NPR + 1
F32 = jnp.float32
exact = lax.Precision.HIGHEST
ORDER = (1, 2, 3, 4, 5, 6, 7, 8, 0, 9)


def iota(shape, axis):
    return lax.broadcasted_iota(jnp.int32, shape, axis)


def hat(point, vertex):
    place = (point.astype(F32) + 0.5) / NPR
    return jnp.maximum(0.0, 1.0 - jnp.abs(place - vertex.astype(F32)))


def moved(rows, table):
    high = rows.astype(jnp.bfloat16)
    rest = rows - high.astype(F32)
    middle = rest.astype(jnp.bfloat16)
    low = (rest - middle.astype(F32)).astype(jnp.bfloat16)
    total = jnp.dot(low, table, preferred_element_type=F32)
    total = total + jnp.dot(middle, table, preferred_element_type=F32)
    return total + jnp.dot(high, table, preferred_element_type=F32)


def plane_hat(point, vertex):
    third = (vertex.astype(F32) + 0.5) / 3.0
    big = third.astype(jnp.int32)
    return hat(point >> 4, big) * hat(point & 15, vertex - 3 * big)


def down_kernel(
    res_hbm, num_hbm, pan_hbm, cls_hbm, basis_hbm, value_hbm,
    pay_ref, own_ref, cls_ref, top_ref, res_ref, table_ref, eigen_ref,
    line_ref, basis_ref, value_ref, low_ref, num_ref, sems,
):
    q = lax.axis_index("gy")
    pairs = [
        (res_hbm, res_ref), (num_hbm, num_ref), (cls_hbm, cls_ref), (basis_hbm, basis_ref), (value_hbm, value_ref),
        (pan_hbm.at[pl.ds(0, TOP), :], top_ref), (pan_hbm.at[pl.ds(TOP, 255 - TOP), :], low_ref),
    ]
    copies = [pltpu.make_async_copy(source, target, sems.at[n]) for n, (source, target) in enumerate(pairs)]
    for copy in copies:
        copy.start()
    plane = plane_hat(iota((16, 512), 1), iota((16, 512), 0))
    depth = hat(iota((128, 17), 0), iota((128, 17), 1))
    line_ref[...] = jnp.zeros((40, LANES), F32)
    copies[0].wait()
    half = jnp.dot(plane, res_ref[...], precision=exact)
    vertex = jnp.dot(half, depth, precision=exact)
    low_face = res_ref[pl.ds(0, 32, stride=16), :]
    high_face = res_ref[pl.ds(15, 32, stride=16), :]
    for peer in range(8):
        pay_ref[peer, 0:32, :] = jnp.where(peer < q, low_face, high_face)
    copies[1].wait()
    rows = iota((256, 17), 0)
    spread = jnp.zeros((256, 17), F32)
    for i in range(5):
        for j in range(3):
            k = 3 * i + j
            spread = spread + jnp.where(num_ref[i, j : j + 1, :] == rows, vertex[k : k + 1, :], 0.0)
    ordered = jnp.broadcast_to(jnp.sum(spread, axis=1, keepdims=True), (256, LANES))

    for copy in copies[2:5]:
        copy.wait()
    for d in range(3):
        eigen_ref[:, 10 * d : 10 * d + 10] = value_ref[d]
        for i in range(10):
            low = 100 * d + 10 * i
            table_ref[:, low : low + 10] = basis_ref[d, i]
    for copy in copies[5:]:
        copy.wait()
    for c, (cut, width) in enumerate(CUTS):
        piece = jnp.sum(top_ref[:, cut] * ordered[:TOP, :width], axis=0, keepdims=True)
        piece = piece + jnp.sum(low_ref[:, cut] * ordered[TOP:255, :width], axis=0, keepdims=True)
        line_ref[8 + c : 9 + c, :width] = piece
    here = pltpu.roll(line_ref[8:32], 1, 1)
    before = pltpu.roll(line_ref[7:31], 1, 1)
    own_ref[...] = jnp.where(iota((24, LANES), 1) == 0, before, here)
    for peer in range(8):
        pay_ref[peer, 32:35, :] = own_ref[2:5, :]
        pay_ref[peer, 35:37, :] = own_ref[8 + 2 * peer : 10 + 2 * peer, :]
        pay_ref[peer, 37:40, :] = own_ref[5:8, :] if peer == 7 else jnp.zeros((3, LANES), F32)


def sum_kernel(got_ref, own_ref, tree_ref, four_ref):
    q = lax.axis_index("gy")
    total = got_ref[0, 35:40, :]
    for peer in range(1, 8):
        total = total + got_ref[peer, 35:40, :]
    four_ref[0:3, :] = total[2:5]
    four_ref[6:8, :] = own_ref[0:2, :]
    for level in range(1, 4):
        low = jnp.zeros((1, LANES), F32)
        for peer in range(8):
            inside = (peer >> level) == (q >> level)
            low = low + jnp.where(inside, got_ref[peer, 31 + level : 32 + level, :], 0.0)
        four_ref[2 + level : 3 + level, :] = low
    line = jnp.concatenate([total[0:1], total[1:2]], axis=1)
    for t in range(64):
        tree_ref[t] = line


def pack_kernel(got_ref, res_ref, cls_ref, four_ref, right_ref, left_ref, face_ref):
    q = lax.axis_index("gy")
    face_ref[0:32, :] = jnp.where(q > 0, got_ref[jnp.maximum(q - 1, 0), 0:32, :], 0.0)
    face_ref[32:64, :] = jnp.where(q < 7, got_ref[jnp.minimum(q + 1, 7), 0:32, :], 0.0)
    for ref, column, first in ((right_ref, 3, 23), (left_ref, 0, 0)):
        ref[0:144, :] = res_ref[16 * first : 16 * first + 144, :]
        ref[144:153, :] = face_ref[first : first + 9, :]
        ref[153:162, :] = face_ref[32 + first : 41 + first, :]
        ref[162:168, :] = jnp.zeros((6, LANES), F32)
        ref[162:164, 0:16] = (cls_ref[column] + 1).astype(F32)
        ref[164:167, :] = four_ref[0:3, :]


def grids():
    sub = iota((8, LANES), 0)
    lane = iota((8, LANES), 1)
    return sub, lane, lane & 15


def split_z(rows):
    lane = iota((LANES, LANES), 1)
    return moved(rows, (iota((LANES, LANES), 0) == (((lane & 15) << 3) | (lane >> 4))).astype(jnp.bfloat16))


def join_rows(rows):
    lane = iota((LANES, LANES), 0)
    return moved(rows, (iota((LANES, LANES), 1) == (((lane & 15) << 3) | (lane >> 4))).astype(jnp.bfloat16))


def exchange(groups):
    lane = iota((8, LANES), 1)
    groups = [list(parts) for parts in groups]
    for bit in (4, 2, 1):
        inside = (lane & (16 * bit)) != 0
        for parts in groups:
            for n in range(8):
                if n & bit:
                    continue
                low, high = parts[n], parts[n | bit]
                if bit == 4:
                    swap = pltpu.roll(jnp.where(inside, low, high), 64, 1)
                    parts[n] = jnp.where(inside, swap, low)
                    parts[n | bit] = jnp.where(inside, high, swap)
                else:
                    parts[n] = jnp.where(inside, pltpu.roll(high, 16 * bit, 1), low)
                    parts[n | bit] = jnp.where(inside, high, pltpu.roll(low, LANES - 16 * bit, 1))
    return groups


def with_outer(groups):
    kz = iota((8, LANES), 1) & 15
    before = [jnp.where(kz == 0, 0.0, pltpu.roll(parts[7], 1, 1)) for parts in groups]
    after = [jnp.where(kz == 15, 0.0, pltpu.roll(parts[0], 127, 1)) for parts in groups]
    return [parts + [b, a] for parts, b, a in zip(groups, before, after, strict=True)]


def at(i, j):
    return pl.ds(pl.multiple_of((i * 11 + j) * 16, 16), 16)


def join_z(total, sub, kz):
    main = total[0:8]
    tail = pltpu.roll(total[8:16], 7, 0)
    return main + jnp.where(
        sub == 7,
        jnp.where(kz == 15, 0.0, pltpu.roll(tail, 127, 1)),
        jnp.where((sub == 0) & (kz != 0), pltpu.roll(tail, 1, 1), 0.0),
    )


def row(ref, n):
    return jnp.broadcast_to(ref[pl.ds(n, 1), :], (16, LANES))


def dot_rows(pairs):
    total = None
    for a, b in pairs:
        total = a * b if total is None else total + a * b
    return total


def chosen(table, onehot):
    high = table.astype(jnp.bfloat16)
    rest = table - high.astype(F32)
    middle = rest.astype(jnp.bfloat16)
    low = (rest - middle.astype(F32)).astype(jnp.bfloat16)
    dims = (((0,), (0,)), ((), ()))
    total = lax.dot_general(low, onehot, dims, preferred_element_type=F32)
    total = total + lax.dot_general(middle, onehot, dims, preferred_element_type=F32)
    return total + lax.dot_general(high, onehot, dims, preferred_element_type=F32)


def pick_tables(kind, table_ref, eigen_ref, pick, eig):
    group = iota((8, LANES), 0)
    lane = iota((8, LANES), 1)
    spread = (iota((16, LANES), 0) == (iota((16, LANES), 1) & 15)).astype(F32)
    laid = jnp.dot(kind, spread, precision=exact)
    laid = jnp.sum(jnp.where(group == (lane >> 4), laid, 0.0), axis=0, keepdims=True)
    onehot = (laid == (group + 1).astype(F32)).astype(jnp.bfloat16)
    pick[0:300, :] = chosen(table_ref[:, 0:300], onehot)
    eig[0:30, :] = chosen(eigen_ref[:, 0:30], onehot)
    eig[20:30, :] = eig[20:30, :] + jnp.where(laid == 0.0, 1.0, 0.0)
    eig[30:40, :] = jnp.ones((10, LANES), F32)


def forward_z(pick, zfwd):
    for n, k in enumerate(ORDER):
        zfwd[n, 0:10, :] = pick[200 + 10 * k : 210 + 10 * k, :]
        zfwd[n, 10:16, :] = jnp.zeros((6, LANES), F32)


def backward_z(pick, zback):
    for c in range(10):
        zback[c, 0:8, :] = pick[pl.ds(210 + c, 8, stride=10), :]
        zback[c, 8:16, :] = jnp.zeros((8, LANES), F32)
        zback[c, 8:9, :] = pick[200 + c : 201 + c, :]
        zback[c, 9:10, :] = pick[290 + c : 291 + c, :]


def x_forward(win, table, target, count):
    def step(j, _):
        column = [win[at(i, j), :] for i in range(10)]
        for a in range(count):
            target[a, j] = dot_rows([(row(table, count * i + a), column[i]) for i in range(10)])
        return 0

    lax.fori_loop(0, 10, step, 0, unroll=2)


def through_z(source, zfwd, store):
    table = [zfwd[k] for k in range(10)]
    for b in range(10):
        store(b, dot_rows([(table[k], jnp.broadcast_to(source[b, k : k + 1, :], (16, LANES))) for k in range(10)]))


def y_forward(column, pick, target):
    for b in range(10):
        target[b] = dot_rows([(row(pick, 100 + 10 * j + b), column[j]) for j in range(10)])


def y_back(source, pick, store):
    column = [source[b] for b in range(10)]
    for j in range(10):
        store(j, dot_rows([(row(pick, 100 + 10 * j + b), column[b]) for b in range(10)]))


def into(ref, *place):
    def store(n, value):
        ref[(*place, n)] = value

    return store


def spectral_kernel(
    res_ref, face_ref, cls_ref, table_ref, eigen_ref,
    spec, sides, pick, eig, table_out,
    zfwd, rows_ref, rows_f, win, work, tmp,
):
    wide = iota((16, LANES), 1)
    upper = (wide & 16) != 0
    rows_ref[...] = split_z(res_ref[...])
    rows_f[...] = split_z(face_ref[...])
    kind = jnp.concatenate([cls_ref[ix].astype(F32) + 1.0 for ix in range(4)], axis=0)
    table_out[...] = table_ref[...]
    pick_tables(kind, table_ref, eigen_ref, pick, eig)
    forward_z(pick, zfwd)
    columns = range(8)
    groups = [
        [rows_ref[128 * (r // 2) + 16 * i + 8 * (r % 2) : 128 * (r // 2) + 16 * i + 8 * (r % 2) + 8, :] for r in range(8)]
        for i in columns
    ]
    groups.append([rows_f[32 * (r % 2) + 8 * (r // 2) : 32 * (r % 2) + 8 * (r // 2) + 8, :] for r in range(8)])
    groups = with_outer(exchange(groups))
    for k in range(10):
        win[pl.ds(21 * 16 + k, 8, stride=176), :] = groups[8][k]
    for i in columns:
        for k, part in enumerate(groups[i]):
            win[pl.ds((i * 11 + 12) * 16 + k, 8, stride=16), :] = part
    lines = (1, 2, 3, 4, 5, 6, 7, 8, 10)
    ahead = [win[at(8, j), :] for j in lines]
    back = [win[at(1, j), :] for j in lines]
    for n, j in enumerate(lines):
        sides[0, j] = back[n]
        sides[1, j] = ahead[n]
        win[at(0, j), :] = jnp.where(wide >= 32, pltpu.roll(ahead[n], 32, 1), 0.0)
        win[at(9, j), :] = jnp.where(wide < 96, pltpu.roll(back[n], 96, 1), 0.0)

    def y_halo(n, _):
        columns = [5 * n + m for m in range(5)]
        outer = [win[at(i, 10), :] for i in columns]
        last = [pltpu.roll(win[at(i, 8), :], 16, 1) for i in columns]
        first = [pltpu.roll(win[at(i, 1), :], 112, 1) for i in columns]
        for m, i in enumerate(columns):
            win[at(i, 0), :] = jnp.where(upper, last[m], outer[m])
            win[at(i, 9), :] = jnp.where(upper, outer[m], first[m])
        return 0

    lax.fori_loop(0, 2, y_halo, 0)
    x_forward(win, pick, work, 10)

    def step(a, _):
        y_forward([work[a, j] for j in range(10)], pick, tmp)
        through_z(tmp, zfwd, into(spec, a))
        return 0

    lax.fori_loop(0, 10, step, 0, unroll=2)


def solve_kernel(
    spec, sides, table_ref, eigen_ref, pick_m, eig_m, from_left, from_right, pan_hbm,
    fine_ref, rim_ref, low_ref,
    work, edge, ends, tiles, rows_ref, rows_f, rows_e, win_e, pick_e, eig_e, zfwd_e, zback_e, zfwd_m, zback_m,
    half_e, lxe, work_e, tmp_a, tmp_b, tmp_c, rim_rows, late, sems,
):
    copy = pltpu.make_async_copy(pan_hbm.at[pl.ds(TOP, 255 - TOP), :], low_ref, sems.at[0])
    copy.start()
    sub, lane, kz = grids()
    wide = iota((16, LANES), 1)
    upper = (wide & 16) != 0

    rows_f[0:24, :] = from_left[144:168, :]
    rows_f[24:48, :] = from_right[144:168, :]
    rows_f[0:48, :] = split_z(rows_f[0:48, :])
    rows_e[0:144, :] = from_left[0:144, :]
    rows_e[144:288, :] = from_right[0:144, :]
    rows_e[...] = split_z(rows_e[...])
    beside = [rows_f[first : first + 8, :] for first in (1, 10, 24, 33)]
    corner = [jnp.broadcast_to(rows_f[n : n + 1, :], (8, LANES)) for n in (0, 9, 32, 41)]
    beside, corner = with_outer(exchange([beside + beside, corner + corner]))
    for k in range(10):
        win_e[pl.ds(21 * 16 + k, 8, stride=176), :] = beside[k]
        win_e[109 * 16 + k : 109 * 16 + k + 1, :] = corner[k][0:1]

    def fill(n, _):
        columns = [9 * n + m for m in range(9)]
        groups = []
        for i in columns:
            layer = jnp.where(i == 8, 0, i + 1)
            parts = [rows_e[pl.ds(pl.multiple_of(16 * layer + 8 * jy, 8), 8), :] for jy in range(2)]
            parts += [rows_e[pl.ds(pl.multiple_of(144 + 16 * i + 8 * jy, 8), 8), :] for jy in range(2)]
            groups.append(parts + parts)
        for i, parts in zip(columns, with_outer(exchange(groups)), strict=True):
            for k, part in enumerate(parts):
                win_e[pl.ds((i * 11 + 12) * 16 + k, 8, stride=16), :] = part
        return 0

    lax.fori_loop(0, 1, fill, 0)

    near = [from_left[162:164, 0:16], from_right[162:164, 0:16]]
    pick_tables(jnp.concatenate(near + near, axis=0), table_ref, eigen_ref, pick_e, eig_e)
    for pick, zfwd, zback in ((pick_e, zfwd_e, zback_e), (pick_m, zfwd_m, zback_m)):
        forward_z(pick, zfwd)
        backward_z(pick, zback)
    low_half = iota((5, LANES), 1) < 64
    for i in range(10):
        half_e[5 * i : 5 * i + 5, :] = jnp.where(low_half, pick_e[10 * i : 10 * i + 5, :], pick_e[10 * i + 5 : 10 * i + 10, :])
    half_e[50:55, :] = jnp.where((iota((5, LANES), 1) & 32) == 0, half_e[45:50, :], half_e[0:5, :])
    lxe[0:5, :] = jnp.where(low_half, eig_e[0:5, :], eig_e[5:10, :])

    second = (wide & 32) != 0
    lines = (1, 2, 3, 4, 5, 6, 7, 8, 10)
    both = [pltpu.roll(jnp.where(wide < 64, sides[0, j], sides[1, j]), 64, 1) for j in lines]
    for n, j in enumerate(lines):
        extra = win_e[at(9, j), :]
        win_e[at(0, j), :] = jnp.where(second, jnp.where(wide >= 64, sides[1, j], both[n]), extra)
        win_e[at(9, j), :] = jnp.where(second, extra, jnp.where(wide < 64, sides[0, j], both[n]))
    outer = [win_e[at(i, 10), :] for i in range(10)]
    last = [pltpu.roll(win_e[at(i, 8), :], 16, 1) for i in range(10)]
    first = [pltpu.roll(win_e[at(i, 1), :], 112, 1) for i in range(10)]
    for i in range(10):
        win_e[at(i, 0), :] = jnp.where(upper, last[i], outer[i])
        win_e[at(i, 9), :] = jnp.where(upper, outer[i], first[i])

    def scale(level, eig, b):
        return level + row(eig, 10 + b)

    x_forward(win_e, half_e, work_e, 5)
    for b in range(10):
        edge[b] = jnp.zeros((16, LANES), F32)

    def edge_step(a, _):
        y_forward([work_e[a, j] for j in range(10)], pick_e, tmp_a)
        level = row(lxe, a) + eig_e[20:36, :]
        weight = row(half_e, 50 + a)

        def add(b, value):
            edge[b] = edge[b] + weight * (value / scale(level, eig_e, b))

        through_z(tmp_a, zfwd_e, add)
        return 0

    lax.fori_loop(0, 5, edge_step, 0)
    for b in range(10):
        tmp_b[b] = edge[b] + pltpu.roll(edge[b], 64, 1)
    through_z(tmp_b, zback_e, into(tmp_c))
    y_back(tmp_c, pick_e, into(edge))

    inner = (wide >= 32) & (wide < 96)
    beyond = [jnp.where(inner, 0.0, jnp.where(wide < 32, win_e[at(8, j), :], win_e[at(1, j), :])) for j in range(10)]
    y_forward(beyond, pick_m, tmp_a)
    through_z(tmp_a, zfwd_m, into(late))
    lxe[0:16, :] = jnp.where(iota((16, LANES), 1) < 64, pick_m[0:16, :], pick_m[90:106, :])

    def main_step(a, _):
        level = row(eig_m, a) + eig_m[20:36, :]
        weight = row(lxe, a)
        for b in range(10):
            tmp_b[b] = (spec[a, b] + weight * late[b]) / scale(level, eig_m, b)
        through_z(tmp_b, zback_m, into(tmp_c))
        y_back(tmp_c, pick_m, into(work, a))
        return 0

    lax.fori_loop(0, 10, main_step, 0)

    for n, j in ((0, 0), (1, 9)):
        def put_end(i, main, n=n):
            ends[n, i - 1] = main

        x_back(work, edge, pick_m, j, put_end)
    for i in range(8):
        rim_rows[8 * i : 8 * i + 8, :] = jnp.where(upper[0:8], ends[1, i], ends[0, i])
    (parts,) = exchange([[rim_rows[pl.ds(k, 8, stride=8), :] for k in range(8)]])
    for r in range(8):
        rows_f[32 * (r % 2) + 8 * (r // 2) : 32 * (r % 2) + 8 * (r // 2) + 8, :] = parts[r]
    rim_ref[...] = join_rows(rows_f[0:64, :])
    inner = upper[0:8]

    def solve(j, _):
        def put(i, tile):
            tile = tile + jnp.where(inner & (j == 1), pltpu.roll(ends[1, i - 1], 16, 1), 0.0)
            tile = tile + jnp.where(inner | (j != 8), 0.0, pltpu.roll(ends[0, i - 1], 112, 1))
            tiles[pl.ds(pl.multiple_of(((i - 1) * 8 + j - 1) * 8, 8), 8), :] = tile

        x_back(work, edge, pick_m, j, put)
        return 0

    lax.fori_loop(1, 9, solve, 0, unroll=8)

    def step(n, _):
        columns = [8 * n + m for m in range(8)]
        groups = exchange([[tiles[pl.ds(i * 64 + k, 8, stride=8), :] for k in range(8)] for i in columns])
        for i, parts in zip(columns, groups, strict=True):
            for r in range(8):
                rows_ref[pl.ds(pl.multiple_of(128 * (r // 2) + 16 * i + 8 * (r % 2), 8), 8), :] = parts[r]
        return 0

    lax.fori_loop(0, 1, step, 0)
    fine_ref[...] = join_rows(rows_ref[...])
    copy.wait()


def x_back(work, edge, pick, j, put):
    sub, lane, kz = grids()
    wide = iota((16, LANES), 1)
    column = [work[a, j] for a in range(10)]
    first = dot_rows([(row(pick, a), column[a]) for a in range(10)])
    last = dot_rows([(row(pick, 90 + a), column[a]) for a in range(10)])
    side = edge[j]
    for i in range(1, 9):
        total = dot_rows([(row(pick, 10 * i + a), column[a]) for a in range(10)])
        if i == 1:
            total = total + jnp.where(wide >= 32, pltpu.roll(last, 32, 1), side)
        if i == 8:
            total = total + jnp.where(wide < 96, pltpu.roll(first, 96, 1), side)
        put(i, join_z(total, sub, kz))


def tree_kernel(got_ref, rim_ref, four_ref, from_left, from_right, pay_ref):
    p = lax.axis_index("gx")
    q = lax.axis_index("gy")
    totals = []
    for n in range(2):
        bits = 2 + (2 * q + n) // 3
        total = jnp.zeros((1, LANES), F32)
        for t in range(64):
            inside = (t >> bits) == (p >> bits)
            total = total + jnp.where(inside, got_ref[t, :, LANES * n : LANES * (n + 1)], 0.0)
        totals.append(total)
    four = four_ref[0:3, :] + jnp.where((p & 1) == 0, from_right[164:167, :], from_left[164:167, :])
    for peer in range(8):
        pay_ref[peer, 0:32, :] = jnp.where(peer < q, rim_ref[0:32, :], rim_ref[32:64, :])
        pay_ref[peer, 32:33, :] = totals[0]
        pay_ref[peer, 33:34, :] = totals[1]
        pay_ref[peer, 34:37, :] = four
        pay_ref[peer, 37:40, :] = jnp.zeros((3, LANES), F32)


def up_kernel(
    four_ref, got_ref, num_hbm, top_ref, low_ref, fine_ref, out_ref, line_ref, coeff_ref, sums_ref, vertex_ref, num_ref, sems
):
    q = lax.axis_index("gy")
    copy = pltpu.make_async_copy(num_hbm, num_ref, sems.at[0])
    copy.start()
    line_ref[...] = jnp.zeros((32, LANES), F32)
    line_ref[0:2, :] = four_ref[6:8, :]
    line_ref[2:5, :] = four_ref[3:6, :]
    line_ref[5:8, :] = got_ref[7, 34:37, :]
    for peer in range(8):
        line_ref[8 + 2 * peer : 10 + 2 * peer, :] = got_ref[peer, 32:34, :]
    here = pltpu.roll(line_ref[0:24], 127, 1)
    after = pltpu.roll(line_ref[1:25], 127, 1)
    coeff_ref[...] = jnp.where(iota((24, LANES), 1) == 127, after, here)
    weights = [jnp.broadcast_to(coeff_ref[c : c + 1, :width], (8, width)) for c, (_, width) in enumerate(CUTS)]

    def product(ref, first, place, count):
        total = ref[place, CUTS[0][0]] * weights[0][:count]
        for weight, (cut, _) in zip(weights[1:22], CUTS[1:22], strict=True):
            total = total + ref[place, cut] * weight[:count]
        end = ref[place, CUTS[22][0]] * weights[22][:count]
        sums_ref[pl.ds(first, count), :] = total
        sums_ref[pl.ds(first, count), 0:127] = total[:, 0:127] + end

    def step(g, _):
        first = pl.multiple_of(8 * g, 8)
        product(top_ref, first, pl.ds(first, 8), 8)
        return 0

    lax.fori_loop(0, TOP // 8, step, 0, unroll=TOP // 16)
    for low in range(0, 248 - TOP, 8):
        product(low_ref, TOP + low, pl.ds(low, 8), 8)
    product(low_ref, 248, pl.ds(248 - TOP, 7), 7)
    sums_ref[255:256, :] = jnp.zeros((1, LANES), F32)
    values = jnp.broadcast_to(jnp.sum(sums_ref[...], axis=1, keepdims=True), (256, 17))
    vertex_ref[...] = jnp.zeros((16, LANES), F32)
    rows = iota((256, 17), 0)
    copy.wait()
    for i in range(5):
        for j in range(3):
            k = 3 * i + j
            vertex_ref[k : k + 1, 0:17] = jnp.sum(jnp.where(num_ref[i, j : j + 1, :] == rows, values, 0.0), axis=0, keepdims=True)
    depth = hat(iota((LANES, LANES), 1), iota((LANES, LANES), 0)).astype(jnp.bfloat16)
    vertex_ref[...] = moved(vertex_ref[...], depth)
    rise = (2.0 * iota((8, LANES), 0).astype(F32) + 1.0) / 16.0
    planes = []
    for i in range(5):
        three = [jnp.broadcast_to(vertex_ref[3 * i + j : 3 * i + j + 1, :], (8, LANES)) for j in range(3)]
        planes.append([three[jy] * (1.0 - rise) + three[jy + 1] * rise for jy in range(2)])
    faces = (
        jnp.where(q > 0, got_ref[jnp.maximum(q - 1, 0), 0:32, :], 0.0),
        jnp.where(q < 7, got_ref[jnp.minimum(q + 1, 7), 0:32, :], 0.0),
    )
    edges = (iota((8, LANES), 0) == 0, iota((8, LANES), 0) == 7)
    for ix in range(4):
        for i in range(8):
            x = 8 * ix + i
            far = (2 * i + 1) / 16.0
            for jy in range(2):
                place = slice(16 * x + 8 * jy, 16 * x + 8 * jy + 8)
                value = fine_ref[place, :] + planes[ix][jy] * (1.0 - far) + planes[ix + 1][jy] * far
                out_ref[place, :] = value + jnp.where(edges[jy], faces[jy][x : x + 1, :], 0.0)


VM = pltpu.VMEM
ANYWHERE = None


def call(kernel, outs, scratch=(), ins=None, sems=0, cost=0, limit=24, aliases=None):
    shapes = [
        jax.ShapeDtypeStruct(o[0], o[2] if len(o) > 2 else F32) if o[1] is None else o[1](o[0], o[2] if len(o) > 2 else F32)
        for o in outs
    ]
    spaces = [pltpu.VMEM(s, F32) if isinstance(s, tuple) else s for s in scratch]
    if sems:
        spaces.append(pltpu.SemaphoreType.DMA((sems,)))
    run = pl.pallas_call(
        kernel,
        out_shape=shapes,
        in_specs=[pl.BlockSpec(memory_space=m or pltpu.VMEM) for m in ins],
        out_specs=[pl.BlockSpec(memory_space=pltpu.VMEM) for _ in outs],
        scratch_shapes=spaces,
        input_output_aliases=aliases or {},
        compiler_params=pltpu.CompilerParams(vmem_limit_bytes=limit << 20),
        cost_estimate=pl.CostEstimate(flops=cost, bytes_accessed=cost // 400, transcendentals=0),
    )

    def apply(*operands):
        held = [x if m is None else pltpu.with_memory_space_constraint(x, m) for x, m in zip(operands, ins, strict=True)]
        return run(*held)

    return apply


def spread_to(block, axis):
    return lax.all_to_all(block, axis, 0, 0, tiled=True)


def shards(residual, elem_class, basis, eigenvalues, vertex_number, panels):
    field = residual.reshape(512, LANES)
    I32 = jnp.int32
    pay, own, cls, top, res, table, eigen = call(
        down_kernel,
        [
            ((8, 40, 128), VM), ((24, 128), VM), ((4, 2, 16), VM, I32), ((TOP, 2943), VM),
            ((512, 128), VM), ((8, 300), VM), ((8, 30), VM),
        ],
        [(40, 128), (3, 10, 8, 10), (3, 8, 10), (255 - TOP, 2943), VM((5, 3, 17), I32)], ins=[pltpu.HBM] * 6, sems=7,
    )(field, vertex_number, panels, elem_class, basis.transpose(1, 2, 0, 3), eigenvalues.transpose(1, 0, 2))
    first = spread_to(pay, "gy")
    tree, four = call(sum_kernel, [((64, 1, 256), VM), ((8, 128), VM)], ins=[None, VM])(first, own)
    summed = spread_to(tree, "gx")
    right, left, face = call(
        pack_kernel, [((168, 128), VM), ((168, 128), VM), ((64, 128), VM)], ins=[None, VM, VM, VM], cost=2_000_000_000
    )(first, res, cls, four)
    from_left = lax.ppermute(right, "gx", [(i, i + 1) for i in range(63)])
    from_right = lax.ppermute(left, "gx", [(i + 1, i) for i in range(63)])
    spec, sides, pick, eig, table_out = call(
        spectral_kernel,
        [
            ((10, 10, 16, 128), VM), ((2, 11, 16, 128), VM), ((304, 128), VM), ((40, 128), VM), ((8, 300), VM),
        ],
        [(10, 16, 128), (512, 128), (64, 128), (1760, 128), (10, 10, 16, 128), (10, 16, 128)], ins=[VM] * 5, cost=2_000_000_000,
    )(res, face, cls, table, eigen)
    fine, rim, low = call(
        solve_kernel,
        [((512, 128), VM), ((64, 128), VM), ((255 - TOP, 2943), VM)],
        [
            (10, 10, 16, 128), (10, 16, 128), (2, 8, 8, 128), (512, 128), (512, 128),
            (64, 128), (288, 128), (1760, 128), (304, 128), (40, 128), (10, 16, 128), (10, 16, 128), (10, 16, 128), (10, 16, 128),
            (56, 128), (16, 128), (5, 10, 16, 128), (10, 16, 128), (10, 16, 128), (10, 16, 128), (64, 128), (10, 16, 128),
        ],
        ins=[VM] * 6 + [None, None, pltpu.HBM], sems=1, cost=1_000_000_000,
    )(spec, sides, table_out, eigen, pick, eig, from_left, from_right, panels)
    (pay,) = call(tree_kernel, [((8, 40, 128), VM)], ins=[None, VM, VM, None, None])(summed, rim, four, from_left, from_right)
    second = spread_to(pay, "gy")
    (out,) = call(
        up_kernel, [((512, 128), None)], [(32, 128), (24, 128), (256, 128), (16, 128), VM((5, 3, 17), I32)],
        ins=[VM, None, pltpu.HBM, VM, VM, VM], sems=1,
    )(four, second, vertex_number, top, low, fine)
    return out.reshape(residual.shape)


def solution(mesh):
    return jax.shard_map(
        shards,
        mesh=mesh,
        in_specs=(
            P(None, "gx", "gy", None),
            P("gx", "gy", None),
            P(),
            P(),
            P("gx", "gy", None),
            P("gx", "gy"),
        ),
        out_specs=P(None, "gx", "gy", None),
        check_vma=False,
    )
```

```python
import functools

import jax
import jax.numpy as jnp
from jax import lax
from jax.experimental import pallas as pl
from jax.experimental.pallas import tpu as pltpu
from jax.sharding import PartitionSpec as P

NPR = 8
NEXT = 10
NCLASS = 8
LANES = 128
TOP = 208
CUTS = [(slice(low, min(low + 128, 2943)), min(128, 2943 - low)) for low in range(0, 2943, 128)]
HALO = NPR + 1
F32 = jnp.float32
exact = lax.Precision.HIGHEST
ORDER = (1, 2, 3, 4, 5, 6, 7, 8, 0, 9)


def iota(shape, axis):
    return lax.broadcasted_iota(jnp.int32, shape, axis)


def hat(point, vertex):
    place = (point.astype(F32) + 0.5) / NPR
    return jnp.maximum(0.0, 1.0 - jnp.abs(place - vertex.astype(F32)))


def moved(rows, table):
    high = rows.astype(jnp.bfloat16)
    rest = rows - high.astype(F32)
    middle = rest.astype(jnp.bfloat16)
    low = (rest - middle.astype(F32)).astype(jnp.bfloat16)
    total = jnp.dot(low, table, preferred_element_type=F32)
    total = total + jnp.dot(middle, table, preferred_element_type=F32)
    return total + jnp.dot(high, table, preferred_element_type=F32)


def plane_hat(point, vertex):
    third = (vertex.astype(F32) + 0.5) / 3.0
    big = third.astype(jnp.int32)
    return hat(point >> 4, big) * hat(point & 15, vertex - 3 * big)


def down_kernel(
    res_hbm, num_hbm, pan_hbm, cls_hbm, basis_hbm, value_hbm,
    pay_ref, own_ref, cls_ref, top_ref, res_ref, table_ref, eigen_ref,
    line_ref, basis_ref, value_ref, low_ref, num_ref, sems,
):
    q = lax.axis_index("gy")
    pairs = [
        (res_hbm, res_ref), (num_hbm, num_ref), (cls_hbm, cls_ref), (basis_hbm, basis_ref), (value_hbm, value_ref),
        (pan_hbm.at[pl.ds(0, TOP), :], top_ref), (pan_hbm.at[pl.ds(TOP, 255 - TOP), :], low_ref),
    ]
    copies = [pltpu.make_async_copy(source, target, sems.at[n]) for n, (source, target) in enumerate(pairs)]
    for copy in copies:
        copy.start()
    plane = plane_hat(iota((16, 512), 1), iota((16, 512), 0))
    depth = hat(iota((128, 17), 0), iota((128, 17), 1))
    line_ref[...] = jnp.zeros((40, LANES), F32)
    copies[0].wait()
    half = jnp.dot(plane, res_ref[...], precision=exact)
    vertex = jnp.dot(half, depth, precision=exact)
    low_face = res_ref[pl.ds(0, 32, stride=16), :]
    high_face = res_ref[pl.ds(15, 32, stride=16), :]
    for peer in range(8):
        pay_ref[peer, 0:32, :] = jnp.where(peer < q, low_face, high_face)
    copies[1].wait()
    rows = iota((256, 17), 0)
    spread = jnp.zeros((256, 17), F32)
    for i in range(5):
        for j in range(3):
            k = 3 * i + j
            spread = spread + jnp.where(num_ref[i, j : j + 1, :] == rows, vertex[k : k + 1, :], 0.0)
    ordered = jnp.broadcast_to(jnp.sum(spread, axis=1, keepdims=True), (256, LANES))

    for copy in copies[2:5]:
        copy.wait()
    for d in range(3):
        eigen_ref[:, 10 * d : 10 * d + 10] = value_ref[d]
        for i in range(10):
            low = 100 * d + 10 * i
            table_ref[:, low : low + 10] = basis_ref[d, i]
    own_ref[24:40, :] = jnp.zeros((16, LANES), F32)
    for i in range(5):
        own_ref[24 + 3 * i : 27 + 3 * i, 0:17] = num_ref[i].astype(F32)
    copies[5].wait()
    for c, (cut, width) in enumerate(CUTS):
        line_ref[8 + c : 9 + c, :width] = jnp.sum(top_ref[:, cut] * ordered[:TOP, :width], axis=0, keepdims=True)
    copies[6].wait()
    for c, (cut, width) in enumerate(CUTS):
        piece = jnp.sum(low_ref[:, cut] * ordered[TOP:255, :width], axis=0, keepdims=True)
        line_ref[8 + c : 9 + c, :width] = line_ref[8 + c : 9 + c, :width] + piece
    here = pltpu.roll(line_ref[8:32], 1, 1)
    before = pltpu.roll(line_ref[7:31], 1, 1)
    own_ref[0:24, :] = jnp.where(iota((24, LANES), 1) == 0, before, here)
    for peer in range(8):
        pay_ref[peer, 32:35, :] = own_ref[2:5, :]
        pay_ref[peer, 35:37, :] = own_ref[8 + 2 * peer : 10 + 2 * peer, :]
        pay_ref[peer, 37:40, :] = own_ref[5:8, :] if peer == 7 else jnp.zeros((3, LANES), F32)


def sum_kernel(got_ref, own_ref, tree_ref, four_ref):
    q = lax.axis_index("gy")
    total = got_ref[0, 35:40, :]
    for peer in range(1, 8):
        total = total + got_ref[peer, 35:40, :]
    four_ref[0:3, :] = total[2:5]
    four_ref[6:8, :] = own_ref[0:2, :]
    four_ref[8:24, :] = own_ref[24:40, :]
    for level in range(1, 4):
        low = jnp.zeros((1, LANES), F32)
        for peer in range(8):
            inside = (peer >> level) == (q >> level)
            low = low + jnp.where(inside, got_ref[peer, 31 + level : 32 + level, :], 0.0)
        four_ref[2 + level : 3 + level, :] = low
    line = jnp.concatenate([total[0:1], total[1:2]], axis=1)
    for t in range(64):
        tree_ref[t] = line


def pack_kernel(got_ref, res_ref, cls_ref, four_ref, right_ref, left_ref, face_ref):
    q = lax.axis_index("gy")
    face_ref[0:32, :] = jnp.where(q > 0, got_ref[jnp.maximum(q - 1, 0), 0:32, :], 0.0)
    face_ref[32:64, :] = jnp.where(q < 7, got_ref[jnp.minimum(q + 1, 7), 0:32, :], 0.0)
    for ref, column, first in ((right_ref, 3, 23), (left_ref, 0, 0)):
        ref[0:144, :] = res_ref[16 * first : 16 * first + 144, :]
        ref[144:153, :] = face_ref[first : first + 9, :]
        ref[153:162, :] = face_ref[32 + first : 41 + first, :]
        ref[162:168, :] = jnp.zeros((6, LANES), F32)
        ref[162:164, 0:16] = (cls_ref[column] + 1).astype(F32)
        ref[164:167, :] = four_ref[0:3, :]


def grids():
    sub = iota((8, LANES), 0)
    lane = iota((8, LANES), 1)
    return sub, lane, lane & 15


def split_z(rows):
    lane = iota((LANES, LANES), 1)
    return moved(rows, (iota((LANES, LANES), 0) == (((lane & 15) << 3) | (lane >> 4))).astype(jnp.bfloat16))


def join_rows(rows):
    lane = iota((LANES, LANES), 0)
    return moved(rows, (iota((LANES, LANES), 1) == (((lane & 15) << 3) | (lane >> 4))).astype(jnp.bfloat16))


def exchange(groups):
    lane = iota((8, LANES), 1)
    groups = [list(parts) for parts in groups]
    for bit in (4, 2, 1):
        inside = (lane & (16 * bit)) != 0
        for parts in groups:
            for n in range(8):
                if n & bit:
                    continue
                low, high = parts[n], parts[n | bit]
                if bit == 4:
                    swap = pltpu.roll(jnp.where(inside, low, high), 64, 1)
                    parts[n] = jnp.where(inside, swap, low)
                    parts[n | bit] = jnp.where(inside, high, swap)
                else:
                    parts[n] = jnp.where(inside, pltpu.roll(high, 16 * bit, 1), low)
                    parts[n | bit] = jnp.where(inside, high, pltpu.roll(low, LANES - 16 * bit, 1))
    return groups


def with_outer(groups):
    kz = iota((8, LANES), 1) & 15
    before = [jnp.where(kz == 0, 0.0, pltpu.roll(parts[7], 1, 1)) for parts in groups]
    after = [jnp.where(kz == 15, 0.0, pltpu.roll(parts[0], 127, 1)) for parts in groups]
    return [parts + [b, a] for parts, b, a in zip(groups, before, after, strict=True)]


def at(i, j):
    return pl.ds(pl.multiple_of((i * 11 + j) * 16, 16), 16)


def join_z(total, sub, kz):
    main = total[0:8]
    tail = pltpu.roll(total[8:16], 7, 0)
    return main + jnp.where(
        sub == 7,
        jnp.where(kz == 15, 0.0, pltpu.roll(tail, 127, 1)),
        jnp.where((sub == 0) & (kz != 0), pltpu.roll(tail, 1, 1), 0.0),
    )


def row(ref, n):
    return jnp.broadcast_to(ref[pl.ds(n, 1), :], (16, LANES))


def dot_rows(pairs):
    total = None
    for a, b in pairs:
        total = a * b if total is None else total + a * b
    return total


def chosen(table, onehot):
    high = table.astype(jnp.bfloat16)
    rest = table - high.astype(F32)
    middle = rest.astype(jnp.bfloat16)
    low = (rest - middle.astype(F32)).astype(jnp.bfloat16)
    dims = (((0,), (0,)), ((), ()))
    total = lax.dot_general(low, onehot, dims, preferred_element_type=F32)
    total = total + lax.dot_general(middle, onehot, dims, preferred_element_type=F32)
    return total + lax.dot_general(high, onehot, dims, preferred_element_type=F32)


def pick_tables(kind, table_ref, eigen_ref, pick, eig):
    group = iota((8, LANES), 0)
    lane = iota((8, LANES), 1)
    spread = (iota((16, LANES), 0) == (iota((16, LANES), 1) & 15)).astype(F32)
    laid = jnp.dot(kind, spread, precision=exact)
    laid = jnp.sum(jnp.where(group == (lane >> 4), laid, 0.0), axis=0, keepdims=True)
    onehot = (laid == (group + 1).astype(F32)).astype(jnp.bfloat16)
    pick[0:300, :] = chosen(table_ref[:, 0:300], onehot)
    eig[0:30, :] = chosen(eigen_ref[:, 0:30], onehot)
    eig[20:30, :] = eig[20:30, :] + jnp.where(laid == 0.0, 1.0, 0.0)
    eig[30:40, :] = jnp.ones((10, LANES), F32)


def forward_z(pick, zfwd):
    for n, k in enumerate(ORDER):
        zfwd[n, 0:10, :] = pick[200 + 10 * k : 210 + 10 * k, :]
        zfwd[n, 10:16, :] = jnp.zeros((6, LANES), F32)


def backward_z(pick, zback):
    for c in range(10):
        zback[c, 0:8, :] = pick[pl.ds(210 + c, 8, stride=10), :]
        zback[c, 8:16, :] = jnp.zeros((8, LANES), F32)
        zback[c, 8:9, :] = pick[200 + c : 201 + c, :]
        zback[c, 9:10, :] = pick[290 + c : 291 + c, :]


def x_forward(win, table, target, count):
    def step(j, _):
        column = [win[at(i, j), :] for i in range(10)]
        for a in range(count):
            target[a, j] = dot_rows([(row(table, count * i + a), column[i]) for i in range(10)])
        return 0

    lax.fori_loop(0, 10, step, 0, unroll=2)


def through_z(source, zfwd, store):
    table = [zfwd[k] for k in range(10)]
    for b in range(10):
        store(b, dot_rows([(table[k], jnp.broadcast_to(source[b, k : k + 1, :], (16, LANES))) for k in range(10)]))


def y_forward(column, pick, target):
    for b in range(10):
        target[b] = dot_rows([(row(pick, 100 + 10 * j + b), column[j]) for j in range(10)])


def y_back(source, pick, store):
    column = [source[b] for b in range(10)]
    for j in range(10):
        store(j, dot_rows([(row(pick, 100 + 10 * j + b), column[b]) for b in range(10)]))


def into(ref, *place):
    def store(n, value):
        ref[(*place, n)] = value

    return store


def spectral_kernel(
    res_ref, face_ref, cls_ref, table_ref, eigen_ref,
    spec, sides, pick, eig, table_out,
    zfwd, rows_ref, rows_f, win, work, tmp,
):
    wide = iota((16, LANES), 1)
    upper = (wide & 16) != 0
    rows_ref[...] = split_z(res_ref[...])
    rows_f[...] = split_z(face_ref[...])
    kind = jnp.concatenate([cls_ref[ix].astype(F32) + 1.0 for ix in range(4)], axis=0)
    table_out[...] = table_ref[...]
    pick_tables(kind, table_ref, eigen_ref, pick, eig)
    forward_z(pick, zfwd)
    columns = range(8)
    groups = [
        [rows_ref[128 * (r // 2) + 16 * i + 8 * (r % 2) : 128 * (r // 2) + 16 * i + 8 * (r % 2) + 8, :] for r in range(8)]
        for i in columns
    ]
    groups.append([rows_f[32 * (r % 2) + 8 * (r // 2) : 32 * (r % 2) + 8 * (r // 2) + 8, :] for r in range(8)])
    groups = with_outer(exchange(groups))
    for k in range(10):
        win[pl.ds(21 * 16 + k, 8, stride=176), :] = groups[8][k]
    for i in columns:
        for k, part in enumerate(groups[i]):
            win[pl.ds((i * 11 + 12) * 16 + k, 8, stride=16), :] = part
    lines = (1, 2, 3, 4, 5, 6, 7, 8, 10)
    ahead = [win[at(8, j), :] for j in lines]
    back = [win[at(1, j), :] for j in lines]
    for n, j in enumerate(lines):
        sides[0, n] = back[n]
        sides[1, n] = ahead[n]
        win[at(0, j), :] = jnp.where(wide >= 32, pltpu.roll(ahead[n], 32, 1), 0.0)
        win[at(9, j), :] = jnp.where(wide < 96, pltpu.roll(back[n], 96, 1), 0.0)

    def y_halo(n, _):
        columns = [5 * n + m for m in range(5)]
        outer = [win[at(i, 10), :] for i in columns]
        last = [pltpu.roll(win[at(i, 8), :], 16, 1) for i in columns]
        first = [pltpu.roll(win[at(i, 1), :], 112, 1) for i in columns]
        for m, i in enumerate(columns):
            win[at(i, 0), :] = jnp.where(upper, last[m], outer[m])
            win[at(i, 9), :] = jnp.where(upper, outer[m], first[m])
        return 0

    lax.fori_loop(0, 2, y_halo, 0)
    x_forward(win, pick, work, 10)

    def step(a, _):
        y_forward([work[a, j] for j in range(10)], pick, tmp)
        through_z(tmp, zfwd, into(spec, a))
        return 0

    lax.fori_loop(0, 10, step, 0, unroll=2)


def solve_kernel(
    spec, sides, table_ref, eigen_ref, pick_m, eig_m, four_ref, from_left, from_right, pan_hbm,
    fine_ref, low_ref,
    work, edge, ends, tiles, rows_ref, rows_f, rows_e, win_e, pick_e, eig_e, zfwd_e, zback_e, zfwd_m, zback_m,
    half_e, lxe, work_e, tmp_a, tmp_b, tmp_c, rim_rows, late, sems,
):
    copy = pltpu.make_async_copy(pan_hbm.at[pl.ds(TOP, 255 - TOP), :], low_ref, sems.at[0])
    copy.start()
    sub, lane, kz = grids()
    wide = iota((16, LANES), 1)
    upper = (wide & 16) != 0

    rows_f[0:24, :] = from_left[144:168, :]
    rows_f[24:48, :] = from_right[144:168, :]
    rows_f[0:48, :] = split_z(rows_f[0:48, :])
    rows_e[0:144, :] = from_left[0:144, :]
    rows_e[144:288, :] = from_right[0:144, :]
    rows_e[...] = split_z(rows_e[...])
    beside = [rows_f[first : first + 8, :] for first in (1, 10, 24, 33)]
    corner = [jnp.broadcast_to(rows_f[n : n + 1, :], (8, LANES)) for n in (0, 9, 32, 41)]
    beside, corner = with_outer(exchange([beside + beside, corner + corner]))
    for k in range(10):
        win_e[pl.ds(21 * 16 + k, 8, stride=176), :] = beside[k]
        win_e[109 * 16 + k : 109 * 16 + k + 1, :] = corner[k][0:1]

    def fill(n, _):
        columns = [9 * n + m for m in range(9)]
        groups = []
        for i in columns:
            layer = jnp.where(i == 8, 0, i + 1)
            parts = [rows_e[pl.ds(pl.multiple_of(16 * layer + 8 * jy, 8), 8), :] for jy in range(2)]
            parts += [rows_e[pl.ds(pl.multiple_of(144 + 16 * i + 8 * jy, 8), 8), :] for jy in range(2)]
            groups.append(parts + parts)
        for i, parts in zip(columns, with_outer(exchange(groups)), strict=True):
            for k, part in enumerate(parts):
                win_e[pl.ds((i * 11 + 12) * 16 + k, 8, stride=16), :] = part
        return 0

    lax.fori_loop(0, 1, fill, 0)

    near = [from_left[162:164, 0:16], from_right[162:164, 0:16]]
    pick_tables(jnp.concatenate(near + near, axis=0), table_ref, eigen_ref, pick_e, eig_e)
    for pick, zfwd, zback in ((pick_e, zfwd_e, zback_e), (pick_m, zfwd_m, zback_m)):
        forward_z(pick, zfwd)
        backward_z(pick, zback)
    low_half = iota((5, LANES), 1) < 64
    for i in range(10):
        half_e[5 * i : 5 * i + 5, :] = jnp.where(low_half, pick_e[10 * i : 10 * i + 5, :], pick_e[10 * i + 5 : 10 * i + 10, :])
    half_e[50:55, :] = jnp.where((iota((5, LANES), 1) & 32) == 0, half_e[45:50, :], half_e[0:5, :])
    lxe[0:5, :] = jnp.where(low_half, eig_e[0:5, :], eig_e[5:10, :])

    second = (wide & 32) != 0
    lines = (1, 2, 3, 4, 5, 6, 7, 8, 10)
    both = [pltpu.roll(jnp.where(wide < 64, sides[0, n], sides[1, n]), 64, 1) for n in range(9)]
    for n, j in enumerate(lines):
        extra = win_e[at(9, j), :]
        win_e[at(0, j), :] = jnp.where(second, jnp.where(wide >= 64, sides[1, n], both[n]), extra)
        win_e[at(9, j), :] = jnp.where(second, extra, jnp.where(wide < 64, sides[0, n], both[n]))
    outer = [win_e[at(i, 10), :] for i in range(10)]
    last = [pltpu.roll(win_e[at(i, 8), :], 16, 1) for i in range(10)]
    first = [pltpu.roll(win_e[at(i, 1), :], 112, 1) for i in range(10)]
    for i in range(10):
        win_e[at(i, 0), :] = jnp.where(upper, last[i], outer[i])
        win_e[at(i, 9), :] = jnp.where(upper, outer[i], first[i])

    def scale(level, eig, b):
        return level + row(eig, 10 + b)

    x_forward(win_e, half_e, work_e, 5)
    for b in range(10):
        edge[b] = jnp.zeros((16, LANES), F32)

    def edge_step(a, _):
        y_forward([work_e[a, j] for j in range(10)], pick_e, tmp_a)
        level = row(lxe, a) + eig_e[20:36, :]
        weight = row(half_e, 50 + a)

        def add(b, value):
            edge[b] = edge[b] + weight * (value / scale(level, eig_e, b))

        through_z(tmp_a, zfwd_e, add)
        return 0

    lax.fori_loop(0, 5, edge_step, 0)
    for b in range(10):
        tmp_b[b] = edge[b] + pltpu.roll(edge[b], 64, 1)
    through_z(tmp_b, zback_e, into(tmp_c))
    y_back(tmp_c, pick_e, into(edge))

    inner = (wide >= 32) & (wide < 96)
    beyond = [jnp.where(inner, 0.0, jnp.where(wide < 32, win_e[at(8, j), :], win_e[at(1, j), :])) for j in range(10)]
    y_forward(beyond, pick_m, tmp_a)
    through_z(tmp_a, zfwd_m, into(late))
    lxe[0:16, :] = jnp.where(iota((16, LANES), 1) < 64, pick_m[0:16, :], pick_m[90:106, :])

    def main_step(a, _):
        level = row(eig_m, a) + eig_m[20:36, :]
        weight = row(lxe, a)
        for b in range(10):
            tmp_b[b] = (spec[a, b] + weight * late[b]) / scale(level, eig_m, b)
        through_z(tmp_b, zback_m, into(tmp_c))
        y_back(tmp_c, pick_m, into(work, a))
        return 0

    lax.fori_loop(0, 10, main_step, 0)

    for n, j in ((0, 0), (1, 9)):
        def put_end(i, main, n=n):
            ends[n, i - 1] = main

        x_back(work, edge, pick_m, j, put_end)
    for i in range(8):
        rim_rows[8 * i : 8 * i + 8, :] = jnp.where(upper[0:8], ends[1, i], ends[0, i])
    (parts,) = exchange([[rim_rows[pl.ds(k, 8, stride=8), :] for k in range(8)]])
    for r in range(8):
        rows_f[32 * (r % 2) + 8 * (r // 2) : 32 * (r % 2) + 8 * (r // 2) + 8, :] = parts[r]
    fine_ref[576:600, :] = four_ref[...]
    fine_ref[512:576, :] = join_rows(rows_f[0:64, :])
    inner = upper[0:8]

    def solve(j, _):
        def put(i, tile):
            tile = tile + jnp.where(inner & (j == 1), pltpu.roll(ends[1, i - 1], 16, 1), 0.0)
            tile = tile + jnp.where(inner | (j != 8), 0.0, pltpu.roll(ends[0, i - 1], 112, 1))
            tiles[pl.ds(pl.multiple_of(((i - 1) * 8 + j - 1) * 8, 8), 8), :] = tile

        x_back(work, edge, pick_m, j, put)
        return 0

    lax.fori_loop(1, 9, solve, 0, unroll=8)

    def step(n, _):
        columns = [8 * n + m for m in range(8)]
        groups = exchange([[tiles[pl.ds(i * 64 + k, 8, stride=8), :] for k in range(8)] for i in columns])
        for i, parts in zip(columns, groups, strict=True):
            for r in range(8):
                rows_ref[pl.ds(pl.multiple_of(128 * (r // 2) + 16 * i + 8 * (r % 2), 8), 8), :] = parts[r]
        return 0

    lax.fori_loop(0, 1, step, 0)
    fine_ref[0:512, :] = join_rows(rows_ref[...])
    copy.wait()


def x_back(work, edge, pick, j, put):
    sub, lane, kz = grids()
    wide = iota((16, LANES), 1)
    column = [work[a, j] for a in range(10)]
    first = dot_rows([(row(pick, a), column[a]) for a in range(10)])
    last = dot_rows([(row(pick, 90 + a), column[a]) for a in range(10)])
    side = edge[j]
    for i in range(1, 9):
        total = dot_rows([(row(pick, 10 * i + a), column[a]) for a in range(10)])
        if i == 1:
            total = total + jnp.where(wide >= 32, pltpu.roll(last, 32, 1), side)
        if i == 8:
            total = total + jnp.where(wide < 96, pltpu.roll(first, 96, 1), side)
        put(i, join_z(total, sub, kz))


def tree_kernel(got_ref, fine_ref, from_left, from_right, pay_ref):
    p = lax.axis_index("gx")
    q = lax.axis_index("gy")
    totals = []
    for n in range(2):
        bits = 2 + (2 * q + n) // 3
        total = jnp.zeros((1, LANES), F32)
        for t in range(64):
            inside = (t >> bits) == (p >> bits)
            total = total + jnp.where(inside, got_ref[t, :, LANES * n : LANES * (n + 1)], 0.0)
        totals.append(total)
    four = fine_ref[576:579, :] + jnp.where((p & 1) == 0, from_right[164:167, :], from_left[164:167, :])
    for peer in range(8):
        pay_ref[peer, 0:32, :] = jnp.where(peer < q, fine_ref[512:544, :], fine_ref[544:576, :])
        pay_ref[peer, 32:33, :] = totals[0]
        pay_ref[peer, 33:34, :] = totals[1]
        pay_ref[peer, 34:37, :] = four
        pay_ref[peer, 37:40, :] = jnp.zeros((3, LANES), F32)


def up_kernel(
    got_ref, top_ref, low_ref, fine_ref, out_ref, line_ref, coeff_ref, sums_ref, vertex_ref
):
    q = lax.axis_index("gy")
    line_ref[...] = jnp.zeros((32, LANES), F32)
    line_ref[0:2, :] = fine_ref[582:584, :]
    line_ref[2:5, :] = fine_ref[579:582, :]
    line_ref[5:8, :] = got_ref[7, 34:37, :]
    for peer in range(8):
        line_ref[8 + 2 * peer : 10 + 2 * peer, :] = got_ref[peer, 32:34, :]
    here = pltpu.roll(line_ref[0:24], 127, 1)
    after = pltpu.roll(line_ref[1:25], 127, 1)
    coeff_ref[...] = jnp.where(iota((24, LANES), 1) == 127, after, here)
    weights = [jnp.broadcast_to(coeff_ref[c : c + 1, :width], (8, width)) for c, (_, width) in enumerate(CUTS)]

    def product(ref, first, place, count):
        total = ref[place, CUTS[0][0]] * weights[0][:count]
        for weight, (cut, _) in zip(weights[1:22], CUTS[1:22], strict=True):
            total = total + ref[place, cut] * weight[:count]
        end = ref[place, CUTS[22][0]] * weights[22][:count]
        sums_ref[pl.ds(first, count), :] = total
        sums_ref[pl.ds(first, count), 0:127] = total[:, 0:127] + end

    def step(g, _):
        first = pl.multiple_of(8 * g, 8)
        product(top_ref, first, pl.ds(first, 8), 8)
        return 0

    lax.fori_loop(0, TOP // 8, step, 0, unroll=TOP // 16)
    for low in range(0, 248 - TOP, 8):
        product(low_ref, TOP + low, pl.ds(low, 8), 8)
    product(low_ref, 248, pl.ds(248 - TOP, 7), 7)
    sums_ref[255:256, :] = jnp.zeros((1, LANES), F32)
    values = jnp.broadcast_to(jnp.sum(sums_ref[...], axis=1, keepdims=True), (256, 17))
    vertex_ref[...] = jnp.zeros((16, LANES), F32)
    rows = iota((256, 17), 0).astype(F32)
    for i in range(5):
        for j in range(3):
            k = 3 * i + j
            vertex_ref[k : k + 1, 0:17] = jnp.sum(
                jnp.where(fine_ref[584 + k : 585 + k, 0:17] == rows, values, 0.0), axis=0, keepdims=True
            )
    depth = hat(iota((LANES, LANES), 1), iota((LANES, LANES), 0)).astype(jnp.bfloat16)
    vertex_ref[...] = moved(vertex_ref[...], depth)
    rise = (2.0 * iota((8, LANES), 0).astype(F32) + 1.0) / 16.0
    planes = []
    for i in range(5):
        three = [jnp.broadcast_to(vertex_ref[3 * i + j : 3 * i + j + 1, :], (8, LANES)) for j in range(3)]
        planes.append([three[jy] * (1.0 - rise) + three[jy + 1] * rise for jy in range(2)])
    faces = (
        jnp.where(q > 0, got_ref[jnp.maximum(q - 1, 0), 0:32, :], 0.0),
        jnp.where(q < 7, got_ref[jnp.minimum(q + 1, 7), 0:32, :], 0.0),
    )
    edges = (iota((8, LANES), 0) == 0, iota((8, LANES), 0) == 7)
    for ix in range(4):
        for i in range(8):
            x = 8 * ix + i
            far = (2 * i + 1) / 16.0
            for jy in range(2):
                place = slice(16 * x + 8 * jy, 16 * x + 8 * jy + 8)
                value = fine_ref[place, :] + planes[ix][jy] * (1.0 - far) + planes[ix + 1][jy] * far
                out_ref[place, :] = value + jnp.where(edges[jy], faces[jy][x : x + 1, :], 0.0)


VM = pltpu.VMEM
ANYWHERE = None


def call(kernel, outs, scratch=(), ins=None, sems=0, cost=0, limit=24, aliases=None):
    shapes = [
        jax.ShapeDtypeStruct(o[0], o[2] if len(o) > 2 else F32) if o[1] is None else o[1](o[0], o[2] if len(o) > 2 else F32)
        for o in outs
    ]
    spaces = [pltpu.VMEM(s, F32) if isinstance(s, tuple) else s for s in scratch]
    if sems:
        spaces.append(pltpu.SemaphoreType.DMA((sems,)))
    run = pl.pallas_call(
        kernel,
        out_shape=shapes,
        in_specs=[pl.BlockSpec(memory_space=m or pltpu.VMEM) for m in ins],
        out_specs=[pl.BlockSpec(memory_space=pltpu.VMEM) for _ in outs],
        scratch_shapes=spaces,
        input_output_aliases=aliases or {},
        compiler_params=pltpu.CompilerParams(vmem_limit_bytes=limit << 20),
        cost_estimate=pl.CostEstimate(flops=cost, bytes_accessed=cost // 400, transcendentals=0),
    )

    def apply(*operands):
        held = [x if m is None else pltpu.with_memory_space_constraint(x, m) for x, m in zip(operands, ins, strict=True)]
        return run(*held)

    return apply


def spread_to(block, axis):
    return lax.all_to_all(block, axis, 0, 0, tiled=True)


def shards(residual, elem_class, basis, eigenvalues, vertex_number, panels):
    field = residual.reshape(512, LANES)
    I32 = jnp.int32
    pay, own, cls, top, res, table, eigen = call(
        down_kernel,
        [
            ((8, 40, 128), VM), ((40, 128), VM), ((4, 2, 16), VM, I32), ((TOP, 2943), VM),
            ((512, 128), VM), ((8, 300), VM), ((8, 30), VM),
        ],
        [(40, 128), (3, 10, 8, 10), (3, 8, 10), (255 - TOP, 2943), VM((5, 3, 17), I32)], ins=[pltpu.HBM] * 6, sems=7,
    )(field, vertex_number, panels, elem_class, basis.transpose(1, 2, 0, 3), eigenvalues.transpose(1, 0, 2))
    first = spread_to(pay, "gy")
    tree, four = call(sum_kernel, [((64, 1, 256), VM), ((24, 128), VM)], ins=[None, VM])(first, own)
    summed = spread_to(tree, "gx")
    right, left, face = call(
        pack_kernel, [((168, 128), VM), ((168, 128), VM), ((64, 128), VM)], ins=[None, VM, VM, VM], cost=2_000_000_000
    )(first, res, cls, four)
    from_left = lax.ppermute(right, "gx", [(i, i + 1) for i in range(63)])
    from_right = lax.ppermute(left, "gx", [(i + 1, i) for i in range(63)])
    spec, sides, pick, eig, table_out = call(
        spectral_kernel,
        [
            ((10, 10, 16, 128), VM), ((2, 9, 16, 128), VM), ((304, 128), VM), ((40, 128), VM), ((8, 300), VM),
        ],
        [(10, 16, 128), (512, 128), (64, 128), (1760, 128), (10, 10, 16, 128), (10, 16, 128)], ins=[VM] * 5, cost=2_000_000_000,
    )(res, face, cls, table, eigen)
    fine, low = call(
        solve_kernel,
        [((600, 128), VM), ((255 - TOP, 2943), VM)],
        [
            (10, 10, 16, 128), (10, 16, 128), (2, 8, 8, 128), (512, 128), (512, 128),
            (64, 128), (288, 128), (1760, 128), (304, 128), (40, 128), (10, 16, 128), (10, 16, 128), (10, 16, 128), (10, 16, 128),
            (56, 128), (16, 128), (5, 10, 16, 128), (10, 16, 128), (10, 16, 128), (10, 16, 128), (64, 128), (10, 16, 128),
        ],
        ins=[VM] * 7 + [None, None, pltpu.HBM], sems=1, cost=1_000_000_000,
    )(spec, sides, table_out, eigen, pick, eig, four, from_left, from_right, panels)
    (pay,) = call(tree_kernel, [((8, 40, 128), VM)], ins=[None, VM, None, None])(summed, fine, from_left, from_right)
    second = spread_to(pay, "gy")
    (out,) = call(
        up_kernel, [((512, 128), None)], [(32, 128), (24, 128), (256, 128), (16, 128)], ins=[None, VM, VM, VM]
    )(second, top, low, fine)
    return out.reshape(residual.shape)


def solution(mesh):
    return jax.shard_map(
        shards,
        mesh=mesh,
        in_specs=(
            P(None, "gx", "gy", None),
            P("gx", "gy", None),
            P(),
            P(),
            P("gx", "gy", None),
            P("gx", "gy"),
        ),
        out_specs=P(None, "gx", "gy", None),
        check_vma=False,
    )
```

```python
import functools

import jax
import jax.numpy as jnp
from jax import lax
from jax.experimental import pallas as pl
from jax.experimental.pallas import tpu as pltpu
from jax.sharding import PartitionSpec as P

NPR = 8
NEXT = 10
NCLASS = 8
LANES = 128
TOP = 208
CUTS = [(slice(low, min(low + 128, 2943)), min(128, 2943 - low)) for low in range(0, 2943, 128)]
HALO = NPR + 1
F32 = jnp.float32
exact = lax.Precision.HIGHEST
ORDER = (1, 2, 3, 4, 5, 6, 7, 8, 0, 9)


def iota(shape, axis):
    return lax.broadcasted_iota(jnp.int32, shape, axis)


def hat(point, vertex):
    place = (point.astype(F32) + 0.5) / NPR
    return jnp.maximum(0.0, 1.0 - jnp.abs(place - vertex.astype(F32)))


def moved(rows, table):
    high = rows.astype(jnp.bfloat16)
    rest = rows - high.astype(F32)
    middle = rest.astype(jnp.bfloat16)
    low = (rest - middle.astype(F32)).astype(jnp.bfloat16)
    total = jnp.dot(low, table, preferred_element_type=F32)
    total = total + jnp.dot(middle, table, preferred_element_type=F32)
    return total + jnp.dot(high, table, preferred_element_type=F32)


def plane_hat(point, vertex):
    third = (vertex.astype(F32) + 0.5) / 3.0
    big = third.astype(jnp.int32)
    return hat(point >> 4, big) * hat(point & 15, vertex - 3 * big)


def down_kernel(
    res_hbm, num_hbm, pan_hbm, cls_hbm, basis_hbm, value_hbm,
    pay_ref, own_ref, cls_ref, top_ref, res_ref, table_ref, eigen_ref,
    line_ref, basis_ref, value_ref, low_ref, num_ref, sems,
):
    q = lax.axis_index("gy")
    pairs = [
        (res_hbm, res_ref), (num_hbm, num_ref), (cls_hbm, cls_ref), (basis_hbm, basis_ref), (value_hbm, value_ref),
        (pan_hbm.at[pl.ds(0, TOP), :], top_ref), (pan_hbm.at[pl.ds(TOP, 255 - TOP), :], low_ref),
    ]
    copies = [pltpu.make_async_copy(source, target, sems.at[n]) for n, (source, target) in enumerate(pairs)]
    for copy in copies:
        copy.start()
    plane = plane_hat(iota((16, 512), 1), iota((16, 512), 0))
    depth = hat(iota((128, 17), 0), iota((128, 17), 1))
    line_ref[...] = jnp.zeros((40, LANES), F32)
    copies[0].wait()
    half = jnp.dot(plane, res_ref[...], precision=exact)
    vertex = jnp.dot(half, depth, precision=exact)
    low_face = res_ref[pl.ds(0, 32, stride=16), :]
    high_face = res_ref[pl.ds(15, 32, stride=16), :]
    for peer in range(8):
        pay_ref[peer, 0:32, :] = jnp.where(peer < q, low_face, high_face)
    copies[1].wait()
    rows = iota((256, 17), 0)
    spread = jnp.zeros((256, 17), F32)
    for i in range(5):
        for j in range(3):
            k = 3 * i + j
            spread = spread + jnp.where(num_ref[i, j : j + 1, :] == rows, vertex[k : k + 1, :], 0.0)
    ordered = jnp.broadcast_to(jnp.sum(spread, axis=1, keepdims=True), (256, LANES))

    for copy in copies[2:5]:
        copy.wait()
    for d in range(3):
        eigen_ref[:, 10 * d : 10 * d + 10] = value_ref[d]
        for i in range(10):
            low = 100 * d + 10 * i
            table_ref[:, low : low + 10] = basis_ref[d, i]
    own_ref[24:40, :] = jnp.zeros((16, LANES), F32)
    for i in range(5):
        own_ref[24 + 3 * i : 27 + 3 * i, 0:17] = num_ref[i].astype(F32)
    copies[5].wait()
    for c, (cut, width) in enumerate(CUTS):
        line_ref[8 + c : 9 + c, :width] = jnp.sum(top_ref[:, cut] * ordered[:TOP, :width], axis=0, keepdims=True)
    copies[6].wait()
    for c, (cut, width) in enumerate(CUTS):
        piece = jnp.sum(low_ref[:, cut] * ordered[TOP:255, :width], axis=0, keepdims=True)
        line_ref[8 + c : 9 + c, :width] = line_ref[8 + c : 9 + c, :width] + piece
    here = pltpu.roll(line_ref[8:32], 1, 1)
    before = pltpu.roll(line_ref[7:31], 1, 1)
    own_ref[0:24, :] = jnp.where(iota((24, LANES), 1) == 0, before, here)
    for peer in range(8):
        pay_ref[peer, 32:35, :] = own_ref[2:5, :]
        pay_ref[peer, 35:37, :] = own_ref[8 + 2 * peer : 10 + 2 * peer, :]
        pay_ref[peer, 37:40, :] = own_ref[5:8, :] if peer == 7 else jnp.zeros((3, LANES), F32)


def sum_kernel(got_ref, own_ref, tree_ref, four_ref):
    q = lax.axis_index("gy")
    total = got_ref[0, 35:40, :]
    for peer in range(1, 8):
        total = total + got_ref[peer, 35:40, :]
    four_ref[0:3, :] = total[2:5]
    four_ref[6:8, :] = own_ref[0:2, :]
    four_ref[8:24, :] = own_ref[24:40, :]
    for level in range(1, 4):
        low = jnp.zeros((1, LANES), F32)
        for peer in range(8):
            inside = (peer >> level) == (q >> level)
            low = low + jnp.where(inside, got_ref[peer, 31 + level : 32 + level, :], 0.0)
        four_ref[2 + level : 3 + level, :] = low
    line = jnp.concatenate([total[0:1], total[1:2]], axis=1)
    for t in range(64):
        tree_ref[t] = line


def pack_kernel(got_ref, res_ref, cls_ref, four_ref, right_ref, left_ref, face_ref):
    q = lax.axis_index("gy")
    face_ref[0:32, :] = jnp.where(q > 0, got_ref[jnp.maximum(q - 1, 0), 0:32, :], 0.0)
    face_ref[32:64, :] = jnp.where(q < 7, got_ref[jnp.minimum(q + 1, 7), 0:32, :], 0.0)
    for ref, column, first in ((right_ref, 3, 23), (left_ref, 0, 0)):
        ref[0:144, :] = res_ref[16 * first : 16 * first + 144, :]
        ref[144:153, :] = face_ref[first : first + 9, :]
        ref[153:162, :] = face_ref[32 + first : 41 + first, :]
        ref[162:168, :] = jnp.zeros((6, LANES), F32)
        ref[162:164, 0:16] = (cls_ref[column] + 1).astype(F32)
        ref[164:167, :] = four_ref[0:3, :]


def grids():
    sub = iota((8, LANES), 0)
    lane = iota((8, LANES), 1)
    return sub, lane, lane & 15


def split_z(rows):
    lane = iota((LANES, LANES), 1)
    return moved(rows, (iota((LANES, LANES), 0) == (((lane & 15) << 3) | (lane >> 4))).astype(jnp.bfloat16))


def join_rows(rows):
    lane = iota((LANES, LANES), 0)
    return moved(rows, (iota((LANES, LANES), 1) == (((lane & 15) << 3) | (lane >> 4))).astype(jnp.bfloat16))


def exchange(groups):
    lane = iota((8, LANES), 1)
    groups = [list(parts) for parts in groups]
    for bit in (4, 2, 1):
        inside = (lane & (16 * bit)) != 0
        for parts in groups:
            for n in range(8):
                if n & bit:
                    continue
                low, high = parts[n], parts[n | bit]
                if bit == 4:
                    swap = pltpu.roll(jnp.where(inside, low, high), 64, 1)
                    parts[n] = jnp.where(inside, swap, low)
                    parts[n | bit] = jnp.where(inside, high, swap)
                else:
                    parts[n] = jnp.where(inside, pltpu.roll(high, 16 * bit, 1), low)
                    parts[n | bit] = jnp.where(inside, high, pltpu.roll(low, LANES - 16 * bit, 1))
    return groups


def with_outer(groups):
    kz = iota((8, LANES), 1) & 15
    before = [jnp.where(kz == 0, 0.0, pltpu.roll(parts[7], 1, 1)) for parts in groups]
    after = [jnp.where(kz == 15, 0.0, pltpu.roll(parts[0], 127, 1)) for parts in groups]
    return [parts + [b, a] for parts, b, a in zip(groups, before, after, strict=True)]


def at(i, j):
    return pl.ds(pl.multiple_of((i * 11 + j) * 16, 16), 16)


def join_z(total, sub, kz):
    main = total[0:8]
    tail = pltpu.roll(total[8:16], 7, 0)
    return main + jnp.where(
        sub == 7,
        jnp.where(kz == 15, 0.0, pltpu.roll(tail, 127, 1)),
        jnp.where((sub == 0) & (kz != 0), pltpu.roll(tail, 1, 1), 0.0),
    )


def row(ref, n):
    return jnp.broadcast_to(ref[pl.ds(n, 1), :], (16, LANES))


def dot_rows(pairs):
    total = None
    for a, b in pairs:
        total = a * b if total is None else total + a * b
    return total


def chosen(table, onehot):
    high = table.astype(jnp.bfloat16)
    rest = table - high.astype(F32)
    middle = rest.astype(jnp.bfloat16)
    low = (rest - middle.astype(F32)).astype(jnp.bfloat16)
    dims = (((0,), (0,)), ((), ()))
    total = lax.dot_general(low, onehot, dims, preferred_element_type=F32)
    total = total + lax.dot_general(middle, onehot, dims, preferred_element_type=F32)
    return total + lax.dot_general(high, onehot, dims, preferred_element_type=F32)


def pick_tables(kind, table_ref, eigen_ref, pick, eig):
    group = iota((8, LANES), 0)
    lane = iota((8, LANES), 1)
    spread = (iota((16, LANES), 0) == (iota((16, LANES), 1) & 15)).astype(F32)
    laid = jnp.dot(kind, spread, precision=exact)
    laid = jnp.sum(jnp.where(group == (lane >> 4), laid, 0.0), axis=0, keepdims=True)
    onehot = (laid == (group + 1).astype(F32)).astype(jnp.bfloat16)
    pick[0:300, :] = chosen(table_ref[:, 0:300], onehot)
    eig[0:30, :] = chosen(eigen_ref[:, 0:30], onehot)
    eig[20:30, :] = eig[20:30, :] + jnp.where(laid == 0.0, 1.0, 0.0)
    eig[30:40, :] = jnp.ones((10, LANES), F32)


def forward_z(pick, zfwd):
    for n, k in enumerate(ORDER):
        zfwd[n, 0:10, :] = pick[200 + 10 * k : 210 + 10 * k, :]
        zfwd[n, 10:16, :] = jnp.zeros((6, LANES), F32)


def backward_z(pick, zback):
    for c in range(10):
        zback[c, 0:8, :] = pick[pl.ds(210 + c, 8, stride=10), :]
        zback[c, 8:16, :] = jnp.zeros((8, LANES), F32)
        zback[c, 8:9, :] = pick[200 + c : 201 + c, :]
        zback[c, 9:10, :] = pick[290 + c : 291 + c, :]


def x_forward(win, table, target, count):
    def step(j, _):
        column = [win[at(i, j), :] for i in range(10)]
        for a in range(count):
            target[a, j] = dot_rows([(row(table, count * i + a), column[i]) for i in range(10)])
        return 0

    lax.fori_loop(0, 10, step, 0, unroll=2)


def through_z(source, zfwd, store):
    table = [zfwd[k] for k in range(10)]
    for b in range(10):
        store(b, dot_rows([(table[k], jnp.broadcast_to(source[b, k : k + 1, :], (16, LANES))) for k in range(10)]))


def y_forward(column, pick, target):
    for b in range(10):
        target[b] = dot_rows([(row(pick, 100 + 10 * j + b), column[j]) for j in range(10)])


def y_back(source, pick, store):
    column = [source[b] for b in range(10)]
    for j in range(10):
        store(j, dot_rows([(row(pick, 100 + 10 * j + b), column[b]) for b in range(10)]))


def into(ref, *place):
    def store(n, value):
        ref[(*place, n)] = value

    return store


def spectral_kernel(
    res_ref, face_ref, cls_ref, table_ref, eigen_ref,
    spec, sides, pick, eig, table_out,
    zfwd, rows_ref, rows_f, win, work, tmp,
):
    wide = iota((16, LANES), 1)
    upper = (wide & 16) != 0
    rows_ref[...] = split_z(res_ref[...])
    rows_f[...] = split_z(face_ref[...])
    kind = jnp.concatenate([cls_ref[ix].astype(F32) + 1.0 for ix in range(4)], axis=0)
    table_out[...] = table_ref[...]
    pick_tables(kind, table_ref, eigen_ref, pick, eig)
    forward_z(pick, zfwd)
    columns = range(8)
    groups = [
        [rows_ref[128 * (r // 2) + 16 * i + 8 * (r % 2) : 128 * (r // 2) + 16 * i + 8 * (r % 2) + 8, :] for r in range(8)]
        for i in columns
    ]
    groups.append([rows_f[32 * (r % 2) + 8 * (r // 2) : 32 * (r % 2) + 8 * (r // 2) + 8, :] for r in range(8)])
    groups = with_outer(exchange(groups))
    for k in range(10):
        win[pl.ds(21 * 16 + k, 8, stride=176), :] = groups[8][k]
    for i in columns:
        for k, part in enumerate(groups[i]):
            win[pl.ds((i * 11 + 12) * 16 + k, 8, stride=16), :] = part
    lines = (1, 2, 3, 4, 5, 6, 7, 8, 10)
    ahead = [win[at(8, j), :] for j in lines]
    back = [win[at(1, j), :] for j in lines]
    for n, j in enumerate(lines):
        sides[0, n] = back[n]
        sides[1, n] = ahead[n]
        win[at(0, j), :] = jnp.where(wide >= 32, pltpu.roll(ahead[n], 32, 1), 0.0)
        win[at(9, j), :] = jnp.where(wide < 96, pltpu.roll(back[n], 96, 1), 0.0)

    def y_halo(n, _):
        columns = [5 * n + m for m in range(5)]
        outer = [win[at(i, 10), :] for i in columns]
        last = [pltpu.roll(win[at(i, 8), :], 16, 1) for i in columns]
        first = [pltpu.roll(win[at(i, 1), :], 112, 1) for i in columns]
        for m, i in enumerate(columns):
            win[at(i, 0), :] = jnp.where(upper, last[m], outer[m])
            win[at(i, 9), :] = jnp.where(upper, outer[m], first[m])
        return 0

    lax.fori_loop(0, 2, y_halo, 0)
    x_forward(win, pick, work, 10)

    def step(a, _):
        y_forward([work[a, j] for j in range(10)], pick, tmp)
        through_z(tmp, zfwd, into(spec, a))
        return 0

    lax.fori_loop(0, 10, step, 0, unroll=2)


def solve_kernel(
    spec, sides, table_ref, eigen_ref, pick_m, eig_m, four_ref, from_left, from_right, pan_hbm,
    fine_ref, low_ref,
    work, edge, ends, tiles, rows_ref, rows_f, rows_e, win_e, pick_e, eig_e, zfwd_e, zback_e, zfwd_m, zback_m,
    half_e, lxe, work_e, tmp_a, tmp_b, tmp_c, rim_rows, late, sems,
):
    copy = pltpu.make_async_copy(pan_hbm.at[pl.ds(TOP, 255 - TOP), :], low_ref, sems.at[0])
    copy.start()
    sub, lane, kz = grids()
    wide = iota((16, LANES), 1)
    upper = (wide & 16) != 0

    rows_f[0:24, :] = from_left[144:168, :]
    rows_f[24:48, :] = from_right[144:168, :]
    rows_f[0:48, :] = split_z(rows_f[0:48, :])
    rows_e[0:144, :] = from_left[0:144, :]
    rows_e[144:288, :] = from_right[0:144, :]
    rows_e[...] = split_z(rows_e[...])
    beside = [rows_f[first : first + 8, :] for first in (1, 10, 24, 33)]
    corner = [jnp.broadcast_to(rows_f[n : n + 1, :], (8, LANES)) for n in (0, 9, 32, 41)]
    beside, corner = with_outer(exchange([beside + beside, corner + corner]))
    for k in range(10):
        win_e[pl.ds(21 * 16 + k, 8, stride=176), :] = beside[k]
        win_e[109 * 16 + k : 109 * 16 + k + 1, :] = corner[k][0:1]

    def fill(n, _):
        columns = [9 * n + m for m in range(9)]
        groups = []
        for i in columns:
            layer = jnp.where(i == 8, 0, i + 1)
            parts = [rows_e[pl.ds(pl.multiple_of(16 * layer + 8 * jy, 8), 8), :] for jy in range(2)]
            parts += [rows_e[pl.ds(pl.multiple_of(144 + 16 * i + 8 * jy, 8), 8), :] for jy in range(2)]
            groups.append(parts + parts)
        for i, parts in zip(columns, with_outer(exchange(groups)), strict=True):
            for k, part in enumerate(parts):
                win_e[pl.ds((i * 11 + 12) * 16 + k, 8, stride=16), :] = part
        return 0

    lax.fori_loop(0, 1, fill, 0)

    near = [from_left[162:164, 0:16], from_right[162:164, 0:16]]
    pick_tables(jnp.concatenate(near + near, axis=0), table_ref, eigen_ref, pick_e, eig_e)
    for pick, zfwd, zback in ((pick_e, zfwd_e, zback_e), (pick_m, zfwd_m, zback_m)):
        forward_z(pick, zfwd)
        backward_z(pick, zback)
    low_half = iota((5, LANES), 1) < 64
    for i in range(10):
        half_e[5 * i : 5 * i + 5, :] = jnp.where(low_half, pick_e[10 * i : 10 * i + 5, :], pick_e[10 * i + 5 : 10 * i + 10, :])
    half_e[50:55, :] = jnp.where((iota((5, LANES), 1) & 32) == 0, half_e[45:50, :], half_e[0:5, :])
    lxe[0:5, :] = jnp.where(low_half, eig_e[0:5, :], eig_e[5:10, :])

    second = (wide & 32) != 0
    lines = (1, 2, 3, 4, 5, 6, 7, 8, 10)
    both = [pltpu.roll(jnp.where(wide < 64, sides[0, n], sides[1, n]), 64, 1) for n in range(9)]
    for n, j in enumerate(lines):
        extra = win_e[at(9, j), :]
        win_e[at(0, j), :] = jnp.where(second, jnp.where(wide >= 64, sides[1, n], both[n]), extra)
        win_e[at(9, j), :] = jnp.where(second, extra, jnp.where(wide < 64, sides[0, n], both[n]))
    outer = [win_e[at(i, 10), :] for i in range(10)]
    last = [pltpu.roll(win_e[at(i, 8), :], 16, 1) for i in range(10)]
    first = [pltpu.roll(win_e[at(i, 1), :], 112, 1) for i in range(10)]
    for i in range(10):
        win_e[at(i, 0), :] = jnp.where(upper, last[i], outer[i])
        win_e[at(i, 9), :] = jnp.where(upper, outer[i], first[i])

    def scale(level, eig, b):
        return level + row(eig, 10 + b)

    x_forward(win_e, half_e, work_e, 5)
    for b in range(10):
        edge[b] = jnp.zeros((16, LANES), F32)

    def edge_step(a, _):
        y_forward([work_e[a, j] for j in range(10)], pick_e, tmp_a)
        level = row(lxe, a) + eig_e[20:36, :]
        weight = row(half_e, 50 + a)

        def add(b, value):
            edge[b] = edge[b] + weight * (value / scale(level, eig_e, b))

        through_z(tmp_a, zfwd_e, add)
        return 0

    lax.fori_loop(0, 5, edge_step, 0)
    for b in range(10):
        tmp_b[b] = edge[b] + pltpu.roll(edge[b], 64, 1)
    through_z(tmp_b, zback_e, into(tmp_c))
    y_back(tmp_c, pick_e, into(edge))

    inner = (wide >= 32) & (wide < 96)
    beyond = [jnp.where(inner, 0.0, jnp.where(wide < 32, win_e[at(8, j), :], win_e[at(1, j), :])) for j in range(10)]
    y_forward(beyond, pick_m, tmp_a)
    through_z(tmp_a, zfwd_m, into(late))
    lxe[0:16, :] = jnp.where(iota((16, LANES), 1) < 64, pick_m[0:16, :], pick_m[90:106, :])

    def main_step(a, _):
        level = row(eig_m, a) + eig_m[20:36, :]
        weight = row(lxe, a)
        for b in range(10):
            tmp_b[b] = (spec[a, b] + weight * late[b]) / scale(level, eig_m, b)
        through_z(tmp_b, zback_m, into(tmp_c))
        y_back(tmp_c, pick_m, into(work, a))
        return 0

    lax.fori_loop(0, 10, main_step, 0)

    for n, j in ((0, 0), (1, 9)):
        def put_end(i, main, n=n):
            ends[n, i - 1] = main

        x_back(work, edge, pick_m, j, put_end)
    for i in range(8):
        rim_rows[8 * i : 8 * i + 8, :] = jnp.where(upper[0:8], ends[1, i], ends[0, i])
    (parts,) = exchange([[rim_rows[pl.ds(k, 8, stride=8), :] for k in range(8)]])
    for r in range(8):
        rows_f[32 * (r % 2) + 8 * (r // 2) : 32 * (r % 2) + 8 * (r // 2) + 8, :] = parts[r]
    fine_ref[576:600, :] = four_ref[...]
    even = lax.axis_index("gx") % 2 == 0
    fine_ref[576:579, :] = four_ref[0:3, :] + jnp.where(even, from_right[164:167, :], from_left[164:167, :])
    fine_ref[512:576, :] = join_rows(rows_f[0:64, :])
    inner = upper[0:8]

    def solve(j, _):
        def put(i, tile):
            tile = tile + jnp.where(inner & (j == 1), pltpu.roll(ends[1, i - 1], 16, 1), 0.0)
            tile = tile + jnp.where(inner | (j != 8), 0.0, pltpu.roll(ends[0, i - 1], 112, 1))
            tiles[pl.ds(pl.multiple_of(((i - 1) * 8 + j - 1) * 8, 8), 8), :] = tile

        x_back(work, edge, pick_m, j, put)
        return 0

    lax.fori_loop(1, 9, solve, 0, unroll=8)

    def step(n, _):
        columns = [8 * n + m for m in range(8)]
        groups = exchange([[tiles[pl.ds(i * 64 + k, 8, stride=8), :] for k in range(8)] for i in columns])
        for i, parts in zip(columns, groups, strict=True):
            for r in range(8):
                rows_ref[pl.ds(pl.multiple_of(128 * (r // 2) + 16 * i + 8 * (r % 2), 8), 8), :] = parts[r]
        return 0

    lax.fori_loop(0, 1, step, 0)
    fine_ref[0:512, :] = join_rows(rows_ref[...])
    copy.wait()


def x_back(work, edge, pick, j, put):
    sub, lane, kz = grids()
    wide = iota((16, LANES), 1)
    column = [work[a, j] for a in range(10)]
    first = dot_rows([(row(pick, a), column[a]) for a in range(10)])
    last = dot_rows([(row(pick, 90 + a), column[a]) for a in range(10)])
    side = edge[j]
    for i in range(1, 9):
        total = dot_rows([(row(pick, 10 * i + a), column[a]) for a in range(10)])
        if i == 1:
            total = total + jnp.where(wide >= 32, pltpu.roll(last, 32, 1), side)
        if i == 8:
            total = total + jnp.where(wide < 96, pltpu.roll(first, 96, 1), side)
        put(i, join_z(total, sub, kz))


def tree_kernel(got_ref, fine_ref, pay_ref):
    p = lax.axis_index("gx")
    q = lax.axis_index("gy")
    totals = []
    for n in range(2):
        bits = 2 + (2 * q + n) // 3
        total = jnp.zeros((1, LANES), F32)
        for t in range(64):
            inside = (t >> bits) == (p >> bits)
            total = total + jnp.where(inside, got_ref[t, :, LANES * n : LANES * (n + 1)], 0.0)
        totals.append(total)
    four = fine_ref[576:579, :]
    for peer in range(8):
        pay_ref[peer, 0:32, :] = jnp.where(peer < q, fine_ref[512:544, :], fine_ref[544:576, :])
        pay_ref[peer, 32:33, :] = totals[0]
        pay_ref[peer, 33:34, :] = totals[1]
        pay_ref[peer, 34:37, :] = four
        pay_ref[peer, 37:40, :] = jnp.zeros((3, LANES), F32)


def up_kernel(
    got_ref, top_ref, low_ref, fine_ref, out_ref, line_ref, coeff_ref, sums_ref, vertex_ref
):
    q = lax.axis_index("gy")
    line_ref[...] = jnp.zeros((32, LANES), F32)
    line_ref[0:2, :] = fine_ref[582:584, :]
    line_ref[2:5, :] = fine_ref[579:582, :]
    line_ref[5:8, :] = got_ref[7, 34:37, :]
    for peer in range(8):
        line_ref[8 + 2 * peer : 10 + 2 * peer, :] = got_ref[peer, 32:34, :]
    here = pltpu.roll(line_ref[0:24], 127, 1)
    after = pltpu.roll(line_ref[1:25], 127, 1)
    coeff_ref[...] = jnp.where(iota((24, LANES), 1) == 127, after, here)
    weights = [jnp.broadcast_to(coeff_ref[c : c + 1, :width], (8, width)) for c, (_, width) in enumerate(CUTS)]

    def product(ref, first, place, count):
        total = ref[place, CUTS[0][0]] * weights[0][:count]
        for weight, (cut, _) in zip(weights[1:22], CUTS[1:22], strict=True):
            total = total + ref[place, cut] * weight[:count]
        end = ref[place, CUTS[22][0]] * weights[22][:count]
        sums_ref[pl.ds(first, count), :] = total
        sums_ref[pl.ds(first, count), 0:127] = total[:, 0:127] + end

    def step(g, _):
        first = pl.multiple_of(8 * g, 8)
        product(top_ref, first, pl.ds(first, 8), 8)
        return 0

    lax.fori_loop(0, TOP // 8, step, 0, unroll=TOP // 16)
    for low in range(0, 248 - TOP, 8):
        product(low_ref, TOP + low, pl.ds(low, 8), 8)
    product(low_ref, 248, pl.ds(248 - TOP, 7), 7)
    sums_ref[255:256, :] = jnp.zeros((1, LANES), F32)
    values = jnp.broadcast_to(jnp.sum(sums_ref[...], axis=1, keepdims=True), (256, 17))
    vertex_ref[...] = jnp.zeros((16, LANES), F32)
    rows = iota((256, 17), 0).astype(F32)
    for i in range(5):
        for j in range(3):
            k = 3 * i + j
            vertex_ref[k : k + 1, 0:17] = jnp.sum(
                jnp.where(fine_ref[584 + k : 585 + k, 0:17] == rows, values, 0.0), axis=0, keepdims=True
            )
    depth = hat(iota((LANES, LANES), 1), iota((LANES, LANES), 0)).astype(jnp.bfloat16)
    vertex_ref[...] = moved(vertex_ref[...], depth)
    rise = (2.0 * iota((8, LANES), 0).astype(F32) + 1.0) / 16.0
    planes = []
    for i in range(5):
        three = [jnp.broadcast_to(vertex_ref[3 * i + j : 3 * i + j + 1, :], (8, LANES)) for j in range(3)]
        planes.append([three[jy] * (1.0 - rise) + three[jy + 1] * rise for jy in range(2)])
    faces = (
        jnp.where(q > 0, got_ref[jnp.maximum(q - 1, 0), 0:32, :], 0.0),
        jnp.where(q < 7, got_ref[jnp.minimum(q + 1, 7), 0:32, :], 0.0),
    )
    edges = (iota((8, LANES), 0) == 0, iota((8, LANES), 0) == 7)
    for ix in range(4):
        for i in range(8):
            x = 8 * ix + i
            far = (2 * i + 1) / 16.0
            for jy in range(2):
                place = slice(16 * x + 8 * jy, 16 * x + 8 * jy + 8)
                value = fine_ref[place, :] + planes[ix][jy] * (1.0 - far) + planes[ix + 1][jy] * far
                out_ref[place, :] = value + jnp.where(edges[jy], faces[jy][x : x + 1, :], 0.0)


VM = pltpu.VMEM
ANYWHERE = None


def call(kernel, outs, scratch=(), ins=None, sems=0, cost=0, limit=24, aliases=None):
    shapes = [
        jax.ShapeDtypeStruct(o[0], o[2] if len(o) > 2 else F32) if o[1] is None else o[1](o[0], o[2] if len(o) > 2 else F32)
        for o in outs
    ]
    spaces = [pltpu.VMEM(s, F32) if isinstance(s, tuple) else s for s in scratch]
    if sems:
        spaces.append(pltpu.SemaphoreType.DMA((sems,)))
    run = pl.pallas_call(
        kernel,
        out_shape=shapes,
        in_specs=[pl.BlockSpec(memory_space=m or pltpu.VMEM) for m in ins],
        out_specs=[pl.BlockSpec(memory_space=pltpu.VMEM) for _ in outs],
        scratch_shapes=spaces,
        input_output_aliases=aliases or {},
        compiler_params=pltpu.CompilerParams(vmem_limit_bytes=limit << 20),
        cost_estimate=pl.CostEstimate(flops=cost, bytes_accessed=cost // 400, transcendentals=0),
    )

    def apply(*operands):
        held = [x if m is None else pltpu.with_memory_space_constraint(x, m) for x, m in zip(operands, ins, strict=True)]
        return run(*held)

    return apply


def spread_to(block, axis):
    return lax.all_to_all(block, axis, 0, 0, tiled=True)


def shards(residual, elem_class, basis, eigenvalues, vertex_number, panels):
    field = residual.reshape(512, LANES)
    I32 = jnp.int32
    pay, own, cls, top, res, table, eigen = call(
        down_kernel,
        [
            ((8, 40, 128), VM), ((40, 128), VM), ((4, 2, 16), VM, I32), ((TOP, 2943), VM),
            ((512, 128), VM), ((8, 300), VM), ((8, 30), VM),
        ],
        [(40, 128), (3, 10, 8, 10), (3, 8, 10), (255 - TOP, 2943), VM((5, 3, 17), I32)], ins=[pltpu.HBM] * 6, sems=7,
    )(field, vertex_number, panels, elem_class, basis.transpose(1, 2, 0, 3), eigenvalues.transpose(1, 0, 2))
    first = spread_to(pay, "gy")
    tree, four = call(sum_kernel, [((64, 1, 256), VM), ((24, 128), VM)], ins=[None, VM])(first, own)
    summed = spread_to(tree, "gx")
    right, left, face = call(
        pack_kernel, [((168, 128), VM), ((168, 128), VM), ((64, 128), VM)], ins=[None, VM, VM, VM], cost=2_000_000_000
    )(first, res, cls, four)
    from_left = lax.ppermute(right, "gx", [(i, i + 1) for i in range(63)])
    from_right = lax.ppermute(left, "gx", [(i + 1, i) for i in range(63)])
    spec, sides, pick, eig, table_out = call(
        spectral_kernel,
        [
            ((10, 10, 16, 128), VM), ((2, 9, 16, 128), VM), ((304, 128), VM), ((40, 128), VM), ((8, 300), VM),
        ],
        [(10, 16, 128), (512, 128), (64, 128), (1760, 128), (10, 10, 16, 128), (10, 16, 128)], ins=[VM] * 5, cost=2_000_000_000,
    )(res, face, cls, table, eigen)
    fine, low = call(
        solve_kernel,
        [((600, 128), VM), ((255 - TOP, 2943), VM)],
        [
            (10, 10, 16, 128), (10, 16, 128), (2, 8, 8, 128), (512, 128), (512, 128),
            (64, 128), (288, 128), (1760, 128), (304, 128), (40, 128), (10, 16, 128), (10, 16, 128), (10, 16, 128), (10, 16, 128),
            (56, 128), (16, 128), (5, 10, 16, 128), (10, 16, 128), (10, 16, 128), (10, 16, 128), (64, 128), (10, 16, 128),
        ],
        ins=[VM] * 7 + [None, None, pltpu.HBM], sems=1, cost=1_000_000_000,
    )(spec, sides, table_out, eigen, pick, eig, four, from_left, from_right, panels)
    (pay,) = call(tree_kernel, [((8, 40, 128), VM)], ins=[None, VM])(summed, fine)
    second = spread_to(pay, "gy")
    (out,) = call(
        up_kernel, [((512, 128), None)], [(32, 128), (24, 128), (256, 128), (16, 128)], ins=[None, VM, VM, VM]
    )(second, top, low, fine)
    return out.reshape(residual.shape)


def solution(mesh):
    return jax.shard_map(
        shards,
        mesh=mesh,
        in_specs=(
            P(None, "gx", "gy", None),
            P("gx", "gy", None),
            P(),
            P(),
            P("gx", "gy", None),
            P("gx", "gy"),
        ),
        out_specs=P(None, "gx", "gy", None),
        check_vma=False,
    )
```

```python
import functools

import jax
import jax.numpy as jnp
from jax import lax
from jax.experimental import pallas as pl
from jax.experimental.pallas import tpu as pltpu
from jax.sharding import PartitionSpec as P

NPR = 8
NEXT = 10
NCLASS = 8
LANES = 128
TOP = 208
CUTS = [(slice(low, min(low + 128, 2943)), min(128, 2943 - low)) for low in range(0, 2943, 128)]
HALO = NPR + 1
F32 = jnp.float32
exact = lax.Precision.HIGHEST
ORDER = (1, 2, 3, 4, 5, 6, 7, 8, 0, 9)


def iota(shape, axis):
    return lax.broadcasted_iota(jnp.int32, shape, axis)


def hat(point, vertex):
    place = (point.astype(F32) + 0.5) / NPR
    return jnp.maximum(0.0, 1.0 - jnp.abs(place - vertex.astype(F32)))


def moved(rows, table):
    high = rows.astype(jnp.bfloat16)
    rest = rows - high.astype(F32)
    middle = rest.astype(jnp.bfloat16)
    low = (rest - middle.astype(F32)).astype(jnp.bfloat16)
    total = jnp.dot(low, table, preferred_element_type=F32)
    total = total + jnp.dot(middle, table, preferred_element_type=F32)
    return total + jnp.dot(high, table, preferred_element_type=F32)


def plane_hat(point, vertex):
    third = (vertex.astype(F32) + 0.5) / 3.0
    big = third.astype(jnp.int32)
    return hat(point >> 4, big) * hat(point & 15, vertex - 3 * big)


def down_kernel(
    res_hbm, num_hbm, pan_hbm, cls_hbm, basis_hbm, value_hbm,
    pay_ref, own_ref, cls_ref, top_ref, res_ref, table_ref, eigen_ref,
    line_ref, basis_ref, value_ref, low_ref, num_ref, sems,
):
    q = lax.axis_index("gy")
    pairs = [
        (res_hbm, res_ref), (num_hbm, num_ref), (cls_hbm, cls_ref), (basis_hbm, basis_ref), (value_hbm, value_ref),
        (pan_hbm.at[pl.ds(0, TOP), :], top_ref), (pan_hbm.at[pl.ds(TOP, 255 - TOP), :], low_ref),
    ]
    copies = [pltpu.make_async_copy(source, target, sems.at[n]) for n, (source, target) in enumerate(pairs)]
    for copy in copies:
        copy.start()
    plane = plane_hat(iota((16, 512), 1), iota((16, 512), 0))
    depth = hat(iota((128, 17), 0), iota((128, 17), 1))
    line_ref[...] = jnp.zeros((40, LANES), F32)
    copies[0].wait()
    half = jnp.dot(plane, res_ref[...], precision=exact)
    vertex = jnp.dot(half, depth, precision=exact)
    low_face = res_ref[pl.ds(0, 32, stride=16), :]
    high_face = res_ref[pl.ds(15, 32, stride=16), :]
    for peer in range(8):
        pay_ref[peer, 0:32, :] = jnp.where(peer < q, low_face, high_face)
    copies[1].wait()
    rows = iota((256, 17), 0)
    spread = jnp.zeros((256, 17), F32)
    for i in range(5):
        for j in range(3):
            k = 3 * i + j
            spread = spread + jnp.where(num_ref[i, j : j + 1, :] == rows, vertex[k : k + 1, :], 0.0)
    ordered = jnp.broadcast_to(jnp.sum(spread, axis=1, keepdims=True), (256, LANES))

    for copy in copies[2:5]:
        copy.wait()
    for d in range(3):
        eigen_ref[:, 10 * d : 10 * d + 10] = value_ref[d]
        for i in range(10):
            low = 100 * d + 10 * i
            table_ref[:, low : low + 10] = basis_ref[d, i]
    own_ref[24:40, :] = jnp.full((16, LANES), -1.0, F32)
    for k in range(15):
        low = 17 * (k % 7)
        own_ref[24 + k // 7 : 25 + k // 7, low : low + 17] = num_ref[k // 3, k % 3 : k % 3 + 1, :].astype(F32)
    copies[5].wait()
    for c, (cut, width) in enumerate(CUTS):
        line_ref[8 + c : 9 + c, :width] = jnp.sum(top_ref[:, cut] * ordered[:TOP, :width], axis=0, keepdims=True)
    copies[6].wait()
    for c, (cut, width) in enumerate(CUTS):
        piece = jnp.sum(low_ref[:, cut] * ordered[TOP:255, :width], axis=0, keepdims=True)
        line_ref[8 + c : 9 + c, :width] = line_ref[8 + c : 9 + c, :width] + piece
    here = pltpu.roll(line_ref[8:32], 1, 1)
    before = pltpu.roll(line_ref[7:31], 1, 1)
    own_ref[0:24, :] = jnp.where(iota((24, LANES), 1) == 0, before, here)
    for peer in range(8):
        pay_ref[peer, 32:35, :] = own_ref[2:5, :]
        pay_ref[peer, 35:37, :] = own_ref[8 + 2 * peer : 10 + 2 * peer, :]
        pay_ref[peer, 37:40, :] = own_ref[5:8, :] if peer == 7 else jnp.zeros((3, LANES), F32)


def sum_kernel(got_ref, own_ref, tree_ref, four_ref):
    q = lax.axis_index("gy")
    total = got_ref[0, 35:40, :]
    for peer in range(1, 8):
        total = total + got_ref[peer, 35:40, :]
    four_ref[0:3, :] = total[2:5]
    four_ref[6:8, :] = own_ref[0:2, :]
    four_ref[8:24, :] = own_ref[24:40, :]
    for level in range(1, 4):
        low = jnp.zeros((1, LANES), F32)
        for peer in range(8):
            inside = (peer >> level) == (q >> level)
            low = low + jnp.where(inside, got_ref[peer, 31 + level : 32 + level, :], 0.0)
        four_ref[2 + level : 3 + level, :] = low
    line = jnp.concatenate([total[0:1], total[1:2]], axis=1)
    for t in range(64):
        tree_ref[t] = line


def pack_kernel(got_ref, res_ref, cls_ref, four_ref, right_ref, left_ref, face_ref):
    q = lax.axis_index("gy")
    face_ref[0:32, :] = jnp.where(q > 0, got_ref[jnp.maximum(q - 1, 0), 0:32, :], 0.0)
    face_ref[32:64, :] = jnp.where(q < 7, got_ref[jnp.minimum(q + 1, 7), 0:32, :], 0.0)
    for ref, column, first in ((right_ref, 3, 23), (left_ref, 0, 0)):
        ref[0:144, :] = res_ref[16 * first : 16 * first + 144, :]
        ref[144:153, :] = face_ref[first : first + 9, :]
        ref[153:162, :] = face_ref[32 + first : 41 + first, :]
        ref[162:168, :] = jnp.zeros((6, LANES), F32)
        ref[162:164, 0:16] = (cls_ref[column] + 1).astype(F32)
        ref[164:167, :] = four_ref[0:3, :]


def grids():
    sub = iota((8, LANES), 0)
    lane = iota((8, LANES), 1)
    return sub, lane, lane & 15


def split_z(rows):
    lane = iota((LANES, LANES), 1)
    return moved(rows, (iota((LANES, LANES), 0) == (((lane & 15) << 3) | (lane >> 4))).astype(jnp.bfloat16))


def join_rows(rows):
    lane = iota((LANES, LANES), 0)
    return moved(rows, (iota((LANES, LANES), 1) == (((lane & 15) << 3) | (lane >> 4))).astype(jnp.bfloat16))


def exchange(groups):
    lane = iota((8, LANES), 1)
    groups = [list(parts) for parts in groups]
    for bit in (4, 2, 1):
        inside = (lane & (16 * bit)) != 0
        for parts in groups:
            for n in range(8):
                if n & bit:
                    continue
                low, high = parts[n], parts[n | bit]
                if bit == 4:
                    swap = pltpu.roll(jnp.where(inside, low, high), 64, 1)
                    parts[n] = jnp.where(inside, swap, low)
                    parts[n | bit] = jnp.where(inside, high, swap)
                else:
                    parts[n] = jnp.where(inside, pltpu.roll(high, 16 * bit, 1), low)
                    parts[n | bit] = jnp.where(inside, high, pltpu.roll(low, LANES - 16 * bit, 1))
    return groups


def with_outer(groups):
    kz = iota((8, LANES), 1) & 15
    before = [jnp.where(kz == 0, 0.0, pltpu.roll(parts[7], 1, 1)) for parts in groups]
    after = [jnp.where(kz == 15, 0.0, pltpu.roll(parts[0], 127, 1)) for parts in groups]
    return [parts + [b, a] for parts, b, a in zip(groups, before, after, strict=True)]


def at(i, j):
    return pl.ds(pl.multiple_of((i * 11 + j) * 16, 16), 16)


def join_z(total, sub, kz):
    main = total[0:8]
    tail = pltpu.roll(total[8:16], 7, 0)
    return main + jnp.where(
        sub == 7,
        jnp.where(kz == 15, 0.0, pltpu.roll(tail, 127, 1)),
        jnp.where((sub == 0) & (kz != 0), pltpu.roll(tail, 1, 1), 0.0),
    )


def row(ref, n):
    return jnp.broadcast_to(ref[pl.ds(n, 1), :], (16, LANES))


def dot_rows(pairs):
    total = None
    for a, b in pairs:
        total = a * b if total is None else total + a * b
    return total


def chosen(table, onehot):
    high = table.astype(jnp.bfloat16)
    rest = table - high.astype(F32)
    middle = rest.astype(jnp.bfloat16)
    low = (rest - middle.astype(F32)).astype(jnp.bfloat16)
    dims = (((0,), (0,)), ((), ()))
    total = lax.dot_general(low, onehot, dims, preferred_element_type=F32)
    total = total + lax.dot_general(middle, onehot, dims, preferred_element_type=F32)
    return total + lax.dot_general(high, onehot, dims, preferred_element_type=F32)


def pick_tables(kind, table_ref, eigen_ref, pick, eig):
    group = iota((8, LANES), 0)
    lane = iota((8, LANES), 1)
    spread = (iota((16, LANES), 0) == (iota((16, LANES), 1) & 15)).astype(F32)
    laid = jnp.dot(kind, spread, precision=exact)
    laid = jnp.sum(jnp.where(group == (lane >> 4), laid, 0.0), axis=0, keepdims=True)
    onehot = (laid == (group + 1).astype(F32)).astype(jnp.bfloat16)
    pick[0:300, :] = chosen(table_ref[:, 0:300], onehot)
    eig[0:30, :] = chosen(eigen_ref[:, 0:30], onehot)
    eig[20:30, :] = eig[20:30, :] + jnp.where(laid == 0.0, 1.0, 0.0)
    eig[30:40, :] = jnp.ones((10, LANES), F32)


def forward_z(pick, zfwd):
    for n, k in enumerate(ORDER):
        zfwd[n, 0:10, :] = pick[200 + 10 * k : 210 + 10 * k, :]
        zfwd[n, 10:16, :] = jnp.zeros((6, LANES), F32)


def backward_z(pick, zback):
    for c in range(10):
        zback[c, 0:8, :] = pick[pl.ds(210 + c, 8, stride=10), :]
        zback[c, 8:16, :] = jnp.zeros((8, LANES), F32)
        zback[c, 8:9, :] = pick[200 + c : 201 + c, :]
        zback[c, 9:10, :] = pick[290 + c : 291 + c, :]


def x_forward(win, table, target, count):
    def step(j, _):
        column = [win[at(i, j), :] for i in range(10)]
        for a in range(count):
            target[a, j] = dot_rows([(row(table, count * i + a), column[i]) for i in range(10)])
        return 0

    lax.fori_loop(0, 10, step, 0, unroll=2)


def through_z(source, zfwd, store):
    table = [zfwd[k] for k in range(10)]
    for b in range(10):
        store(b, dot_rows([(table[k], jnp.broadcast_to(source[b, k : k + 1, :], (16, LANES))) for k in range(10)]))


def y_forward(column, pick, target):
    for b in range(10):
        target[b] = dot_rows([(row(pick, 100 + 10 * j + b), column[j]) for j in range(10)])


def y_back(source, pick, store):
    column = [source[b] for b in range(10)]
    for j in range(10):
        store(j, dot_rows([(row(pick, 100 + 10 * j + b), column[b]) for b in range(10)]))


def into(ref, *place):
    def store(n, value):
        ref[(*place, n)] = value

    return store


def spectral_kernel(
    res_ref, face_ref, cls_ref, table_ref, eigen_ref,
    spec, sides, pick, eig, table_out,
    zfwd, rows_ref, rows_f, win, work, tmp,
):
    wide = iota((16, LANES), 1)
    upper = (wide & 16) != 0
    rows_ref[...] = split_z(res_ref[...])
    rows_f[...] = split_z(face_ref[...])
    kind = jnp.concatenate([cls_ref[ix].astype(F32) + 1.0 for ix in range(4)], axis=0)
    table_out[...] = table_ref[...]
    pick_tables(kind, table_ref, eigen_ref, pick, eig)
    forward_z(pick, zfwd)
    columns = range(8)
    groups = [
        [rows_ref[128 * (r // 2) + 16 * i + 8 * (r % 2) : 128 * (r // 2) + 16 * i + 8 * (r % 2) + 8, :] for r in range(8)]
        for i in columns
    ]
    groups.append([rows_f[32 * (r % 2) + 8 * (r // 2) : 32 * (r % 2) + 8 * (r // 2) + 8, :] for r in range(8)])
    groups = with_outer(exchange(groups))
    for k in range(10):
        win[pl.ds(21 * 16 + k, 8, stride=176), :] = groups[8][k]
    for i in columns:
        for k, part in enumerate(groups[i]):
            win[pl.ds((i * 11 + 12) * 16 + k, 8, stride=16), :] = part
    lines = (1, 2, 3, 4, 5, 6, 7, 8, 10)
    ahead = [win[at(8, j), :] for j in lines]
    back = [win[at(1, j), :] for j in lines]
    for n, j in enumerate(lines):
        sides[0, n] = back[n]
        sides[1, n] = ahead[n]
        win[at(0, j), :] = jnp.where(wide >= 32, pltpu.roll(ahead[n], 32, 1), 0.0)
        win[at(9, j), :] = jnp.where(wide < 96, pltpu.roll(back[n], 96, 1), 0.0)

    def y_halo(n, _):
        columns = [5 * n + m for m in range(5)]
        outer = [win[at(i, 10), :] for i in columns]
        last = [pltpu.roll(win[at(i, 8), :], 16, 1) for i in columns]
        first = [pltpu.roll(win[at(i, 1), :], 112, 1) for i in columns]
        for m, i in enumerate(columns):
            win[at(i, 0), :] = jnp.where(upper, last[m], outer[m])
            win[at(i, 9), :] = jnp.where(upper, outer[m], first[m])
        return 0

    lax.fori_loop(0, 2, y_halo, 0)
    x_forward(win, pick, work, 10)

    def step(a, _):
        y_forward([work[a, j] for j in range(10)], pick, tmp)
        through_z(tmp, zfwd, into(spec, a))
        return 0

    lax.fori_loop(0, 10, step, 0, unroll=2)


def solve_kernel(
    spec, sides, table_ref, eigen_ref, pick_m, eig_m, four_ref, from_left, from_right, pan_hbm,
    fine_ref, low_ref,
    work, edge, ends, tiles, rows_ref, rows_f, rows_e, win_e, pick_e, eig_e, zfwd_e, zback_e, zfwd_m, zback_m,
    half_e, lxe, work_e, tmp_a, tmp_b, tmp_c, rim_rows, late, sems,
):
    copy = pltpu.make_async_copy(pan_hbm.at[pl.ds(TOP, 255 - TOP), :], low_ref, sems.at[0])
    copy.start()
    sub, lane, kz = grids()
    wide = iota((16, LANES), 1)
    upper = (wide & 16) != 0

    rows_f[0:24, :] = from_left[144:168, :]
    rows_f[24:48, :] = from_right[144:168, :]
    rows_f[0:48, :] = split_z(rows_f[0:48, :])
    rows_e[0:144, :] = from_left[0:144, :]
    rows_e[144:288, :] = from_right[0:144, :]
    rows_e[...] = split_z(rows_e[...])
    beside = [rows_f[first : first + 8, :] for first in (1, 10, 24, 33)]
    corner = [jnp.broadcast_to(rows_f[n : n + 1, :], (8, LANES)) for n in (0, 9, 32, 41)]
    beside, corner = with_outer(exchange([beside + beside, corner + corner]))
    for k in range(10):
        win_e[pl.ds(21 * 16 + k, 8, stride=176), :] = beside[k]
        win_e[109 * 16 + k : 109 * 16 + k + 1, :] = corner[k][0:1]

    def fill(n, _):
        columns = [9 * n + m for m in range(9)]
        groups = []
        for i in columns:
            layer = jnp.where(i == 8, 0, i + 1)
            parts = [rows_e[pl.ds(pl.multiple_of(16 * layer + 8 * jy, 8), 8), :] for jy in range(2)]
            parts += [rows_e[pl.ds(pl.multiple_of(144 + 16 * i + 8 * jy, 8), 8), :] for jy in range(2)]
            groups.append(parts + parts)
        for i, parts in zip(columns, with_outer(exchange(groups)), strict=True):
            for k, part in enumerate(parts):
                win_e[pl.ds((i * 11 + 12) * 16 + k, 8, stride=16), :] = part
        return 0

    lax.fori_loop(0, 1, fill, 0)

    near = [from_left[162:164, 0:16], from_right[162:164, 0:16]]
    pick_tables(jnp.concatenate(near + near, axis=0), table_ref, eigen_ref, pick_e, eig_e)
    for pick, zfwd, zback in ((pick_e, zfwd_e, zback_e), (pick_m, zfwd_m, zback_m)):
        forward_z(pick, zfwd)
        backward_z(pick, zback)
    low_half = iota((5, LANES), 1) < 64
    for i in range(10):
        half_e[5 * i : 5 * i + 5, :] = jnp.where(low_half, pick_e[10 * i : 10 * i + 5, :], pick_e[10 * i + 5 : 10 * i + 10, :])
    half_e[50:55, :] = jnp.where((iota((5, LANES), 1) & 32) == 0, half_e[45:50, :], half_e[0:5, :])
    lxe[0:5, :] = jnp.where(low_half, eig_e[0:5, :], eig_e[5:10, :])

    second = (wide & 32) != 0
    lines = (1, 2, 3, 4, 5, 6, 7, 8, 10)
    both = [pltpu.roll(jnp.where(wide < 64, sides[0, n], sides[1, n]), 64, 1) for n in range(9)]
    for n, j in enumerate(lines):
        extra = win_e[at(9, j), :]
        win_e[at(0, j), :] = jnp.where(second, jnp.where(wide >= 64, sides[1, n], both[n]), extra)
        win_e[at(9, j), :] = jnp.where(second, extra, jnp.where(wide < 64, sides[0, n], both[n]))
    outer = [win_e[at(i, 10), :] for i in range(10)]
    last = [pltpu.roll(win_e[at(i, 8), :], 16, 1) for i in range(10)]
    first = [pltpu.roll(win_e[at(i, 1), :], 112, 1) for i in range(10)]
    for i in range(10):
        win_e[at(i, 0), :] = jnp.where(upper, last[i], outer[i])
        win_e[at(i, 9), :] = jnp.where(upper, outer[i], first[i])

    def scale(level, eig, b):
        return level + row(eig, 10 + b)

    x_forward(win_e, half_e, work_e, 5)
    for b in range(10):
        edge[b] = jnp.zeros((16, LANES), F32)

    def edge_step(a, _):
        y_forward([work_e[a, j] for j in range(10)], pick_e, tmp_a)
        level = row(lxe, a) + eig_e[20:36, :]
        weight = row(half_e, 50 + a)

        def add(b, value):
            edge[b] = edge[b] + weight * (value / scale(level, eig_e, b))

        through_z(tmp_a, zfwd_e, add)
        return 0

    lax.fori_loop(0, 5, edge_step, 0)
    for b in range(10):
        tmp_b[b] = edge[b] + pltpu.roll(edge[b], 64, 1)
    through_z(tmp_b, zback_e, into(tmp_c))
    y_back(tmp_c, pick_e, into(edge))

    inner = (wide >= 32) & (wide < 96)
    beyond = [jnp.where(inner, 0.0, jnp.where(wide < 32, win_e[at(8, j), :], win_e[at(1, j), :])) for j in range(10)]
    y_forward(beyond, pick_m, tmp_a)
    through_z(tmp_a, zfwd_m, into(late))
    lxe[0:16, :] = jnp.where(iota((16, LANES), 1) < 64, pick_m[0:16, :], pick_m[90:106, :])

    def main_step(a, _):
        level = row(eig_m, a) + eig_m[20:36, :]
        weight = row(lxe, a)
        for b in range(10):
            tmp_b[b] = (spec[a, b] + weight * late[b]) / scale(level, eig_m, b)
        through_z(tmp_b, zback_m, into(tmp_c))
        y_back(tmp_c, pick_m, into(work, a))
        return 0

    lax.fori_loop(0, 10, main_step, 0)

    for n, j in ((0, 0), (1, 9)):
        def put_end(i, main, n=n):
            ends[n, i - 1] = main

        x_back(work, edge, pick_m, j, put_end)
    for i in range(8):
        rim_rows[8 * i : 8 * i + 8, :] = jnp.where(upper[0:8], ends[1, i], ends[0, i])
    (parts,) = exchange([[rim_rows[pl.ds(k, 8, stride=8), :] for k in range(8)]])
    for r in range(8):
        rows_f[32 * (r % 2) + 8 * (r // 2) : 32 * (r % 2) + 8 * (r // 2) + 8, :] = parts[r]
    fine_ref[576:600, :] = four_ref[...]
    even = lax.axis_index("gx") % 2 == 0
    fine_ref[576:579, :] = four_ref[0:3, :] + jnp.where(even, from_right[164:167, :], from_left[164:167, :])
    fine_ref[512:576, :] = join_rows(rows_f[0:64, :])
    inner = upper[0:8]

    def solve(j, _):
        def put(i, tile):
            tile = tile + jnp.where(inner & (j == 1), pltpu.roll(ends[1, i - 1], 16, 1), 0.0)
            tile = tile + jnp.where(inner | (j != 8), 0.0, pltpu.roll(ends[0, i - 1], 112, 1))
            tiles[pl.ds(pl.multiple_of(((i - 1) * 8 + j - 1) * 8, 8), 8), :] = tile

        x_back(work, edge, pick_m, j, put)
        return 0

    lax.fori_loop(1, 9, solve, 0, unroll=8)

    def step(n, _):
        columns = [8 * n + m for m in range(8)]
        groups = exchange([[tiles[pl.ds(i * 64 + k, 8, stride=8), :] for k in range(8)] for i in columns])
        for i, parts in zip(columns, groups, strict=True):
            for r in range(8):
                rows_ref[pl.ds(pl.multiple_of(128 * (r // 2) + 16 * i + 8 * (r % 2), 8), 8), :] = parts[r]
        return 0

    lax.fori_loop(0, 1, step, 0)
    fine_ref[0:512, :] = join_rows(rows_ref[...])
    copy.wait()


def x_back(work, edge, pick, j, put):
    sub, lane, kz = grids()
    wide = iota((16, LANES), 1)
    column = [work[a, j] for a in range(10)]
    first = dot_rows([(row(pick, a), column[a]) for a in range(10)])
    last = dot_rows([(row(pick, 90 + a), column[a]) for a in range(10)])
    side = edge[j]
    for i in range(1, 9):
        total = dot_rows([(row(pick, 10 * i + a), column[a]) for a in range(10)])
        if i == 1:
            total = total + jnp.where(wide >= 32, pltpu.roll(last, 32, 1), side)
        if i == 8:
            total = total + jnp.where(wide < 96, pltpu.roll(first, 96, 1), side)
        put(i, join_z(total, sub, kz))


def tree_kernel(got_ref, fine_ref, pay_ref):
    p = lax.axis_index("gx")
    q = lax.axis_index("gy")
    totals = []
    for n in range(2):
        bits = 2 + (2 * q + n) // 3
        total = jnp.zeros((1, LANES), F32)
        for t in range(64):
            inside = (t >> bits) == (p >> bits)
            total = total + jnp.where(inside, got_ref[t, :, LANES * n : LANES * (n + 1)], 0.0)
        totals.append(total)
    four = fine_ref[576:579, :]
    for peer in range(8):
        pay_ref[peer, 0:32, :] = jnp.where(peer < q, fine_ref[512:544, :], fine_ref[544:576, :])
        pay_ref[peer, 32:33, :] = totals[0]
        pay_ref[peer, 33:34, :] = totals[1]
        pay_ref[peer, 34:37, :] = four
        pay_ref[peer, 37:40, :] = jnp.zeros((3, LANES), F32)


def up_kernel(
    got_ref, top_ref, low_ref, fine_ref, out_ref, line_ref, coeff_ref, sums_ref, vertex_ref
):
    q = lax.axis_index("gy")
    line_ref[...] = jnp.zeros((32, LANES), F32)
    line_ref[0:2, :] = fine_ref[582:584, :]
    line_ref[2:5, :] = fine_ref[579:582, :]
    line_ref[5:8, :] = got_ref[7, 34:37, :]
    for peer in range(8):
        line_ref[8 + 2 * peer : 10 + 2 * peer, :] = got_ref[peer, 32:34, :]
    here = pltpu.roll(line_ref[0:24], 127, 1)
    after = pltpu.roll(line_ref[1:25], 127, 1)
    coeff_ref[...] = jnp.where(iota((24, LANES), 1) == 127, after, here)
    weights = [jnp.broadcast_to(coeff_ref[c : c + 1, :width], (8, width)) for c, (_, width) in enumerate(CUTS)]

    def product(ref, first, place, count):
        total = ref[place, CUTS[0][0]] * weights[0][:count]
        for weight, (cut, _) in zip(weights[1:22], CUTS[1:22], strict=True):
            total = total + ref[place, cut] * weight[:count]
        end = ref[place, CUTS[22][0]] * weights[22][:count]
        sums_ref[pl.ds(first, count), :] = total
        sums_ref[pl.ds(first, count), 0:127] = total[:, 0:127] + end

    def step(g, _):
        first = pl.multiple_of(8 * g, 8)
        product(top_ref, first, pl.ds(first, 8), 8)
        return 0

    lax.fori_loop(0, TOP // 8, step, 0, unroll=TOP // 16)
    for low in range(0, 248 - TOP, 8):
        product(low_ref, TOP + low, pl.ds(low, 8), 8)
    product(low_ref, 248, pl.ds(248 - TOP, 7), 7)
    sums_ref[255:256, :] = jnp.zeros((1, LANES), F32)
    values = jnp.broadcast_to(jnp.sum(sums_ref[...], axis=1, keepdims=True), (256, LANES))
    vertex_ref[...] = jnp.zeros((16, LANES), F32)
    rows = iota((256, LANES), 0).astype(F32)
    for g in range(3):
        line = jnp.sum(jnp.where(fine_ref[584 + g : 585 + g, :] == rows, values, 0.0), axis=0, keepdims=True)
        for k in range(7 * g, min(7 * g + 7, 15)):
            low = 17 * (k % 7)
            vertex_ref[k : k + 1, 0:17] = line[:, low : low + 17]
    depth = hat(iota((LANES, LANES), 1), iota((LANES, LANES), 0)).astype(jnp.bfloat16)
    vertex_ref[...] = moved(vertex_ref[...], depth)
    rise = (2.0 * iota((8, LANES), 0).astype(F32) + 1.0) / 16.0
    planes = []
    for i in range(5):
        three = [jnp.broadcast_to(vertex_ref[3 * i + j : 3 * i + j + 1, :], (8, LANES)) for j in range(3)]
        planes.append([three[jy] * (1.0 - rise) + three[jy + 1] * rise for jy in range(2)])
    faces = (
        jnp.where(q > 0, got_ref[jnp.maximum(q - 1, 0), 0:32, :], 0.0),
        jnp.where(q < 7, got_ref[jnp.minimum(q + 1, 7), 0:32, :], 0.0),
    )
    edges = (iota((8, LANES), 0) == 0, iota((8, LANES), 0) == 7)
    for ix in range(4):
        for i in range(8):
            x = 8 * ix + i
            far = (2 * i + 1) / 16.0
            for jy in range(2):
                place = slice(16 * x + 8 * jy, 16 * x + 8 * jy + 8)
                value = fine_ref[place, :] + planes[ix][jy] * (1.0 - far) + planes[ix + 1][jy] * far
                out_ref[place, :] = value + jnp.where(edges[jy], faces[jy][x : x + 1, :], 0.0)


VM = pltpu.VMEM
ANYWHERE = None


def call(kernel, outs, scratch=(), ins=None, sems=0, cost=0, limit=24, aliases=None):
    shapes = [
        jax.ShapeDtypeStruct(o[0], o[2] if len(o) > 2 else F32) if o[1] is None else o[1](o[0], o[2] if len(o) > 2 else F32)
        for o in outs
    ]
    spaces = [pltpu.VMEM(s, F32) if isinstance(s, tuple) else s for s in scratch]
    if sems:
        spaces.append(pltpu.SemaphoreType.DMA((sems,)))
    run = pl.pallas_call(
        kernel,
        out_shape=shapes,
        in_specs=[pl.BlockSpec(memory_space=m or pltpu.VMEM) for m in ins],
        out_specs=[pl.BlockSpec(memory_space=pltpu.VMEM) for _ in outs],
        scratch_shapes=spaces,
        input_output_aliases=aliases or {},
        compiler_params=pltpu.CompilerParams(vmem_limit_bytes=limit << 20),
        cost_estimate=pl.CostEstimate(flops=cost, bytes_accessed=cost // 400, transcendentals=0),
    )

    def apply(*operands):
        held = [x if m is None else pltpu.with_memory_space_constraint(x, m) for x, m in zip(operands, ins, strict=True)]
        return run(*held)

    return apply


def spread_to(block, axis):
    return lax.all_to_all(block, axis, 0, 0, tiled=True)


def shards(residual, elem_class, basis, eigenvalues, vertex_number, panels):
    field = residual.reshape(512, LANES)
    I32 = jnp.int32
    pay, own, cls, top, res, table, eigen = call(
        down_kernel,
        [
            ((8, 40, 128), VM), ((40, 128), VM), ((4, 2, 16), VM, I32), ((TOP, 2943), VM),
            ((512, 128), VM), ((8, 300), VM), ((8, 30), VM),
        ],
        [(40, 128), (3, 10, 8, 10), (3, 8, 10), (255 - TOP, 2943), VM((5, 3, 17), I32)], ins=[pltpu.HBM] * 6, sems=7,
    )(field, vertex_number, panels, elem_class, basis.transpose(1, 2, 0, 3), eigenvalues.transpose(1, 0, 2))
    first = spread_to(pay, "gy")
    tree, four = call(sum_kernel, [((64, 1, 256), VM), ((24, 128), VM)], ins=[None, VM])(first, own)
    summed = spread_to(tree, "gx")
    right, left, face = call(
        pack_kernel, [((168, 128), VM), ((168, 128), VM), ((64, 128), VM)], ins=[None, VM, VM, VM], cost=2_000_000_000
    )(first, res, cls, four)
    from_left = lax.ppermute(right, "gx", [(i, i + 1) for i in range(63)])
    from_right = lax.ppermute(left, "gx", [(i + 1, i) for i in range(63)])
    spec, sides, pick, eig, table_out = call(
        spectral_kernel,
        [
            ((10, 10, 16, 128), VM), ((2, 9, 16, 128), VM), ((304, 128), VM), ((40, 128), VM), ((8, 300), VM),
        ],
        [(10, 16, 128), (512, 128), (64, 128), (1760, 128), (10, 10, 16, 128), (10, 16, 128)], ins=[VM] * 5, cost=2_000_000_000,
    )(res, face, cls, table, eigen)
    fine, low = call(
        solve_kernel,
        [((600, 128), VM), ((255 - TOP, 2943), VM)],
        [
            (10, 10, 16, 128), (10, 16, 128), (2, 8, 8, 128), (512, 128), (512, 128),
            (64, 128), (288, 128), (1760, 128), (304, 128), (40, 128), (10, 16, 128), (10, 16, 128), (10, 16, 128), (10, 16, 128),
            (56, 128), (16, 128), (5, 10, 16, 128), (10, 16, 128), (10, 16, 128), (10, 16, 128), (64, 128), (10, 16, 128),
        ],
        ins=[VM] * 7 + [None, None, pltpu.HBM], sems=1, cost=1_000_000_000,
    )(spec, sides, table_out, eigen, pick, eig, four, from_left, from_right, panels)
    (pay,) = call(tree_kernel, [((8, 40, 128), VM)], ins=[None, VM])(summed, fine)
    second = spread_to(pay, "gy")
    (out,) = call(
        up_kernel, [((512, 128), None)], [(32, 128), (24, 128), (256, 128), (16, 128)], ins=[None, VM, VM, VM]
    )(second, top, low, fine)
    return out.reshape(residual.shape)


def solution(mesh):
    return jax.shard_map(
        shards,
        mesh=mesh,
        in_specs=(
            P(None, "gx", "gy", None),
            P("gx", "gy", None),
            P(),
            P(),
            P("gx", "gy", None),
            P("gx", "gy"),
        ),
        out_specs=P(None, "gx", "gy", None),
        check_vma=False,
    )
```

```python
import functools

import jax
import jax.numpy as jnp
from jax import lax
from jax.experimental import pallas as pl
from jax.experimental.pallas import tpu as pltpu
from jax.sharding import PartitionSpec as P

NPR = 8
NEXT = 10
NCLASS = 8
LANES = 128
TOP = 208
CUTS = [(slice(low, min(low + 128, 2943)), min(128, 2943 - low)) for low in range(0, 2943, 128)]
HALO = NPR + 1
F32 = jnp.float32
exact = lax.Precision.HIGHEST
ORDER = (1, 2, 3, 4, 5, 6, 7, 8, 0, 9)


def iota(shape, axis):
    return lax.broadcasted_iota(jnp.int32, shape, axis)


def hat(point, vertex):
    place = (point.astype(F32) + 0.5) / NPR
    return jnp.maximum(0.0, 1.0 - jnp.abs(place - vertex.astype(F32)))


def moved(rows, table):
    high = rows.astype(jnp.bfloat16)
    rest = rows - high.astype(F32)
    middle = rest.astype(jnp.bfloat16)
    low = (rest - middle.astype(F32)).astype(jnp.bfloat16)
    total = jnp.dot(low, table, preferred_element_type=F32)
    total = total + jnp.dot(middle, table, preferred_element_type=F32)
    return total + jnp.dot(high, table, preferred_element_type=F32)


def plane_hat(point, vertex):
    third = (vertex.astype(F32) + 0.5) / 3.0
    big = third.astype(jnp.int32)
    return hat(point >> 4, big) * hat(point & 15, vertex - 3 * big)


def down_kernel(
    res_hbm, num_hbm, pan_hbm, cls_hbm, basis_hbm, value_hbm,
    pay_ref, own_ref, cls_ref, top_ref, res_ref, table_ref, eigen_ref,
    line_ref, basis_ref, value_ref, low_ref, num_ref, sems,
):
    q = lax.axis_index("gy")
    pairs = [
        (res_hbm, res_ref), (num_hbm, num_ref), (cls_hbm, cls_ref), (basis_hbm, basis_ref), (value_hbm, value_ref),
        (pan_hbm.at[pl.ds(0, TOP), :], top_ref), (pan_hbm.at[pl.ds(TOP, 255 - TOP), :], low_ref),
    ]
    copies = [pltpu.make_async_copy(source, target, sems.at[n]) for n, (source, target) in enumerate(pairs)]
    for copy in copies:
        copy.start()
    plane = plane_hat(iota((16, 512), 1), iota((16, 512), 0))
    depth = hat(iota((128, 17), 0), iota((128, 17), 1))
    line_ref[...] = jnp.zeros((40, LANES), F32)
    copies[0].wait()
    half = jnp.dot(plane, res_ref[...], precision=exact)
    vertex = jnp.dot(half, depth, precision=exact)
    low_face = res_ref[pl.ds(0, 32, stride=16), :]
    high_face = res_ref[pl.ds(15, 32, stride=16), :]
    for peer in range(8):
        pay_ref[peer, 0:32, :] = jnp.where(peer < q, low_face, high_face)
    copies[1].wait()
    rows = iota((256, 17), 0)
    spread = jnp.zeros((256, 17), F32)
    for i in range(5):
        for j in range(3):
            k = 3 * i + j
            spread = spread + jnp.where(num_ref[i, j : j + 1, :] == rows, vertex[k : k + 1, :], 0.0)
    ordered = jnp.broadcast_to(jnp.sum(spread, axis=1, keepdims=True), (256, LANES))

    for copy in copies[2:5]:
        copy.wait()
    for d in range(3):
        eigen_ref[:, 10 * d : 10 * d + 10] = value_ref[d]
        for i in range(10):
            low = 100 * d + 10 * i
            table_ref[:, low : low + 10] = basis_ref[d, i]
    own_ref[24:40, :] = jnp.full((16, LANES), -1.0, F32)
    for k in range(15):
        low = 17 * (k % 7)
        own_ref[24 + k // 7 : 25 + k // 7, low : low + 17] = num_ref[k // 3, k % 3 : k % 3 + 1, :].astype(F32)
    copies[5].wait()
    for c, (cut, width) in enumerate(CUTS):
        line_ref[8 + c : 9 + c, :width] = jnp.sum(top_ref[:, cut] * ordered[:TOP, :width], axis=0, keepdims=True)
    copies[6].wait()
    for c, (cut, width) in enumerate(CUTS):
        piece = jnp.sum(low_ref[:, cut] * ordered[TOP:255, :width], axis=0, keepdims=True)
        line_ref[8 + c : 9 + c, :width] = line_ref[8 + c : 9 + c, :width] + piece
    here = pltpu.roll(line_ref[8:32], 1, 1)
    before = pltpu.roll(line_ref[7:31], 1, 1)
    own_ref[0:24, :] = jnp.where(iota((24, LANES), 1) == 0, before, here)
    for peer in range(8):
        pay_ref[peer, 32:35, :] = own_ref[2:5, :]
        pay_ref[peer, 35:37, :] = own_ref[8 + 2 * peer : 10 + 2 * peer, :]
        pay_ref[peer, 37:40, :] = own_ref[5:8, :] if peer == 7 else jnp.zeros((3, LANES), F32)


def sum_kernel(got_ref, own_ref, tree_ref, four_ref):
    q = lax.axis_index("gy")
    total = got_ref[0, 35:40, :]
    for peer in range(1, 8):
        total = total + got_ref[peer, 35:40, :]
    four_ref[0:3, :] = total[2:5]
    four_ref[6:8, :] = own_ref[0:2, :]
    four_ref[8:24, :] = own_ref[24:40, :]
    for level in range(1, 4):
        low = jnp.zeros((1, LANES), F32)
        for peer in range(8):
            inside = (peer >> level) == (q >> level)
            low = low + jnp.where(inside, got_ref[peer, 31 + level : 32 + level, :], 0.0)
        four_ref[2 + level : 3 + level, :] = low
    line = jnp.concatenate([total[0:1], total[1:2]], axis=1)
    for t in range(64):
        tree_ref[t] = line


def pack_kernel(got_ref, res_ref, cls_ref, four_ref, right_ref, left_ref, face_ref):
    q = lax.axis_index("gy")
    face_ref[0:32, :] = jnp.where(q > 0, got_ref[jnp.maximum(q - 1, 0), 0:32, :], 0.0)
    face_ref[32:64, :] = jnp.where(q < 7, got_ref[jnp.minimum(q + 1, 7), 0:32, :], 0.0)
    for ref, column, first in ((right_ref, 3, 23), (left_ref, 0, 0)):
        ref[0:144, :] = res_ref[16 * first : 16 * first + 144, :]
        ref[144:153, :] = face_ref[first : first + 9, :]
        ref[153:162, :] = face_ref[32 + first : 41 + first, :]
        ref[162:168, :] = jnp.zeros((6, LANES), F32)
        ref[162:164, 0:16] = (cls_ref[column] + 1).astype(F32)
        ref[164:167, :] = four_ref[0:3, :]


def grids():
    sub = iota((8, LANES), 0)
    lane = iota((8, LANES), 1)
    return sub, lane, lane & 15


def split_z(rows):
    lane = iota((LANES, LANES), 1)
    return moved(rows, (iota((LANES, LANES), 0) == (((lane & 15) << 3) | (lane >> 4))).astype(jnp.bfloat16))


def join_rows(rows):
    lane = iota((LANES, LANES), 0)
    return moved(rows, (iota((LANES, LANES), 1) == (((lane & 15) << 3) | (lane >> 4))).astype(jnp.bfloat16))


def exchange(groups):
    lane = iota((8, LANES), 1)
    groups = [list(parts) for parts in groups]
    for bit in (4, 2, 1):
        inside = (lane & (16 * bit)) != 0
        for parts in groups:
            for n in range(8):
                if n & bit:
                    continue
                low, high = parts[n], parts[n | bit]
                if bit == 4:
                    swap = pltpu.roll(jnp.where(inside, low, high), 64, 1)
                    parts[n] = jnp.where(inside, swap, low)
                    parts[n | bit] = jnp.where(inside, high, swap)
                else:
                    parts[n] = jnp.where(inside, pltpu.roll(high, 16 * bit, 1), low)
                    parts[n | bit] = jnp.where(inside, high, pltpu.roll(low, LANES - 16 * bit, 1))
    return groups


def with_outer(groups):
    kz = iota((8, LANES), 1) & 15
    before = [jnp.where(kz == 0, 0.0, pltpu.roll(parts[7], 1, 1)) for parts in groups]
    after = [jnp.where(kz == 15, 0.0, pltpu.roll(parts[0], 127, 1)) for parts in groups]
    return [parts + [b, a] for parts, b, a in zip(groups, before, after, strict=True)]


def at(i, j):
    return pl.ds(pl.multiple_of((i * 11 + j) * 16, 16), 16)


def join_z(total, sub, kz):
    main = total[0:8]
    tail = pltpu.roll(total[8:16], 7, 0)
    return main + jnp.where(
        sub == 7,
        jnp.where(kz == 15, 0.0, pltpu.roll(tail, 127, 1)),
        jnp.where((sub == 0) & (kz != 0), pltpu.roll(tail, 1, 1), 0.0),
    )


def row(ref, n):
    return jnp.broadcast_to(ref[pl.ds(n, 1), :], (16, LANES))


def dot_rows(pairs):
    total = None
    for a, b in pairs:
        total = a * b if total is None else total + a * b
    return total


def chosen(table, onehot):
    high = table.astype(jnp.bfloat16)
    rest = table - high.astype(F32)
    middle = rest.astype(jnp.bfloat16)
    low = (rest - middle.astype(F32)).astype(jnp.bfloat16)
    dims = (((0,), (0,)), ((), ()))
    total = lax.dot_general(low, onehot, dims, preferred_element_type=F32)
    total = total + lax.dot_general(middle, onehot, dims, preferred_element_type=F32)
    return total + lax.dot_general(high, onehot, dims, preferred_element_type=F32)


def pick_tables(kind, table_ref, eigen_ref, pick, eig):
    group = iota((8, LANES), 0)
    lane = iota((8, LANES), 1)
    spread = (iota((16, LANES), 0) == (iota((16, LANES), 1) & 15)).astype(F32)
    laid = jnp.dot(kind, spread, precision=exact)
    laid = jnp.sum(jnp.where(group == (lane >> 4), laid, 0.0), axis=0, keepdims=True)
    onehot = (laid == (group + 1).astype(F32)).astype(jnp.bfloat16)
    pick[0:300, :] = chosen(table_ref[:, 0:300], onehot)
    eig[0:30, :] = chosen(eigen_ref[:, 0:30], onehot)
    eig[20:30, :] = eig[20:30, :] + jnp.where(laid == 0.0, 1.0, 0.0)
    eig[30:40, :] = jnp.ones((10, LANES), F32)


def forward_z(pick, zfwd):
    for n, k in enumerate(ORDER):
        zfwd[n, 0:10, :] = pick[200 + 10 * k : 210 + 10 * k, :]
        zfwd[n, 10:16, :] = jnp.zeros((6, LANES), F32)


def backward_z(pick, zback):
    for c in range(10):
        zback[c, 0:8, :] = pick[pl.ds(210 + c, 8, stride=10), :]
        zback[c, 8:16, :] = jnp.zeros((8, LANES), F32)
        zback[c, 8:9, :] = pick[200 + c : 201 + c, :]
        zback[c, 9:10, :] = pick[290 + c : 291 + c, :]


def x_forward(win, table, target, count):
    def step(j, _):
        column = [win[at(i, j), :] for i in range(10)]
        for a in range(count):
            target[a, j] = dot_rows([(row(table, count * i + a), column[i]) for i in range(10)])
        return 0

    lax.fori_loop(0, 10, step, 0, unroll=2)


def through_z(source, zfwd, store):
    table = [zfwd[k] for k in range(10)]
    for b in range(10):
        store(b, dot_rows([(table[k], jnp.broadcast_to(source[b, k : k + 1, :], (16, LANES))) for k in range(10)]))


def y_forward(column, pick, target):
    for b in range(10):
        target[b] = dot_rows([(row(pick, 100 + 10 * j + b), column[j]) for j in range(10)])


def y_back(source, pick, store):
    column = [source[b] for b in range(10)]
    for j in range(10):
        store(j, dot_rows([(row(pick, 100 + 10 * j + b), column[b]) for b in range(10)]))


def into(ref, *place):
    def store(n, value):
        ref[(*place, n)] = value

    return store


def spectral_kernel(
    res_ref, face_ref, cls_ref, table_ref, eigen_ref,
    spec, sides, pick, eig, table_out,
    zfwd, rows_ref, rows_f, win, work, tmp,
):
    wide = iota((16, LANES), 1)
    upper = (wide & 16) != 0
    rows_ref[...] = split_z(res_ref[...])
    rows_f[...] = split_z(face_ref[...])
    kind = jnp.concatenate([cls_ref[ix].astype(F32) + 1.0 for ix in range(4)], axis=0)
    table_out[...] = table_ref[...]
    pick_tables(kind, table_ref, eigen_ref, pick, eig)
    forward_z(pick, zfwd)
    columns = range(8)
    groups = [
        [rows_ref[128 * (r // 2) + 16 * i + 8 * (r % 2) : 128 * (r // 2) + 16 * i + 8 * (r % 2) + 8, :] for r in range(8)]
        for i in columns
    ]
    groups.append([rows_f[32 * (r % 2) + 8 * (r // 2) : 32 * (r % 2) + 8 * (r // 2) + 8, :] for r in range(8)])
    groups = with_outer(exchange(groups))
    for k in range(10):
        win[pl.ds(21 * 16 + k, 8, stride=176), :] = groups[8][k]
    for i in columns:
        for k, part in enumerate(groups[i]):
            win[pl.ds((i * 11 + 12) * 16 + k, 8, stride=16), :] = part
    lines = (1, 2, 3, 4, 5, 6, 7, 8, 10)
    ahead = [win[at(8, j), :] for j in lines]
    back = [win[at(1, j), :] for j in lines]
    for n, j in enumerate(lines):
        sides[0, n] = back[n]
        sides[1, n] = ahead[n]
        win[at(0, j), :] = jnp.where(wide >= 32, pltpu.roll(ahead[n], 32, 1), 0.0)
        win[at(9, j), :] = jnp.where(wide < 96, pltpu.roll(back[n], 96, 1), 0.0)

    def y_halo(n, _):
        columns = [5 * n + m for m in range(5)]
        outer = [win[at(i, 10), :] for i in columns]
        last = [pltpu.roll(win[at(i, 8), :], 16, 1) for i in columns]
        first = [pltpu.roll(win[at(i, 1), :], 112, 1) for i in columns]
        for m, i in enumerate(columns):
            win[at(i, 0), :] = jnp.where(upper, last[m], outer[m])
            win[at(i, 9), :] = jnp.where(upper, outer[m], first[m])
        return 0

    lax.fori_loop(0, 2, y_halo, 0)
    x_forward(win, pick, work, 10)

    def step(a, _):
        y_forward([work[a, j] for j in range(10)], pick, tmp)
        through_z(tmp, zfwd, into(spec, a))
        return 0

    lax.fori_loop(0, 10, step, 0, unroll=2)


def solve_kernel(
    spec, sides, table_ref, eigen_ref, pick_m, eig_m, four_ref, from_left, from_right, pan_hbm,
    fine_ref, low_ref,
    work, edge, ends, tiles, rows_ref, rows_f, rows_e, win_e, pick_e, eig_e, zfwd_e, zback_e, zfwd_m, zback_m,
    half_e, lxe, work_e, tmp_a, tmp_b, tmp_c, rim_rows, late, sems,
):
    copy = pltpu.make_async_copy(pan_hbm.at[pl.ds(TOP, 255 - TOP), :], low_ref, sems.at[0])
    copy.start()
    sub, lane, kz = grids()
    wide = iota((16, LANES), 1)
    upper = (wide & 16) != 0

    rows_f[0:24, :] = from_left[144:168, :]
    rows_f[24:48, :] = from_right[144:168, :]
    rows_f[0:48, :] = split_z(rows_f[0:48, :])
    rows_e[0:144, :] = from_left[0:144, :]
    rows_e[144:288, :] = from_right[0:144, :]
    rows_e[...] = split_z(rows_e[...])
    beside = [rows_f[first : first + 8, :] for first in (1, 10, 24, 33)]
    corner = [jnp.broadcast_to(rows_f[n : n + 1, :], (8, LANES)) for n in (0, 9, 32, 41)]
    beside, corner = with_outer(exchange([beside + beside, corner + corner]))
    for k in range(10):
        win_e[pl.ds(21 * 16 + k, 8, stride=176), :] = beside[k]
        win_e[109 * 16 + k : 109 * 16 + k + 1, :] = corner[k][0:1]

    def fill(n, _):
        columns = [9 * n + m for m in range(9)]
        groups = []
        for i in columns:
            layer = jnp.where(i == 8, 0, i + 1)
            parts = [rows_e[pl.ds(pl.multiple_of(16 * layer + 8 * jy, 8), 8), :] for jy in range(2)]
            parts += [rows_e[pl.ds(pl.multiple_of(144 + 16 * i + 8 * jy, 8), 8), :] for jy in range(2)]
            groups.append(parts + parts)
        for i, parts in zip(columns, with_outer(exchange(groups)), strict=True):
            for k, part in enumerate(parts):
                win_e[pl.ds((i * 11 + 12) * 16 + k, 8, stride=16), :] = part
        return 0

    lax.fori_loop(0, 1, fill, 0)

    near = [from_left[162:164, 0:16], from_right[162:164, 0:16]]
    pick_tables(jnp.concatenate(near + near, axis=0), table_ref, eigen_ref, pick_e, eig_e)
    for pick, zfwd, zback in ((pick_e, zfwd_e, zback_e), (pick_m, zfwd_m, zback_m)):
        forward_z(pick, zfwd)
        backward_z(pick, zback)
    low_half = iota((5, LANES), 1) < 64
    for i in range(10):
        half_e[5 * i : 5 * i + 5, :] = jnp.where(low_half, pick_e[10 * i : 10 * i + 5, :], pick_e[10 * i + 5 : 10 * i + 10, :])
    half_e[50:55, :] = jnp.where((iota((5, LANES), 1) & 32) == 0, half_e[45:50, :], half_e[0:5, :])
    lxe[0:5, :] = jnp.where(low_half, eig_e[0:5, :], eig_e[5:10, :])

    second = (wide & 32) != 0
    lines = (1, 2, 3, 4, 5, 6, 7, 8, 10)
    both = [pltpu.roll(jnp.where(wide < 64, sides[0, n], sides[1, n]), 64, 1) for n in range(9)]
    for n, j in enumerate(lines):
        extra = win_e[at(9, j), :]
        win_e[at(0, j), :] = jnp.where(second, jnp.where(wide >= 64, sides[1, n], both[n]), extra)
        win_e[at(9, j), :] = jnp.where(second, extra, jnp.where(wide < 64, sides[0, n], both[n]))
    outer = [win_e[at(i, 10), :] for i in range(10)]
    last = [pltpu.roll(win_e[at(i, 8), :], 16, 1) for i in range(10)]
    first = [pltpu.roll(win_e[at(i, 1), :], 112, 1) for i in range(10)]
    for i in range(10):
        win_e[at(i, 0), :] = jnp.where(upper, last[i], outer[i])
        win_e[at(i, 9), :] = jnp.where(upper, outer[i], first[i])

    def scale(level, eig, b):
        return level + row(eig, 10 + b)

    x_forward(win_e, half_e, work_e, 5)
    for b in range(10):
        edge[b] = jnp.zeros((16, LANES), F32)

    def edge_step(a, _):
        y_forward([work_e[a, j] for j in range(10)], pick_e, tmp_a)
        level = row(lxe, a) + eig_e[20:36, :]
        weight = row(half_e, 50 + a)

        def add(b, value):
            edge[b] = edge[b] + weight * (value / scale(level, eig_e, b))

        through_z(tmp_a, zfwd_e, add)
        return 0

    lax.fori_loop(0, 5, edge_step, 0)
    for b in range(10):
        tmp_b[b] = edge[b] + pltpu.roll(edge[b], 64, 1)
    through_z(tmp_b, zback_e, into(tmp_c))
    y_back(tmp_c, pick_e, into(edge))

    inner = (wide >= 32) & (wide < 96)
    beyond = [jnp.where(inner, 0.0, jnp.where(wide < 32, win_e[at(8, j), :], win_e[at(1, j), :])) for j in range(10)]
    y_forward(beyond, pick_m, tmp_a)
    through_z(tmp_a, zfwd_m, into(late))
    lxe[0:16, :] = jnp.where(iota((16, LANES), 1) < 64, pick_m[0:16, :], pick_m[90:106, :])

    def main_step(a, _):
        level = row(eig_m, a) + eig_m[20:36, :]
        weight = row(lxe, a)
        for b in range(10):
            tmp_b[b] = (spec[a, b] + weight * late[b]) / scale(level, eig_m, b)
        through_z(tmp_b, zback_m, into(tmp_c))
        y_back(tmp_c, pick_m, into(work, a))
        return 0

    lax.fori_loop(0, 10, main_step, 0, unroll=5)

    for n, j in ((0, 0), (1, 9)):
        def put_end(i, main, n=n):
            ends[n, i - 1] = main

        x_back(work, edge, pick_m, j, put_end)
    for i in range(8):
        rim_rows[8 * i : 8 * i + 8, :] = jnp.where(upper[0:8], ends[1, i], ends[0, i])
    (parts,) = exchange([[rim_rows[pl.ds(k, 8, stride=8), :] for k in range(8)]])
    for r in range(8):
        rows_f[32 * (r % 2) + 8 * (r // 2) : 32 * (r % 2) + 8 * (r // 2) + 8, :] = parts[r]
    fine_ref[576:600, :] = four_ref[...]
    even = lax.axis_index("gx") % 2 == 0
    fine_ref[576:579, :] = four_ref[0:3, :] + jnp.where(even, from_right[164:167, :], from_left[164:167, :])
    fine_ref[512:576, :] = join_rows(rows_f[0:64, :])
    inner = upper[0:8]

    def solve(j, _):
        def put(i, tile):
            tile = tile + jnp.where(inner & (j == 1), pltpu.roll(ends[1, i - 1], 16, 1), 0.0)
            tile = tile + jnp.where(inner | (j != 8), 0.0, pltpu.roll(ends[0, i - 1], 112, 1))
            tiles[pl.ds(pl.multiple_of(((i - 1) * 8 + j - 1) * 8, 8), 8), :] = tile

        x_back(work, edge, pick_m, j, put)
        return 0

    lax.fori_loop(1, 9, solve, 0, unroll=8)

    def step(n, _):
        columns = [8 * n + m for m in range(8)]
        groups = exchange([[tiles[pl.ds(i * 64 + k, 8, stride=8), :] for k in range(8)] for i in columns])
        for i, parts in zip(columns, groups, strict=True):
            for r in range(8):
                rows_ref[pl.ds(pl.multiple_of(128 * (r // 2) + 16 * i + 8 * (r % 2), 8), 8), :] = parts[r]
        return 0

    lax.fori_loop(0, 1, step, 0)
    fine_ref[0:512, :] = join_rows(rows_ref[...])
    copy.wait()


def x_back(work, edge, pick, j, put):
    sub, lane, kz = grids()
    wide = iota((16, LANES), 1)
    column = [work[a, j] for a in range(10)]
    first = dot_rows([(row(pick, a), column[a]) for a in range(10)])
    last = dot_rows([(row(pick, 90 + a), column[a]) for a in range(10)])
    side = edge[j]
    for i in range(1, 9):
        total = dot_rows([(row(pick, 10 * i + a), column[a]) for a in range(10)])
        if i == 1:
            total = total + jnp.where(wide >= 32, pltpu.roll(last, 32, 1), side)
        if i == 8:
            total = total + jnp.where(wide < 96, pltpu.roll(first, 96, 1), side)
        put(i, join_z(total, sub, kz))


def tree_kernel(got_ref, fine_ref, pay_ref):
    p = lax.axis_index("gx")
    q = lax.axis_index("gy")
    totals = []
    for n in range(2):
        bits = 2 + (2 * q + n) // 3
        total = jnp.zeros((1, LANES), F32)
        for t in range(64):
            inside = (t >> bits) == (p >> bits)
            total = total + jnp.where(inside, got_ref[t, :, LANES * n : LANES * (n + 1)], 0.0)
        totals.append(total)
    four = fine_ref[576:579, :]
    for peer in range(8):
        pay_ref[peer, 0:32, :] = jnp.where(peer < q, fine_ref[512:544, :], fine_ref[544:576, :])
        pay_ref[peer, 32:33, :] = totals[0]
        pay_ref[peer, 33:34, :] = totals[1]
        pay_ref[peer, 34:37, :] = four
        pay_ref[peer, 37:40, :] = jnp.zeros((3, LANES), F32)


def up_kernel(
    got_ref, top_ref, low_ref, fine_ref, out_ref, line_ref, coeff_ref, sums_ref, vertex_ref
):
    q = lax.axis_index("gy")
    line_ref[...] = jnp.zeros((32, LANES), F32)
    line_ref[0:2, :] = fine_ref[582:584, :]
    line_ref[2:5, :] = fine_ref[579:582, :]
    line_ref[5:8, :] = got_ref[7, 34:37, :]
    for peer in range(8):
        line_ref[8 + 2 * peer : 10 + 2 * peer, :] = got_ref[peer, 32:34, :]
    here = pltpu.roll(line_ref[0:24], 127, 1)
    after = pltpu.roll(line_ref[1:25], 127, 1)
    coeff_ref[...] = jnp.where(iota((24, LANES), 1) == 127, after, here)
    weights = [jnp.broadcast_to(coeff_ref[c : c + 1, :width], (8, width)) for c, (_, width) in enumerate(CUTS)]

    def product(ref, first, place, count):
        total = ref[place, CUTS[0][0]] * weights[0][:count]
        for weight, (cut, _) in zip(weights[1:22], CUTS[1:22], strict=True):
            total = total + ref[place, cut] * weight[:count]
        end = ref[place, CUTS[22][0]] * weights[22][:count]
        sums_ref[pl.ds(first, count), :] = total
        sums_ref[pl.ds(first, count), 0:127] = total[:, 0:127] + end

    def step(g, _):
        first = pl.multiple_of(8 * g, 8)
        product(top_ref, first, pl.ds(first, 8), 8)
        return 0

    lax.fori_loop(0, TOP // 8, step, 0, unroll=TOP // 16)
    for low in range(0, 248 - TOP, 8):
        product(low_ref, TOP + low, pl.ds(low, 8), 8)
    product(low_ref, 248, pl.ds(248 - TOP, 7), 7)
    sums_ref[255:256, :] = jnp.zeros((1, LANES), F32)
    values = jnp.broadcast_to(jnp.sum(sums_ref[...], axis=1, keepdims=True), (256, LANES))
    vertex_ref[...] = jnp.zeros((16, LANES), F32)
    rows = iota((256, LANES), 0).astype(F32)
    for g in range(3):
        line = jnp.sum(jnp.where(fine_ref[584 + g : 585 + g, :] == rows, values, 0.0), axis=0, keepdims=True)
        for k in range(7 * g, min(7 * g + 7, 15)):
            low = 17 * (k % 7)
            vertex_ref[k : k + 1, 0:17] = line[:, low : low + 17]
    depth = hat(iota((LANES, LANES), 1), iota((LANES, LANES), 0)).astype(jnp.bfloat16)
    vertex_ref[...] = moved(vertex_ref[...], depth)
    rise = (2.0 * iota((8, LANES), 0).astype(F32) + 1.0) / 16.0
    planes = []
    for i in range(5):
        three = [jnp.broadcast_to(vertex_ref[3 * i + j : 3 * i + j + 1, :], (8, LANES)) for j in range(3)]
        planes.append([three[jy] * (1.0 - rise) + three[jy + 1] * rise for jy in range(2)])
    faces = (
        jnp.where(q > 0, got_ref[jnp.maximum(q - 1, 0), 0:32, :], 0.0),
        jnp.where(q < 7, got_ref[jnp.minimum(q + 1, 7), 0:32, :], 0.0),
    )
    edges = (iota((8, LANES), 0) == 0, iota((8, LANES), 0) == 7)
    for ix in range(4):
        for i in range(8):
            x = 8 * ix + i
            far = (2 * i + 1) / 16.0
            for jy in range(2):
                place = slice(16 * x + 8 * jy, 16 * x + 8 * jy + 8)
                value = fine_ref[place, :] + planes[ix][jy] * (1.0 - far) + planes[ix + 1][jy] * far
                out_ref[place, :] = value + jnp.where(edges[jy], faces[jy][x : x + 1, :], 0.0)


VM = pltpu.VMEM
ANYWHERE = None


def call(kernel, outs, scratch=(), ins=None, sems=0, cost=0, limit=24, aliases=None):
    shapes = [
        jax.ShapeDtypeStruct(o[0], o[2] if len(o) > 2 else F32) if o[1] is None else o[1](o[0], o[2] if len(o) > 2 else F32)
        for o in outs
    ]
    spaces = [pltpu.VMEM(s, F32) if isinstance(s, tuple) else s for s in scratch]
    if sems:
        spaces.append(pltpu.SemaphoreType.DMA((sems,)))
    run = pl.pallas_call(
        kernel,
        out_shape=shapes,
        in_specs=[pl.BlockSpec(memory_space=m or pltpu.VMEM) for m in ins],
        out_specs=[pl.BlockSpec(memory_space=pltpu.VMEM) for _ in outs],
        scratch_shapes=spaces,
        input_output_aliases=aliases or {},
        compiler_params=pltpu.CompilerParams(vmem_limit_bytes=limit << 20),
        cost_estimate=pl.CostEstimate(flops=cost, bytes_accessed=cost // 400, transcendentals=0),
    )

    def apply(*operands):
        held = [x if m is None else pltpu.with_memory_space_constraint(x, m) for x, m in zip(operands, ins, strict=True)]
        return run(*held)

    return apply


def spread_to(block, axis):
    return lax.all_to_all(block, axis, 0, 0, tiled=True)


def shards(residual, elem_class, basis, eigenvalues, vertex_number, panels):
    field = residual.reshape(512, LANES)
    I32 = jnp.int32
    pay, own, cls, top, res, table, eigen = call(
        down_kernel,
        [
            ((8, 40, 128), VM), ((40, 128), VM), ((4, 2, 16), VM, I32), ((TOP, 2943), VM),
            ((512, 128), VM), ((8, 300), VM), ((8, 30), VM),
        ],
        [(40, 128), (3, 10, 8, 10), (3, 8, 10), (255 - TOP, 2943), VM((5, 3, 17), I32)], ins=[pltpu.HBM] * 6, sems=7,
    )(field, vertex_number, panels, elem_class, basis.transpose(1, 2, 0, 3), eigenvalues.transpose(1, 0, 2))
    first = spread_to(pay, "gy")
    tree, four = call(sum_kernel, [((64, 1, 256), VM), ((24, 128), VM)], ins=[None, VM])(first, own)
    summed = spread_to(tree, "gx")
    right, left, face = call(
        pack_kernel, [((168, 128), VM), ((168, 128), VM), ((64, 128), VM)], ins=[None, VM, VM, VM], cost=2_000_000_000
    )(first, res, cls, four)
    from_left = lax.ppermute(right, "gx", [(i, i + 1) for i in range(63)])
    from_right = lax.ppermute(left, "gx", [(i + 1, i) for i in range(63)])
    spec, sides, pick, eig, table_out = call(
        spectral_kernel,
        [
            ((10, 10, 16, 128), VM), ((2, 9, 16, 128), VM), ((304, 128), VM), ((40, 128), VM), ((8, 300), VM),
        ],
        [(10, 16, 128), (512, 128), (64, 128), (1760, 128), (10, 10, 16, 128), (10, 16, 128)], ins=[VM] * 5, cost=2_000_000_000,
    )(res, face, cls, table, eigen)
    fine, low = call(
        solve_kernel,
        [((600, 128), VM), ((255 - TOP, 2943), VM)],
        [
            (10, 10, 16, 128), (10, 16, 128), (2, 8, 8, 128), (512, 128), (512, 128),
            (64, 128), (288, 128), (1760, 128), (304, 128), (40, 128), (10, 16, 128), (10, 16, 128), (10, 16, 128), (10, 16, 128),
            (56, 128), (16, 128), (5, 10, 16, 128), (10, 16, 128), (10, 16, 128), (10, 16, 128), (64, 128), (10, 16, 128),
        ],
        ins=[VM] * 7 + [None, None, pltpu.HBM], sems=1, cost=1_000_000_000,
    )(spec, sides, table_out, eigen, pick, eig, four, from_left, from_right, panels)
    (pay,) = call(tree_kernel, [((8, 40, 128), VM)], ins=[None, VM])(summed, fine)
    second = spread_to(pay, "gy")
    (out,) = call(
        up_kernel, [((512, 128), None)], [(32, 128), (24, 128), (256, 128), (16, 128)], ins=[None, VM, VM, VM]
    )(second, top, low, fine)
    return out.reshape(residual.shape)


def solution(mesh):
    return jax.shard_map(
        shards,
        mesh=mesh,
        in_specs=(
            P(None, "gx", "gy", None),
            P("gx", "gy", None),
            P(),
            P(),
            P("gx", "gy", None),
            P("gx", "gy"),
        ),
        out_specs=P(None, "gx", "gy", None),
        check_vma=False,
    )
```
